32 devices in a mesh: expert: 8 (over z, y), tensor: 4 (over x, core).
Axes of the slice: x: 2, y: 2, z: 4, core: 2. Of those that a mesh axis runs over, the one named last changes fastest.
Arguments:
- hidden_in: bfloat16 [3072, 2048], P('expert'), may hold values from -6 to 6
- cotangent: bfloat16 [3072, 2048], P('expert'), may hold values from -6 to 6
- segments: int32 [3072], P('expert'), may hold values from 0 to 7, as said below
- positions: int32 [3072], P('expert'), may hold values from 0 to 1535, as said below
- routes: int32 [3072, 8], P('expert'), may hold values from 0 to 15, as said below
- attn_gain: float32 [2048], replicated, may hold values from 0.5 to 1.5
- w_query: bfloat16 [2048, 4096], P(None, 'tensor')
- w_key: bfloat16 [2048, 512], P(None, 'tensor')
- value_weight: bfloat16 [2048, 512], P(None, 'tensor'), may hold values from -0.125 to 0.125
- q_gain: float32 [128], replicated
- k_gain: float32 [128], replicated
- w_out: bfloat16 [4096, 2048], P('tensor'), may hold values from -0.5 to 0.5
- ffn_gain: float32 [2048], replicated, may hold values from 0.5 to 1.5
- router: bfloat16 [2048, 16], replicated
- w_gate: bfloat16 [16, 2048, 768], P('expert', None, 'tensor'), may hold values from -0.125 to 0.125
- w_up: bfloat16 [16, 2048, 768], P('expert', None, 'tensor'), may hold values from -0.125 to 0.125
- w_down: bfloat16 [16, 768, 2048], P('expert', 'tensor'), may hold values from -0.4375 to 0.4375
Outputs:
- layer_out: bfloat16 [3072, 2048], P('expert')
- input_grad: float32 [3072, 2048], P('expert')
- attn_gain_grad: float32 [2048], P('expert')
- w_query_grad: float32 [2048, 4096], P('expert', 'tensor')
- w_key_grad: float32 [2048, 512], P('expert', 'tensor')
- w_value_grad: float32 [2048, 512], P('expert', 'tensor')
- q_gain_grad: float32 [128], P('expert')
- k_gain_grad: float32 [128], P('expert')
- w_out_grad: float32 [4096, 2048], P('tensor', 'expert')
- ffn_gain_grad: float32 [2048], P('expert')
- router_grad: float32 [2048, 16], P('expert')
- w_gate_grad: float32 [16, 2048, 768], P('expert', None, 'tensor')
- w_up_grad: float32 [16, 2048, 768], P('expert', None, 'tensor')
- w_down_grad: float32 [16, 768, 2048], P('expert', 'tensor')
The draws below stay inside these ranges and needn't reach their ends.
Inputs may be any that keep to these rules, and one draw needn't show every extreme that they name: `routes`: each row names 8 different experts. The rows of one block of 384 consecutive tokens name each expert at least 96 and at most 288 times; one expert, the same for every block, is named exactly 288 times in every block. `segments`: each block of 384 consecutive tokens holds exactly 8 documents, numbered 0 to 7 in order; the numbers never fall and rise by at most one from token to token. Within a document positions rise by one from token to token; the first token of each block of 384 tokens has position 0 and the last has position 1535.
All inputs are finite; a program needn't handle non-finite values.
Results may differ from the reference program's by a relative error of at most 0.02.
Values may be sent and summed in bfloat16 or wider, within the bound.
No kernel may reach another device: no remote copies, remote signals or barrier semaphores. Data moves between devices by JAX's collectives and lax.ppermute only.
A program may use at most 320 MiB of HBM per device.

```python
import math
import jax
import jax.numpy as jnp
from jax import lax

MODEL_DIM = 2048
QUERY_HEADS = 32
KEY_VALUE_HEADS = 4
HEAD_DIM = 128
FF = 768
TOP = 8
TOKENS_PER_SHARD = 384
TOKEN_TOTAL = 3072
EXPERTS = 16
CAP = 288
N_EXPERT = 8


def segment_parts(key):
    block_list = TOKEN_TOTAL // TOKENS_PER_SHARD
    token_index = jnp.arange(TOKENS_PER_SHARD, dtype=jnp.int32)

    def starts_of(block_key):
        chosen = jax.random.permutation(block_key, TOKENS_PER_SHARD - 1)[:7].astype(jnp.int32) + 1
        return jnp.zeros((TOKENS_PER_SHARD,), jnp.int32).at[0].set(1).at[chosen].set(1)
    marked = jax.vmap(starts_of)(jax.random.split(jax.random.fold_in(key, 21), block_list)) > 0
    numbers = jnp.cumsum(marked.astype(jnp.int32), 1) - 1
    starts = lax.cummax(jnp.where(marked, token_index[None, :], 0), axis=1)
    offsets = jax.random.randint(jax.random.fold_in(key, 22), (block_list, TOKENS_PER_SHARD), 0, 3 * TOKENS_PER_SHARD)
    offsets = jnp.where(token_index[None, :] == 0, 0, offsets)
    first_pos = jnp.take_along_axis(offsets, starts, 1)
    placed = token_index[None, :] - starts + first_pos
    placed = jnp.where(numbers == 7, 3 * TOKENS_PER_SHARD + token_index[None, :], placed)
    return (numbers.reshape(-1).astype(jnp.int32), placed.reshape(-1).astype(jnp.int32))


def draw_segments(key, part):
    return segment_parts(key)[0]


def draw_positions(key, part):
    return segment_parts(key)[1]


def draw_routes(key, part):
    block_list = TOKEN_TOTAL // TOKENS_PER_SHARD
    base_load = TOKENS_PER_SHARD * TOP // EXPERTS
    spread_load = base_load // 2
    star = jax.random.randint(jax.random.fold_in(key, 1), (), 0, EXPERTS)

    def one_block(block_key):
        first_key, second_key, third_key, fourth_key = jax.random.split(block_key, 4)
        order = jax.random.permutation(first_key, EXPERTS).astype(jnp.int32)
        star_place = jnp.argmax(order == star)
        leading = order[0]
        order = order.at[star_place].set(leading).at[0].set(star)
        amount = jax.random.randint(second_key, (EXPERTS // 2,), 0, spread_load + 1).at[0].set(spread_load)
        change = jnp.stack([amount, -amount], 1).reshape(-1)
        counts = jnp.zeros((EXPERTS,), jnp.int32).at[order].set(base_load + change)
        ends = jnp.cumsum(counts)
        entry = jnp.searchsorted(ends, jnp.arange(TOKENS_PER_SHARD * TOP, dtype=jnp.int32), side='right').astype(jnp.int32)
        layout = entry.reshape(TOP, TOKENS_PER_SHARD).T
        layout = layout[jax.random.permutation(third_key, TOKENS_PER_SHARD)]
        ranking = jax.random.randint(fourth_key, (TOKENS_PER_SHARD, TOP), 0, 1048576) * TOP + jnp.arange(TOP, dtype=jnp.int32)[None, :]
        shuffle = jnp.argsort(ranking, axis=1)
        return jnp.take_along_axis(layout, shuffle, 1)
    block_keys = jax.random.split(jax.random.fold_in(key, 2), block_list)
    return jax.vmap(one_block)(block_keys).reshape(TOKEN_TOTAL, TOP).astype(jnp.int32)


def draw_w_query(key, part):
    query_matrix = jax.random.normal(jax.random.fold_in(key, 31), (MODEL_DIM, QUERY_HEADS * HEAD_DIM), jnp.float32) * MODEL_DIM ** (-0.5)
    return query_matrix.astype(jnp.bfloat16)


def draw_w_key(key, part):
    key_matrix = jax.random.normal(jax.random.fold_in(key, 32), (MODEL_DIM, KEY_VALUE_HEADS * HEAD_DIM), jnp.float32) * MODEL_DIM ** (-0.5)
    return key_matrix.astype(jnp.bfloat16)


def draw_q_gain(key, part):
    return jax.random.uniform(jax.random.fold_in(key, 41), (HEAD_DIM,), jnp.float32, 0.6, 1.8)


def draw_k_gain(key, part):
    return jax.random.uniform(jax.random.fold_in(key, 42), (HEAD_DIM,), jnp.float32, 0.6, 1.8)


def draw_router(key, part):
    base_mat = jax.random.normal(jax.random.fold_in(key, 51), (MODEL_DIM, EXPERTS), jnp.float32) * MODEL_DIM ** (-0.5)
    lower = math.log(0.05)
    upper = math.log(0.5)
    column_scale = jnp.exp(jax.random.uniform(jax.random.fold_in(key, 52), (1, EXPERTS), jnp.float32, lower, upper))
    return (base_mat * column_scale).astype(jnp.bfloat16)


def levels(own_key, extent, pieces, least, top_value):
    gain, own = 1.0, jax.random.fold_in(own_key, 6)
    for position, shards_of in pieces:
        steps = jnp.exp(jax.random.uniform(jax.random.fold_in(own, position), (shards_of,), jnp.float32, least / len(pieces), top_value / len(pieces)))
        gain = gain * jnp.repeat(steps, extent[position] // shards_of).reshape([-1 if axis == position else 1 for axis in range(len(extent))])
    return gain


def scatter_about(own_key, shape, width, bound, cuts=(), kind=jnp.bfloat16):
    array = width * jax.random.normal(own_key, shape, jnp.float32)
    if cuts:
        array = array * levels(own_key, shape, cuts, -0.22, 0.18)
    return jnp.clip(array, -bound, bound).astype(kind)


def setup_inputs(seed: int = 0) -> dict:
    keys = jax.random.split(jax.random.key(seed), 18)
    return {
        "hidden_in": scatter_about(keys[0], (TOKEN_TOTAL, MODEL_DIM), 1.0, 6.0, ((0, 8),)),
        "cotangent": scatter_about(keys[1], (TOKEN_TOTAL, MODEL_DIM), 1.0, 6.0, ((0, 8),)),
        "segments": draw_segments(jax.random.fold_in(keys[17], 71), 0),
        "positions": draw_positions(jax.random.fold_in(keys[17], 71), 0),
        "routes": draw_routes(jax.random.fold_in(keys[17], 71), 0),
        "attn_gain": jnp.clip(1.0 + 0.1 * jax.random.normal(keys[5], (MODEL_DIM,), jnp.float32), 0.5, 1.5),
        "w_query": draw_w_query(jax.random.fold_in(keys[17], 71), 0),
        "w_key": draw_w_key(jax.random.fold_in(keys[17], 71), 0),
        "value_weight": scatter_about(keys[8], (MODEL_DIM, KEY_VALUE_HEADS * HEAD_DIM), MODEL_DIM ** -0.5, 0.125, ((1, 4),)),
        "q_gain": draw_q_gain(jax.random.fold_in(keys[17], 71), 0),
        "k_gain": draw_k_gain(jax.random.fold_in(keys[17], 71), 0),
        "w_out": scatter_about(keys[11], (QUERY_HEADS * HEAD_DIM, MODEL_DIM), (QUERY_HEADS * HEAD_DIM // 32) ** -0.5, 0.5, ((0, 4),)),
        "ffn_gain": jnp.clip(1.0 + 0.1 * jax.random.normal(keys[12], (MODEL_DIM,), jnp.float32), 0.5, 1.5),
        "router": draw_router(jax.random.fold_in(keys[17], 71), 0),
        "w_gate": scatter_about(keys[14], (EXPERTS, MODEL_DIM, FF), MODEL_DIM ** -0.5, 0.125, ((0, 8), (2, 4))),
        "w_up": scatter_about(keys[15], (EXPERTS, MODEL_DIM, FF), MODEL_DIM ** -0.5, 0.125, ((0, 8), (2, 4))),
        "w_down": scatter_about(keys[16], (EXPERTS, FF, MODEL_DIM), (FF // 4) ** -0.5, 0.4375, ((0, 8), (1, 4))),
    }


epsilon = 1e-06
rope_base = 1000000.0
far_below = -1e+30

@jax.custom_vjp
def lower_precision(v):
    return lax.optimization_barrier(v.astype(jnp.bfloat16)).astype(jnp.float32)

@jax.custom_vjp
def lower_precision_backward(v):
    return v

def low_keep(v):
    return (lower_precision(v), None)

def low_pass(kept, grad):
    return (grad,)

def back_keep(v):
    return (v, None)

def back_low(kept, grad):
    return (lower_precision(grad),)
lower_precision.defvjp(low_keep, low_pass)
lower_precision_backward.defvjp(back_keep, back_low)

def highest_precision(left, right):
    return jnp.dot(left, right, precision=lax.Precision.HIGHEST, preferred_element_type=jnp.float32)

def rope_tables(positions, head_size):
    half_size = head_size // 2
    frequency = rope_base ** (-(jnp.arange(half_size, dtype=jnp.float32) * 2.0) / head_size)
    angles = positions.astype(jnp.float32)[:, None] * frequency[None, :]
    cosine = jnp.cos(angles)
    sine_table = jnp.sin(angles)
    return (jnp.concatenate([cosine, cosine], -1), jnp.concatenate([sine_table, sine_table], -1))

def rotate(value_rows, cosine, sine_table):
    half_size = value_rows.shape[-1] // 2
    turned = jnp.concatenate([-value_rows[..., half_size:], value_rows[..., :half_size]], -1)
    return value_rows * cosine[:, None, :] + turned * sine_table[:, None, :]

def head_norm(value_rows, gain_vec):
    return value_rows * lax.rsqrt(lax.optimization_barrier(jnp.mean(value_rows * value_rows, -1, keepdims=True)) + epsilon) * gain_vec

def reference(hidden_in, cotangent, segments, positions, routes, attn_gain, w_query, w_key, value_weight, q_gain, k_gain, w_out, ffn_gain, router, w_gate, w_up, w_down):
    block_list = TOKEN_TOTAL // TOKENS_PER_SHARD
    query_group_count = QUERY_HEADS // KEY_VALUE_HEADS
    expert_rows = N_EXPERT * CAP
    score_scale = HEAD_DIM ** (-0.5)
    flat_routes = routes.reshape(-1)
    picked = (flat_routes[:, None] == jnp.arange(EXPERTS, dtype=jnp.int32)[None, :]).astype(jnp.int32)
    running = jnp.cumsum(picked.reshape(block_list, TOKENS_PER_SHARD * TOP, EXPERTS), 1).reshape(TOKEN_TOTAL * TOP, EXPERTS) - 1
    places = lax.optimization_barrier(jnp.sum(picked * running, 1))
    entries = jnp.arange(TOKEN_TOTAL * TOP, dtype=jnp.int32)
    slot_index = flat_routes * expert_rows + entries // (TOP * TOKENS_PER_SHARD) * CAP + places
    row_table = jnp.zeros((EXPERTS * expert_rows,), jnp.int32).at[slot_index].set(entries // TOP).reshape(EXPERTS, expert_rows)
    cosine, sine_table = rope_tables(positions, HEAD_DIM)
    token_index = jnp.arange(TOKENS_PER_SHARD, dtype=jnp.int32)
    causal = token_index[:, None] >= token_index[None, :]
    document_block_table = segments.reshape(block_list, TOKENS_PER_SHARD)

    def attend_heads(block_parts):
        query_rows, keys_rotated, value_rows, seg_block = block_parts
        keys_all = jnp.repeat(keys_rotated, query_group_count, axis=1)
        values_all = jnp.repeat(value_rows, query_group_count, axis=1)
        scores = lower_precision_backward(jnp.einsum('thd,shd->hts', query_rows, keys_all, precision=lax.Precision.HIGHEST) * score_scale)
        allowed = (seg_block[:, None] == seg_block[None, :]) & causal
        scores = jnp.where(allowed[None], scores, far_below)
        exponent = jnp.exp(scores - lax.optimization_barrier(jnp.max(scores, -1, keepdims=True)))
        probability = lower_precision(exponent / lax.optimization_barrier(jnp.sum(exponent, -1, keepdims=True)))
        return jnp.einsum('hts,shd->thd', probability, values_all, precision=lax.Precision.HIGHEST)

    def forward(inputs, attn_scale, query_proj, key_projected, value_projected, query_scale, key_scale, out_proj, ffn_scale, router_proj, gate_proj, up_proj, down_proj):
        inv_first = lax.rsqrt(lax.optimization_barrier(jnp.mean(inputs * inputs, -1, keepdims=True)) + epsilon)
        normalized_input = lower_precision(inputs * inv_first * attn_scale)
        query_raw = lower_precision_backward(highest_precision(normalized_input, query_proj)).reshape(TOKEN_TOTAL, QUERY_HEADS, HEAD_DIM)
        key_unrotated = lower_precision_backward(highest_precision(normalized_input, key_projected)).reshape(TOKEN_TOTAL, KEY_VALUE_HEADS, HEAD_DIM)
        value_rows = lower_precision_backward(lower_precision(highest_precision(normalized_input, value_projected))).reshape(TOKEN_TOTAL, KEY_VALUE_HEADS, HEAD_DIM)
        query_rows = lower_precision(rotate(head_norm(query_raw, query_scale), cosine, sine_table))
        keys_rotated = lower_precision(rotate(head_norm(key_unrotated, key_scale), cosine, sine_table))
        attended_rows = lax.map(jax.checkpoint(attend_heads), (query_rows.reshape(block_list, TOKENS_PER_SHARD, QUERY_HEADS, HEAD_DIM), keys_rotated.reshape(block_list, TOKENS_PER_SHARD, KEY_VALUE_HEADS, HEAD_DIM), value_rows.reshape(block_list, TOKENS_PER_SHARD, KEY_VALUE_HEADS, HEAD_DIM), document_block_table))
        attended_rows = lower_precision_backward(lower_precision(attended_rows.reshape(TOKEN_TOTAL, QUERY_HEADS * HEAD_DIM)))
        residual = inputs + lower_precision_backward(highest_precision(attended_rows, out_proj))
        inv_second = lax.rsqrt(lax.optimization_barrier(jnp.mean(residual * residual, -1, keepdims=True)) + epsilon)
        normed_ffn = lower_precision(residual * inv_second * ffn_scale)
        logits = lower_precision_backward(highest_precision(normed_ffn, router_proj))
        chosen = jnp.take_along_axis(logits, routes, 1)
        exponent = jnp.exp(chosen - lax.optimization_barrier(jnp.max(chosen, -1, keepdims=True)))
        gate_weights = exponent / lax.optimization_barrier(jnp.sum(exponent, -1, keepdims=True))

        def expert(block_parts):
            token_rows, gate_mat, up_mat, down_mat = block_parts
            gathered = lower_precision_backward(normed_ffn[token_rows])
            gate_pre = lower_precision_backward(highest_precision(gathered, gate_mat))
            up_pre = lower_precision_backward(highest_precision(gathered, up_mat))
            middle = lower_precision(jax.nn.silu(gate_pre) * up_pre)
            return lower_precision_backward(lower_precision(highest_precision(middle, down_mat)))
        outputs = lax.map(jax.checkpoint(expert), (row_table, gate_proj, up_proj, down_proj))
        routed = outputs.reshape(EXPERTS * expert_rows, MODEL_DIM)[slot_index].reshape(TOKEN_TOTAL, TOP, MODEL_DIM)
        return residual + lax.optimization_barrier(jnp.sum(gate_weights[:, :, None] * routed, 1))
    floats = (hidden_in.astype(jnp.float32), attn_gain, w_query.astype(jnp.float32), w_key.astype(jnp.float32), value_weight.astype(jnp.float32), q_gain, k_gain, w_out.astype(jnp.float32), ffn_gain, router.astype(jnp.float32), w_gate.astype(jnp.float32), w_up.astype(jnp.float32), w_down.astype(jnp.float32))
    layer_out, pullback = jax.vjp(forward, *floats)
    grads = pullback(cotangent.astype(jnp.float32))
    return (layer_out.astype(jnp.bfloat16), grads[0], grads[1], grads[2], grads[3], grads[4], grads[5], grads[6], grads[7], grads[8], grads[9], grads[10], grads[11], grads[12])
```

```python
import jax
import jax.numpy as jnp
from jax import lax
from jax.sharding import PartitionSpec as P

epsilon = 1e-06
rope_base = 1000000.0
far_below = -1e30


def rope_tables(positions, head_size):
    half_size = head_size // 2
    frequency = rope_base ** (-(jnp.arange(half_size, dtype=jnp.float32) * 2.0) / head_size)
    angles = positions.astype(jnp.float32)[:, None] * frequency[None, :]
    cosine = jnp.cos(angles)
    sine_table = jnp.sin(angles)
    return (jnp.concatenate([cosine, cosine], -1), jnp.concatenate([sine_table, sine_table], -1))


def rotate(value_rows, cosine, sine_table):
    half_size = value_rows.shape[-1] // 2
    turned = jnp.concatenate([-value_rows[..., half_size:], value_rows[..., :half_size]], -1)
    return value_rows * cosine[:, None, :] + turned * sine_table[:, None, :]


def rotate_back(gradient, cosine, sine_table):
    half_size = gradient.shape[-1] // 2
    scaled = gradient * sine_table[:, None, :]
    return gradient * cosine[:, None, :] + jnp.concatenate(
        [scaled[..., half_size:], -scaled[..., :half_size]], -1
    )


def norm_back(grad_scaled, value_rows, scales):
    return scales * (
        grad_scaled
        - value_rows * scales * scales * jnp.mean(grad_scaled * value_rows, -1, keepdims=True)
    )


def bf(value):
    return value.astype(jnp.bfloat16)


def mm(left, right, contract=(1, 0)):
    return lax.dot_general(
        left, right, (((contract[0],), (contract[1],)), ((), ())), preferred_element_type=jnp.float32
    )


def swap(value, step):
    size = lax.axis_size("tensor")
    return lax.ppermute(value, "tensor", [(i, i ^ step) for i in range(size)])


class Tokens:
    def __init__(self):
        self.size = lax.axis_size("expert")
        self.line = self.size == 8
        self.me = lax.axis_index("expert")

    def across(self, value, ranks=range(4)):
        pairs = [(z * 2 + y, z * 2 + 1 - y) for z in ranks for y in range(2)]
        return lax.ppermute(value, "expert", pairs)

    def along(self, value, step, ranks):
        pairs = [(z * 2 + y, (z + step) * 2 + y) for z in ranks for y in range(2)]
        return lax.ppermute(value, "expert", pairs)

    def gather(self, own):
        if not self.line:
            return lax.all_gather(own, "expert", axis=0, tiled=False)
        up = [self.along(own, 1, (0, 1, 2))]
        down = [self.along(own, -1, (1, 2, 3))]
        other = self.across(own)
        up.append(self.along(up[0], 1, (1, 2)))
        down.append(self.along(down[0], -1, (1, 2)))
        up_other = [self.across(up[0], (1, 2, 3))]
        down_other = [self.across(down[0], (0, 1, 2))]
        up.append(self.along(up[1], 1, (2,)))
        down.append(self.along(down[1], -1, (1,)))
        up_other.append(self.across(up[1], (2, 3)))
        down_other.append(self.across(down[1], (0, 1)))
        up_other.append(self.across(up[2], (3,)))
        down_other.append(self.across(down[2], (0,)))
        z = self.me // 2
        same = [own] + [jnp.where(z >= 3 - i, up[2 - i], down[i]) for i in range(3)]
        rest = [other] + [jnp.where(z >= 3 - i, up_other[2 - i], down_other[i]) for i in range(3)]
        return jnp.stack(same + rest)

    def scatter(self, parts):
        if not self.line:
            return lax.psum_scatter(parts, "expert", scatter_dimension=0, tiled=False).astype(
                jnp.float32
            )
        sums = [None] * 4
        for i in (3, 1, 2, 0):
            sums[i] = parts[i].astype(jnp.float32) + self.across(parts[4 + i]).astype(jnp.float32)
        up = self.along(bf(sums[3]), 1, (0,)).astype(jnp.float32)
        down = self.along(bf(sums[1]), -1, (3,)).astype(jnp.float32)
        up = self.along(bf(sums[2] + up), 1, (0, 1)).astype(jnp.float32)
        down = self.along(bf(sums[2] + down), -1, (2, 3)).astype(jnp.float32)
        up = self.along(bf(sums[1] + up), 1, (0, 1, 2)).astype(jnp.float32)
        down = self.along(bf(sums[3] + down), -1, (1, 2, 3)).astype(jnp.float32)
        return sums[0] + up + down

    def places(self):
        p = jnp.arange(self.size, dtype=jnp.int32)
        if not self.line:
            return p
        z, y = self.me // 2, self.me % 2
        return (z + p % 4) % 4 * 2 + (y ^ (p // 4))

    def slots(self):
        a = jnp.arange(self.size, dtype=jnp.int32)
        if not self.line:
            return a
        z, y = self.me // 2, self.me % 2
        return (a // 2 - z) % 4 + 4 * ((a % 2) ^ y)


def pick_blocks(blocks, index):
    return jnp.stack([lax.dynamic_index_in_dim(blocks, index[i], 0, False) for i in range(blocks.shape[0])])


def body(
    hidden_in,
    cotangent,
    segments,
    positions,
    routes,
    attn_gain,
    w_query,
    w_key,
    value_weight,
    q_gain,
    k_gain,
    w_out,
    ffn_gain,
    router,
    w_gate,
    w_up,
    w_down,
):
    tok_count, model_width = hidden_in.shape
    head_size = q_gain.shape[0]
    q_heads = w_query.shape[1] // head_size
    kv_heads = w_key.shape[1] // head_size
    query_group_count = q_heads // kv_heads
    experts = router.shape[1]
    local_experts, _, hidden = w_gate.shape
    score_scale = head_size ** (-0.5)
    tensor_size = lax.axis_size("tensor")
    tensor_rank = lax.axis_index("tensor")
    expert_rank = lax.axis_index("expert")
    shard_rows = tok_count // tensor_size
    order = Tokens()
    group = order.size
    places, slots = order.places(), order.slots()

    def own_rows(value):
        return lax.dynamic_slice_in_dim(value, tensor_rank * shard_rows, shard_rows)

    cot_own = own_rows(cotangent)
    grad_all = lax.all_gather(cot_own, "expert", axis=0, tiled=False)
    grad_all = pick_blocks(grad_all, places).reshape(group * shard_rows, model_width)
    expert_ids = jnp.arange(experts, dtype=jnp.int32)
    routes_own = own_rows(routes)
    routes_all = lax.all_gather(routes_own, "expert", axis=0, tiled=False)
    routes_all = pick_blocks(routes_all, places).reshape(group * shard_rows, -1)

    def mask_of(route_rows):
        return jnp.any(route_rows[:, :, None] == expert_ids[None, None, :], 1)

    mask_own, mask_all = mask_of(routes_own), mask_of(routes_all)
    in_own = jnp.concatenate(
        [w_gate[i] for i in range(local_experts)] + [w_up[i] for i in range(local_experts)], 1
    )
    down_own = w_down.reshape(local_experts * hidden, model_width)
    in_far, down_far = swap(in_own, 2), swap(down_own, 2)
    in_mats = [in_own, swap(in_own, 1), in_far, swap(in_far, 1)]
    down_mats = [down_own, swap(down_own, 1), down_far, swap(down_far, 1)]

    inputs = hidden_in.astype(jnp.float32)
    inv_first = lax.rsqrt(jnp.mean(inputs * inputs, -1, keepdims=True) + epsilon)
    normalized_input = (inputs * inv_first * attn_gain).astype(jnp.bfloat16)
    query_raw = jnp.dot(normalized_input, w_query, preferred_element_type=jnp.float32).reshape(
        tok_count, q_heads, head_size
    )
    key_unrotated = jnp.dot(normalized_input, w_key, preferred_element_type=jnp.float32).reshape(
        tok_count, kv_heads, head_size
    )
    value_rows = (
        jnp.dot(normalized_input, value_weight, preferred_element_type=jnp.float32)
        .astype(jnp.bfloat16)
        .reshape(tok_count, kv_heads, head_size)
    )
    cosine, sine_table = rope_tables(positions, head_size)
    query_inv = lax.rsqrt(jnp.mean(query_raw * query_raw, -1, keepdims=True) + epsilon)
    key_inv = lax.rsqrt(jnp.mean(key_unrotated * key_unrotated, -1, keepdims=True) + epsilon)
    query_hat = query_raw * query_inv
    key_hat = key_unrotated * key_inv
    query_rows = (
        rotate(query_hat * q_gain, cosine, sine_table)
        .astype(jnp.bfloat16)
        .reshape(tok_count, kv_heads, query_group_count, head_size)
    )
    keys_rotated = rotate(key_hat * k_gain, cosine, sine_table).astype(jnp.bfloat16)
    token_index = jnp.arange(tok_count, dtype=jnp.int32)
    allowed = (segments[:, None] == segments[None, :]) & (
        token_index[:, None] >= token_index[None, :]
    )

    def scores_of():
        raw_scores = (
            jnp.einsum(
                "tkgd,skd->kgts", query_rows, keys_rotated, preferred_element_type=jnp.float32
            )
            * score_scale
        )
        return jnp.where(allowed, raw_scores, far_below)

    scores = scores_of()
    top_score = jnp.max(scores, -1, keepdims=True)
    log_total = top_score + jnp.log(jnp.sum(jnp.exp(scores - top_score), -1, keepdims=True))
    prob_low = jnp.exp(scores - log_total).astype(jnp.bfloat16)
    attended_rows = (
        jnp.einsum("kgts,skd->tkgd", prob_low, value_rows, preferred_element_type=jnp.float32)
        .astype(jnp.bfloat16)
        .reshape(tok_count, q_heads * head_size)
    )

    pair_count = tensor_size // 2

    def reduce_rows(part):
        part = part.reshape(pair_count, 2, shard_rows, model_width)
        low = tensor_rank % 2
        keep = lax.dynamic_index_in_dim(part, low, 1, False)
        give = lax.dynamic_index_in_dim(part, 1 - low, 1, False)
        half = keep.astype(jnp.float32) + swap(bf(give), 1).astype(jnp.float32)
        high = tensor_rank // 2
        keep = lax.dynamic_index_in_dim(half, high, 0, False)
        give = lax.dynamic_index_in_dim(half, 1 - high, 0, False)
        return keep + swap(bf(give), 2).astype(jnp.float32)

    def gather_rows(own):
        far = swap(own, 2)
        high, low = tensor_rank // 2, tensor_rank % 2
        mine = jnp.where(high == 0, jnp.stack([own, far]), jnp.stack([far, own]))
        theirs = swap(mine, 1)
        both = jnp.where(low == 0, jnp.stack([mine, theirs], 1), jnp.stack([theirs, mine], 1))
        return both.reshape(tok_count, model_width)

    attn_sum = reduce_rows(jnp.dot(attended_rows, w_out, preferred_element_type=jnp.float32))
    residual = own_rows(hidden_in).astype(jnp.float32) + attn_sum
    inv_second = lax.rsqrt(jnp.mean(residual * residual, -1, keepdims=True) + epsilon)
    normed_ffn = (residual * inv_second * ffn_gain).astype(jnp.bfloat16)

    def gates_of(rows, mask):
        logits = jnp.where(mask, mm(rows, router), far_below)
        return jax.nn.softmax(logits, -1)

    gates_own = gates_of(normed_ffn, mask_own)
    normed_all = order.gather(normed_ffn).reshape(group * shard_rows, model_width)
    gates_all = gates_of(normed_all, mask_all)
    local_gates = lax.dynamic_slice_in_dim(
        gates_all, expert_rank * local_experts, local_experts, 1
    )
    gate_wide = jnp.repeat(local_gates, hidden, axis=1)
    width = local_experts * hidden

    out_part = jnp.zeros((group * shard_rows, model_width), jnp.float32)
    back_part = jnp.zeros((group * shard_rows, model_width), jnp.float32)
    gate_grad_all = jnp.zeros((group * shard_rows, local_experts), jnp.float32)
    pre_grads, gated_middles = [], []
    for in_mat, down_mat in zip(in_mats, down_mats):
        pre = mm(normed_all, in_mat)
        gate_pre, up_pre = pre[:, :width], pre[:, width:]
        sigmoid_gate = jax.nn.sigmoid(gate_pre)
        activated = gate_pre * sigmoid_gate
        middle = activated * up_pre
        gated = bf(middle * gate_wide)
        grad_middle = mm(grad_all, down_mat, (1, 1))
        gate_grad_all = gate_grad_all + jnp.sum(
            (middle * grad_middle).reshape(-1, local_experts, hidden), -1
        )
        grad_middle = grad_middle * gate_wide
        grad_gate_pre = bf(
            grad_middle * up_pre * sigmoid_gate * (1.0 + gate_pre * (1.0 - sigmoid_gate))
        )
        grad_up_pre = bf(grad_middle * activated)
        pre_grad = jnp.concatenate([grad_gate_pre, grad_up_pre], 1)
        back_part = back_part + mm(pre_grad, in_mat, (1, 1))
        out_part = out_part + mm(gated, down_mat)
        pre_grads.append(pre_grad)
        gated_middles.append(gated)

    gate_grad_send = pick_blocks(
        gate_grad_all.T.reshape(local_experts, group, shard_rows).transpose(1, 0, 2), slots
    )
    gate_grad_own = (
        lax.all_to_all(gate_grad_send, "expert", split_axis=0, concat_axis=0, tiled=True)
        .reshape(experts, shard_rows)
        .T
    )
    back_sum = order.scatter(bf(back_part).reshape(group, shard_rows, model_width))
    out_blocks = pick_blocks(bf(out_part).reshape(group, shard_rows, model_width), slots)
    out_sum = lax.psum_scatter(out_blocks, "expert", scatter_dimension=0, tiled=False)
    layer_out = gather_rows(bf(residual + out_sum.astype(jnp.float32)))

    def weight_grads(step):
        return (
            mm(normed_all, pre_grads[step], (0, 0)),
            mm(gated_middles[step], grad_all, (0, 0)),
        )

    def give(parts, step):
        return [swap(bf(part), step).astype(jnp.float32) for part in parts]

    near = give(weight_grads(1), 1)
    far = give(weight_grads(3), 1)
    far = give([a + b for a, b in zip(weight_grads(2), far)], 2)
    in_grad, down_grad = [a + b + c for a, b, c in zip(weight_grads(0), near, far)]
    w_gate_grad = jnp.stack([in_grad[:, i * hidden : (i + 1) * hidden] for i in range(local_experts)])
    w_up_grad = jnp.stack(
        [in_grad[:, width + i * hidden : width + (i + 1) * hidden] for i in range(local_experts)]
    )
    w_down_grad = down_grad.reshape(local_experts, hidden, model_width)

    grad_out = cot_own.astype(jnp.float32)
    grad_chosen = gates_own * (
        gate_grad_own - jnp.sum(gates_own * gate_grad_own, -1, keepdims=True)
    )
    grad_logits = bf(jnp.where(mask_own, grad_chosen, 0.0))
    router_part = mm(normed_ffn, grad_logits, (0, 0))
    grad_normed_ffn = back_sum + mm(grad_logits, router, (1, 1))
    ffn_gain_part = jnp.sum(grad_normed_ffn * residual * inv_second, 0)
    grad_residual = grad_out + norm_back(grad_normed_ffn * ffn_gain, residual, inv_second)
    grad_attn = gather_rows(bf(grad_residual))
    w_out_part = bf(mm(attended_rows, grad_attn, (0, 0)))
    w_out_grad = lax.psum_scatter(w_out_part, "expert", scatter_dimension=1, tiled=True).astype(
        jnp.float32
    )
    grad_attended = bf(mm(grad_attn, w_out, (1, 1))).reshape(
        tok_count, kv_heads, query_group_count, head_size
    )
    probability = jnp.exp(scores_of() - log_total)
    prob_again = probability.astype(jnp.bfloat16)
    grad_prob = jnp.einsum(
        "tkgd,skd->kgts", grad_attended, value_rows, preferred_element_type=jnp.float32
    )
    grad_scores = (
        probability * (grad_prob - jnp.sum(probability * grad_prob, -1, keepdims=True))
    ).astype(jnp.bfloat16)
    grad_queries = (
        jnp.einsum("kgts,skd->tkgd", grad_scores, keys_rotated, preferred_element_type=jnp.float32)
        * score_scale
    ).reshape(tok_count, q_heads, head_size)
    grad_keys = (
        jnp.einsum("kgts,tkgd->skd", grad_scores, query_rows, preferred_element_type=jnp.float32)
        * score_scale
    )
    grad_values = (
        jnp.einsum("kgts,tkgd->skd", prob_again, grad_attended, preferred_element_type=jnp.float32)
        .astype(jnp.bfloat16)
        .reshape(tok_count, kv_heads * head_size)
    )
    grad_query_rot = rotate_back(grad_queries, cosine, sine_table)
    grad_key_rot = rotate_back(grad_keys, cosine, sine_table)
    q_gain_part = jnp.sum((grad_query_rot * query_hat).reshape(-1, head_size), 0)
    k_gain_part = jnp.sum((grad_key_rot * key_hat).reshape(-1, head_size), 0)
    grad_query_raw = (
        norm_back(grad_query_rot * q_gain, query_raw, query_inv)
        .astype(jnp.bfloat16)
        .reshape(tok_count, q_heads * head_size)
    )
    grad_key_raw = (
        norm_back(grad_key_rot * k_gain, key_unrotated, key_inv)
        .astype(jnp.bfloat16)
        .reshape(tok_count, kv_heads * head_size)
    )
    grad_heads = jnp.concatenate([grad_query_raw, grad_key_raw, grad_values], 1)
    grad_normed_part = (
        mm(grad_query_raw, w_query, (1, 1))
        + mm(grad_key_raw, w_key, (1, 1))
        + mm(grad_values, value_weight, (1, 1))
    )
    attn_gain_part = jnp.sum(grad_normed_part * inputs * inv_first, 0)
    grad_normed = reduce_rows(grad_normed_part)
    inputs_own, inv_own = own_rows(inputs), own_rows(inv_first)
    input_grad = gather_rows(
        bf(grad_residual + norm_back(grad_normed * attn_gain, inputs_own, inv_own))
    ).astype(jnp.float32)

    heads_part = mm(normalized_input, grad_heads, (0, 0))
    small_width = 128
    gain_rows = jnp.stack([q_gain_part, k_gain_part], 1).reshape(group, -1, 2)
    gain_cols = jnp.pad(
        gain_rows, ((0, 0), (0, model_width // group - gain_rows.shape[1]), (0, 0))
    ).reshape(model_width, 2)
    small = jnp.concatenate([attn_gain_part[:, None], ffn_gain_part[:, None], gain_cols, router_part], 1)
    small = jnp.pad(small, ((0, 0), (0, small_width - small.shape[1])))
    packed = lax.psum_scatter(
        bf(jnp.concatenate([heads_part, small], 1)), "expert", scatter_dimension=0, tiled=True
    )
    query_width, key_width = w_query.shape[1], w_key.shape[1]
    w_query_grad = packed[:, :query_width].astype(jnp.float32)
    w_key_grad = packed[:, query_width : query_width + key_width].astype(jnp.float32)
    w_value_grad = packed[:, query_width + key_width : query_width + 2 * key_width].astype(jnp.float32)
    small = packed[:, query_width + 2 * key_width :]
    small = small.astype(jnp.float32) + swap(small, 1).astype(jnp.float32)
    small = small + swap(bf(small), 2).astype(jnp.float32)
    gain_count = head_size // group
    return (
        layer_out,
        input_grad,
        small[:, 0],
        w_query_grad,
        w_key_grad,
        w_value_grad,
        small[:gain_count, 2],
        small[:gain_count, 3],
        w_out_grad,
        small[:, 1],
        small[:, 4 : 4 + experts],
        w_gate_grad,
        w_up_grad,
        w_down_grad,
    )


def solution(mesh):
    placed = (
        P("expert", None),
        P("expert", None),
        P("expert"),
        P("expert"),
        P("expert", None),
        P(),
        P(None, "tensor"),
        P(None, "tensor"),
        P(None, "tensor"),
        P(),
        P(),
        P("tensor", None),
        P(),
        P(),
        P("expert", None, "tensor"),
        P("expert", None, "tensor"),
        P("expert", "tensor", None),
    )
    return jax.shard_map(
        body,
        mesh=mesh,
        in_specs=placed,
        out_specs=(
            P("expert", None),
            P("expert", None),
            P("expert"),
            P("expert", "tensor"),
            P("expert", "tensor"),
            P("expert", "tensor"),
            P("expert"),
            P("expert"),
            P("tensor", "expert"),
            P("expert"),
            P("expert", None),
            P("expert", None, "tensor"),
            P("expert", None, "tensor"),
            P("expert", "tensor", None),
        ),
        check_vma=False,
    )
```

```python
import functools

import jax
import jax.numpy as jnp
from jax import lax
from jax.experimental import pallas as pl
from jax.experimental.pallas import tpu as pltpu
from jax.sharding import PartitionSpec as P

epsilon = 1e-06
rope_base = 1000000.0
far_below = -1e30


def rope_tables(positions, head_size):
    half_size = head_size // 2
    frequency = rope_base ** (-(jnp.arange(half_size, dtype=jnp.float32) * 2.0) / head_size)
    angles = positions.astype(jnp.float32)[:, None] * frequency[None, :]
    cosine = jnp.cos(angles)
    sine_table = jnp.sin(angles)
    return (jnp.concatenate([cosine, cosine], -1), jnp.concatenate([sine_table, sine_table], -1))


def norm_back(grad_scaled, value_rows, scales):
    return scales * (
        grad_scaled
        - value_rows * scales * scales * jnp.mean(grad_scaled * value_rows, -1, keepdims=True)
    )


def bf(value):
    return value.astype(jnp.bfloat16)


def mm(left, right, contract=(1, 0)):
    return lax.dot_general(
        left, right, (((contract[0],), (contract[1],)), ((), ())), preferred_element_type=jnp.float32
    )


def after(values, first):
    if first is None:
        return values
    return lax.optimization_barrier((*values, first))[: len(values)]


def swap(value, step):
    size = lax.axis_size("tensor")
    return lax.ppermute(value, "tensor", [(i, i ^ step) for i in range(size)])


vmem_bytes = 58 * 2**20
small_cost = pl.CostEstimate(flops=2**20, bytes_accessed=2**16, transcendentals=0)


def whole(shape):
    return pl.BlockSpec(shape, lambda *_: (0,) * len(shape))


def turn(rows):
    return pltpu.roll(rows, rows.shape[-1] // 2, 1)


def inverse_rms(rows):
    return lax.rsqrt(jnp.mean(rows * rows, -1, keepdims=True) + epsilon)


def split_rows(rank_ref, total, keep, give):
    rows = keep.shape[1]
    low = rank_ref[0] % 2
    for high in range(keep.shape[0]):
        start = pl.multiple_of((2 * high + low) * rows, rows)
        keep[high] = total[pl.ds(start, rows), :]
        start = pl.multiple_of((2 * high + 1 - low) * rows, rows)
        give[high] = bf(total[pl.ds(start, rows), :])


def attend_kernel(
    rank_ref, x, gain, w_query, w_key, w_value, q_gain, k_gain, cosine, sine, seg_col, seg_row, w_out,
    xn, qp, kp, q, k, v, prob, o, keep, give, total,
):
    step, steps = pl.program_id(0), pl.num_programs(0)
    tokens, head = kp.shape
    cut = keep.shape[1]

    @pl.when(step == 0)
    def _():
        @pl.loop(0, tokens // cut)
        def _(i):
            rows = pl.ds(pl.multiple_of(i * cut, cut), cut)
            value = x[rows, :].astype(jnp.float32)
            xn[rows, :] = bf(value * inverse_rms(value) * gain[...])

        raw = mm(xn[...], w_key[...])
        kp[...] = raw
        scaled = raw * inverse_rms(raw) * k_gain[...]
        k[...] = bf(scaled * cosine[...] + turn(scaled) * sine[...])
        v[...] = bf(mm(xn[...], w_value[...]))
        total[...] = jnp.zeros_like(total)

    raw_pair = mm(xn[...], w_query[...])
    qp[...] = raw_pair
    visible = (seg_col[...] == seg_row[...]) & (
        lax.broadcasted_iota(jnp.int32, (tokens, tokens), 0)
        >= lax.broadcasted_iota(jnp.int32, (tokens, tokens), 1)
    )
    for i in range(prob.shape[0]):
        cols = slice(i * head, (i + 1) * head)
        raw = raw_pair[:, cols]
        scaled = raw * inverse_rms(raw) * q_gain[...]
        rows = bf(scaled * cosine[...] + turn(scaled) * sine[...])
        q[:, cols] = rows
        scores = jnp.where(visible, mm(rows, k[...], (1, 1)) * head**-0.5, far_below)
        weight = jnp.exp(scores - jnp.max(scores, -1, keepdims=True))
        low = bf(weight * (1.0 / jnp.sum(weight, -1, keepdims=True)))
        prob[i] = low
        o[:, cols] = bf(mm(low, v[...]))
    wide = 512

    @pl.loop(0, total.shape[1] // wide)
    def _(n):
        at = pl.ds(pl.multiple_of(n * wide, wide), wide)
        total[:, at] += mm(o[...], w_out[:, at])

    @pl.when(step == steps - 1)
    def _():
        split_rows(rank_ref, total, keep, give)


def attend(rank, x, gain, w_query, w_key, w_value, q_gain, k_gain, cosine, sine, segments, w_out, cut):
    tokens, width = x.shape
    head = q_gain.shape[0]
    query = w_query.shape[1]
    pair = 2
    steps = query // (pair * head)
    heads = pl.BlockSpec((tokens, pair * head), lambda j, _: (0, j))
    halves = tokens // cut // 2
    return pl.pallas_call(
        attend_kernel,
        grid_spec=pltpu.PrefetchScalarGridSpec(
            num_scalar_prefetch=1,
            grid=(steps,),
            in_specs=[
                whole((tokens, width)),
                whole((1, width)),
                pl.BlockSpec((width, pair * head), lambda j, _: (0, j)),
                whole((width, head)),
                whole((width, head)),
                whole((1, head)),
                whole((1, head)),
                whole((tokens, head)),
                whole((tokens, head)),
                whole((tokens, 1)),
                whole((1, tokens)),
                pl.BlockSpec((pair * head, width), lambda j, _: (j, 0)),
            ],
            out_specs=[
                whole((tokens, width)),
                heads,
                whole((tokens, head)),
                heads,
                whole((tokens, head)),
                whole((tokens, head)),
                pl.BlockSpec((pair, tokens, tokens), lambda j, _: (j, 0, 0)),
                heads,
                whole((halves, cut, width)),
                whole((halves, cut, width)),
            ],
            scratch_shapes=[pltpu.VMEM((tokens, width), jnp.float32)],
        ),
        out_shape=[
            jax.ShapeDtypeStruct((tokens, width), jnp.bfloat16),
            jax.ShapeDtypeStruct((tokens, query), jnp.float32),
            jax.ShapeDtypeStruct((tokens, head), jnp.float32),
            jax.ShapeDtypeStruct((tokens, query), jnp.bfloat16),
            jax.ShapeDtypeStruct((tokens, head), jnp.bfloat16),
            jax.ShapeDtypeStruct((tokens, head), jnp.bfloat16),
            jax.ShapeDtypeStruct((query // head, tokens, tokens), jnp.bfloat16),
            jax.ShapeDtypeStruct((tokens, query), jnp.bfloat16),
            jax.ShapeDtypeStruct((halves, cut, width), jnp.float32),
            jax.ShapeDtypeStruct((halves, cut, width), jnp.bfloat16),
        ],
        compiler_params=pltpu.CompilerParams(vmem_limit_bytes=vmem_bytes),
        cost_estimate=small_cost,
        name="attend",
    )(
        rank, x, gain[None], w_query, w_key, w_value, q_gain[None], k_gain[None], cosine, sine,
        segments[:, None], segments[None, :], w_out,
    )


def attend_back_kernel(
    rank_ref, x, xn, dattn, w_query, w_key, w_value, q_gain, k_gain, cosine, sine, w_out, qp, kp, q, k, v, prob,
    packed, gains, attn_gain, keep, give, total, dk, dv, low,
):
    step, steps = pl.program_id(0), pl.num_programs(0)
    tokens, head = kp.shape
    cut = keep.shape[1]
    scale = head**-0.5
    width = x.shape[1]
    wide = 512
    blocks = packed.shape[0]
    block_rows = width // blocks

    def unrotate(grad):
        return grad * cosine[...] - turn(grad) * sine[...]

    def unnorm(grad, raw, inverse, gain):
        scaled = grad * gain
        return inverse * (scaled - raw * inverse * inverse * jnp.mean(scaled * raw, -1, keepdims=True))

    def add_total(left, right, at):
        total[:, at] += mm(left, right[at, :], (1, 1))

    def put_packed(n):
        at = pl.ds(pl.multiple_of(n * wide, wide), wide)
        grad = bf(mm(xn[:, at], low[...], (0, 0)))
        many = wide // block_rows
        first = n * many
        packed[pl.ds(first, many), pl.ds(0, block_rows), :] = grad.reshape(many, block_rows, -1)

    @pl.when(step == 0)
    def _():
        total[...] = jnp.zeros_like(total)
        dk[...] = jnp.zeros_like(dk)
        dv[...] = jnp.zeros_like(dv)
        gains[...] = jnp.zeros_like(gains)

    @pl.when(step < steps - 1)
    def _():
        dout_pair = bf(mm(dattn[...], w_out[...], (1, 1)))
        for i in range(prob.shape[0]):
            cols = slice(i * head, (i + 1) * head)
            dout = dout_pair[:, cols]
            weight = prob[i]
            dp = mm(dout, v[...], (1, 1))
            wide_weight = weight.astype(jnp.float32)
            ds = bf(wide_weight * (dp - jnp.sum(wide_weight * dp, -1, keepdims=True)))
            dv[...] += mm(weight, dout, (0, 0))
            dk[...] += mm(ds, q[:, cols], (0, 0))
            dqu = unrotate(mm(ds, k[...]) * scale)
            raw = qp[:, cols]
            inverse = inverse_rms(raw)
            gains[0:1, :] += jnp.sum(dqu * raw * inverse, 0, keepdims=True)
            low[:, cols] = bf(unnorm(dqu, raw, inverse, q_gain[...]))

        @pl.loop(0, width // wide)
        def _(n):
            put_packed(n)
            add_total(low[...], w_query, pl.ds(pl.multiple_of(n * wide, wide), wide))

    @pl.when(step == steps - 1)
    def _():
        dku = unrotate(dk[...] * scale)
        raw = kp[...]
        inverse = inverse_rms(raw)
        gains[1:2, :] = jnp.sum(dku * raw * inverse, 0, keepdims=True)
        low[:, :head] = bf(unnorm(dku, raw, inverse, k_gain[...]))
        low[:, head:] = bf(dv[...])

        @pl.loop(0, width // wide)
        def _(n):
            put_packed(n)
            at = pl.ds(pl.multiple_of(n * wide, wide), wide)
            add_total(low[:, :head], w_key, at)
            add_total(low[:, head:], w_value, at)

        attn_gain[...] = jnp.zeros_like(attn_gain)

        @pl.loop(0, tokens // cut)
        def _(i):
            rows = pl.ds(pl.multiple_of(i * cut, cut), cut)
            value = x[rows, :].astype(jnp.float32)
            attn_gain[...] += jnp.sum(total[rows, :] * value * inverse_rms(value), 0, keepdims=True)

        split_rows(rank_ref, total, keep, give)


def attend_back(
    rank, x, xn, dattn, w_query, w_key, w_value, q_gain, k_gain, cosine, sine, w_out, qp, kp, q, k, v, prob,
    cut, blocks, spare,
):
    tokens, width = x.shape
    head = q_gain.shape[0]
    query = w_query.shape[1]
    pair = 2
    steps = query // (pair * head)
    last = steps - 1
    heads = pl.BlockSpec((tokens, pair * head), lambda j, _: (0, jnp.minimum(j, last)))
    halves = tokens // cut // 2
    block_rows = width // blocks + spare
    return pl.pallas_call(
        attend_back_kernel,
        grid_spec=pltpu.PrefetchScalarGridSpec(
            num_scalar_prefetch=1,
            grid=(steps + 1,),
            in_specs=[
                whole((tokens, width)),
                whole((tokens, width)),
                whole((tokens, width)),
                pl.BlockSpec((width, pair * head), lambda j, _: (0, jnp.minimum(j, last))),
                whole((width, head)),
                whole((width, head)),
                whole((1, head)),
                whole((1, head)),
                whole((tokens, head)),
                whole((tokens, head)),
                pl.BlockSpec((pair * head, width), lambda j, _: (jnp.minimum(j, last), 0)),
                heads,
                whole((tokens, head)),
                heads,
                whole((tokens, head)),
                whole((tokens, head)),
                pl.BlockSpec((pair, tokens, tokens), lambda j, _: (jnp.minimum(j, last), 0, 0)),
            ],
            out_specs=[
                pl.BlockSpec((blocks, block_rows, pair * head), lambda j, _: (0, 0, j)),
                whole((8, head)),
                whole((1, width)),
                whole((halves, cut, width)),
                whole((halves, cut, width)),
            ],
            scratch_shapes=[
                pltpu.VMEM((tokens, width), jnp.float32),
                pltpu.VMEM((tokens, head), jnp.float32),
                pltpu.VMEM((tokens, head), jnp.float32),
                pltpu.VMEM((tokens, pair * head), jnp.bfloat16),
            ],
        ),
        out_shape=[
            jax.ShapeDtypeStruct((blocks, block_rows, query + 2 * head), jnp.bfloat16),
            jax.ShapeDtypeStruct((8, head), jnp.float32),
            jax.ShapeDtypeStruct((1, width), jnp.float32),
            jax.ShapeDtypeStruct((halves, cut, width), jnp.float32),
            jax.ShapeDtypeStruct((halves, cut, width), jnp.bfloat16),
        ],
        compiler_params=pltpu.CompilerParams(vmem_limit_bytes=vmem_bytes),
        cost_estimate=small_cost,
        name="attend_back",
    )(
        rank, x, xn, dattn, w_query, w_key, w_value, q_gain[None], k_gain[None], cosine, sine, w_out,
        qp, kp, q, k, v, prob,
    )


class Loads:
    def __init__(self, sources, target, sems, shards):
        height = sources[0].shape[0]
        self.each = len(sources) // shards
        self.copies = [
            pltpu.make_async_copy(source, target.at[pl.ds(i * height, height), :], sems.at[i])
            for i, source in enumerate(sources)
        ]

    def start(self):
        for copy in self.copies:
            copy.start()

    def wait(self, shard):
        for copy in self.copies[shard * self.each : (shard + 1) * self.each]:
            copy.wait()


def forward_kernel(rank_ref, hn, routes, router, *rest, shards, local, hidden, top_count):
    in_hbm, down_hbm = rest[: 2 * shards], rest[2 * shards : 3 * shards]
    out, pre_out, gated, gates, gates_wide, in_all, down_all, in_sems, down_sems = rest[3 * shards :]
    chunk, shard = pl.program_id(0), pl.program_id(1)
    width = local * hidden
    rows = hn.shape[0]
    in_loads = Loads(in_hbm, in_all, in_sems, shards)
    down_loads = Loads(down_hbm, down_all, down_sems, shards)

    @pl.when((chunk == 0) & (shard == 0))
    def _():
        in_loads.start()
        down_loads.start()

    @pl.when(shard == 0)
    def _():
        names = lax.broadcasted_iota(jnp.int32, (rows, router.shape[0]), 1).astype(jnp.float32)
        chosen = routes[...].astype(jnp.float32)
        mask = jnp.zeros(names.shape, jnp.bool_)
        for j in range(top_count):
            mask = mask | (chosen[:, j : j + 1] == names)
        logits = jnp.where(mask, mm(hn[...], router[...], (1, 1)), far_below)
        weight = jnp.exp(logits - jnp.max(logits, -1, keepdims=True))
        weight = weight * (1.0 / jnp.sum(weight, -1, keepdims=True))
        lanes = lax.broadcasted_iota(jnp.int32, gates.shape, 1)
        packed = jnp.zeros(gates.shape, jnp.float32)
        for i in range(local):
            here = names == (rank_ref[1] * local + i).astype(jnp.float32)
            value = jnp.sum(jnp.where(here, weight, 0.0), -1, keepdims=True)
            gates_wide[:, i * hidden : (i + 1) * hidden] = jnp.broadcast_to(value, (rows, hidden))
            packed = packed + jnp.where(lanes == i, value, 0.0)
        gates[...] = packed

    for i in range(shards):
        @pl.when((chunk == 0) & (shard == i))
        def _(i=i):
            in_loads.wait(i)

    at = pl.multiple_of(shard * 2 * width, 2 * width)
    pre = mm(hn[...], in_all[pl.ds(at, 2 * width), :], (1, 1))
    pre_out[...] = pre
    middle = jax.nn.silu(pre[:, :width]) * pre[:, width:]
    gated[:, pl.ds(pl.multiple_of(shard * width, width), width)] = bf(middle * gates_wide[...])

    @pl.when(shard == shards - 1)
    def _():
        @pl.when(chunk == 0)
        def _():
            for i in range(shards):
                down_loads.wait(i)

        wide = 512

        @pl.loop(0, out.shape[1] // wide)
        def _(n):
            cols = pl.ds(pl.multiple_of(n * wide, wide), wide)
            out[:, cols] = bf(mm(gated[...], down_all[:, cols]))


def backward_kernel(rank_ref, g, gates, pre_in, *rest, shards, local, hidden):
    in_hbm, down_hbm = rest[: 2 * shards], rest[2 * shards : 3 * shards]
    back, pre_grad, in_all, down_all, totals, in_sems, down_sems = rest[3 * shards :]
    chunk, shard = pl.program_id(0), pl.program_id(1)
    width = local * hidden
    rows, model = g.shape
    in_loads = Loads(in_hbm, in_all, in_sems, shards)
    down_loads = Loads(down_hbm, down_all, down_sems, shards)

    @pl.when((chunk == 0) & (shard == 0))
    def _():
        down_loads.start()
        in_loads.start()

    for i in range(shards):
        @pl.when((chunk == 0) & (shard == i))
        def _(i=i):
            down_loads.wait(i)

    @pl.when(shard == 0)
    def _():
        totals[...] = jnp.zeros_like(totals)

    at = pl.multiple_of(shard * width, width)
    grad_middle_all = mm(g[...], down_all[pl.ds(at, width), :], (1, 1))
    lanes = lax.broadcasted_iota(jnp.int32, totals.shape, 1)
    experts_at = lax.broadcasted_iota(jnp.int32, (rows, width), 1)
    gate_wide = jnp.zeros((rows, width), jnp.float32)
    for e in range(local):
        gate_wide = jnp.where(experts_at // hidden == e, gates[:, e : e + 1], gate_wide)
    gate_pre, up_pre = pre_in[:, :width], pre_in[:, width:]
    sigmoid_gate = jax.nn.sigmoid(gate_pre)
    activated = gate_pre * sigmoid_gate
    product = activated * up_pre * grad_middle_all
    added = jnp.zeros(totals.shape, jnp.float32)
    for e in range(local):
        part = jnp.sum(product[:, e * hidden : (e + 1) * hidden], -1, keepdims=True)
        added = added + jnp.where(lanes == e, part, 0.0)
    totals[...] += added
    grad_middle = grad_middle_all * gate_wide
    at = pl.multiple_of(shard * 2 * width, 2 * width)
    pre_grad[:, pl.ds(at, width)] = bf(
        grad_middle * up_pre * sigmoid_gate * (1.0 + gate_pre * (1.0 - sigmoid_gate))
    )
    pre_grad[:, pl.ds(pl.multiple_of(at + width, width), width)] = bf(grad_middle * activated)

    @pl.when(shard == shards - 1)
    def _():
        @pl.when(chunk == 0)
        def _():
            for i in range(shards):
                in_loads.wait(i)

        wide = 512

        @pl.loop(0, model // wide)
        def _(n):
            cols = pl.ds(pl.multiple_of(n * wide, wide), wide)
            back[:, cols] = bf(mm(pre_grad[...], in_all[:, cols]))

        spare = back.shape[1] - model
        places = lax.broadcasted_iota(jnp.int32, (rows, spare), 1)
        tail = jnp.zeros((rows, spare), jnp.float32)
        for e in range(local):
            value = totals[:, e : e + 1]
            high = bf(value).astype(jnp.float32)
            here = rank_ref[1] * local + e
            tail = tail + jnp.where(places == here, high, 0.0)
            tail = tail + jnp.where(places == spare // 2 + here, value - high, 0.0)
        back[:, model:] = bf(tail)


def expert_specs(tokens, model, shards, width):
    rows = tokens
    while rows > 768:
        rows //= 2

    def block(cols, step=None):
        if step is None:
            return pl.BlockSpec((rows, cols), lambda c, s, _: (c, 0))
        return pl.BlockSpec((rows, cols), lambda c, s, _: (c, s if step < 0 else step))

    scratch = [
        pltpu.VMEM((shards * 2 * width, model), jnp.bfloat16),
        pltpu.VMEM((shards * width, model), jnp.bfloat16),
        pltpu.SemaphoreType.DMA((2 * shards,)),
        pltpu.SemaphoreType.DMA((shards,)),
    ]
    return rows, block, [pl.BlockSpec(memory_space=pl.ANY)] * (3 * shards), scratch


def experts_forward(ranks, hn, sent, router, in_mats, down_mats, local, top_count):
    tokens, model = hn.shape
    shards, width = len(down_mats), down_mats[0].shape[0]
    rows, block, hbm, scratch = expert_specs(tokens, model, shards, width)
    return pl.pallas_call(
        functools.partial(
            forward_kernel, shards=shards, local=local, hidden=width // local, top_count=top_count
        ),
        grid_spec=pltpu.PrefetchScalarGridSpec(
            num_scalar_prefetch=1,
            grid=(tokens // rows, shards),
            in_specs=[block(model), block(128, model // 128), whole(router.shape)] + hbm,
            out_specs=[block(model), block(2 * width, -1), block(shards * width), block(128)],
            scratch_shapes=[pltpu.VMEM((rows, width), jnp.float32)] + scratch,
        ),
        out_shape=[
            jax.ShapeDtypeStruct((tokens, model), jnp.bfloat16),
            jax.ShapeDtypeStruct((tokens, shards * 2 * width), jnp.float32),
            jax.ShapeDtypeStruct((tokens, shards * width), jnp.bfloat16),
            jax.ShapeDtypeStruct((tokens, 128), jnp.float32),
        ],
        compiler_params=pltpu.CompilerParams(vmem_limit_bytes=vmem_bytes),
        cost_estimate=small_cost,
        name="experts_forward",
    )(ranks, hn, sent, router, *in_mats, *down_mats)


def experts_backward(ranks, sent, gates, pre, in_mats, down_mats, local, spare):
    tokens, model = sent.shape[0], down_mats[0].shape[1]
    shards, width = len(down_mats), down_mats[0].shape[0]
    rows, block, hbm, scratch = expert_specs(tokens, model, shards, width)
    return pl.pallas_call(
        functools.partial(backward_kernel, shards=shards, local=local, hidden=width // local),
        grid_spec=pltpu.PrefetchScalarGridSpec(
            num_scalar_prefetch=1,
            grid=(tokens // rows, shards),
            in_specs=[block(model), block(128), block(2 * width, -1)] + hbm,
            out_specs=[block(model + spare), block(shards * 2 * width)],
            scratch_shapes=scratch[:2] + [pltpu.VMEM((rows, 128), jnp.float32)] + scratch[2:],
        ),
        out_shape=[
            jax.ShapeDtypeStruct((tokens, model + spare), jnp.bfloat16),
            jax.ShapeDtypeStruct((tokens, shards * 2 * width), jnp.bfloat16),
        ],
        compiler_params=pltpu.CompilerParams(vmem_limit_bytes=vmem_bytes),
        cost_estimate=small_cost,
        name="experts_backward",
    )(ranks, sent, gates, pre, *in_mats, *down_mats)


def out_grad_kernel(dattn, o, packed):
    packed[...] = bf(mm(dattn[...], o[...], (0, 0))).reshape(packed.shape)


def out_grad(dattn, o, blocks):
    tokens, width = dattn.shape
    cols = o.shape[1]
    rows = width // blocks
    many = max(1, 256 // rows)
    return pl.pallas_call(
        out_grad_kernel,
        grid=(blocks // many,),
        in_specs=[pl.BlockSpec((tokens, many * rows), lambda i: (0, i)), whole(o.shape)],
        out_specs=pl.BlockSpec((many, rows, cols), lambda i: (i, 0, 0)),
        out_shape=jax.ShapeDtypeStruct((blocks, rows, cols), jnp.bfloat16),
        compiler_params=pltpu.CompilerParams(vmem_limit_bytes=vmem_bytes),
        cost_estimate=small_cost,
        name="out_grad",
    )(dattn, o)


class Tokens:
    def __init__(self):
        self.size = lax.axis_size("expert")
        self.line = self.size == 8
        self.me = lax.axis_index("expert")
        self.z, self.y = self.me // 2, self.me % 2

    def across(self, value):
        return lax.ppermute(value, "expert", [(i, i ^ 1) for i in range(8)])

    def along(self, value, step):
        return lax.ppermute(value, "expert", [(i, i ^ (2 * step)) for i in range(8)])

    def place(self, step, other):
        return (self.z ^ step) * 2 + (1 - self.y if other else self.y)

    def gather(self, own, early=None, late=None):
        if not self.line:
            return lax.all_gather(own, "expert", axis=0, tiled=False)
        blocks = [own] + [self.along(own, step) for step in (1, 2, 3)]
        others = [self.across(own)]
        (blocks[1],) = after((blocks[1],), early)
        blocks[2], blocks[3] = after((blocks[2], blocks[3]), late)
        others += [self.across(value) for value in blocks[1:]]
        rows = jnp.zeros((self.size, *own.shape), own.dtype)
        for step in range(4):
            for value, other in ((blocks[step], False), (others[step], True)):
                rows = lax.dynamic_update_index_in_dim(rows, value, self.place(step, other), 0)
        return rows

    def scatter(self, parts, first=None, second=None, last=None):
        if not self.line:
            return lax.psum_scatter(parts, "expert", scatter_dimension=0, tiled=False).astype(
                jnp.float32
            )

        def part(step, other):
            return lax.dynamic_index_in_dim(parts, self.place(step, other), 0, False)

        sums = {}
        for step in (3, 2, 1, 0):
            sums[step] = part(step, False).astype(jnp.float32)
            sums[step] = sums[step] + self.across(part(step, True)).astype(jnp.float32)
        given = {step: bf(sums[step]) for step in (3, 2, 1)}
        (given[2],) = after((given[2],), first)
        (given[1],) = after((given[1],), second)
        arrived = after(tuple(self.along(given[step], step) for step in (3, 2, 1)), last)
        return sums[0] + sum(value.astype(jnp.float32) for value in arrived)


def body(
    hidden_in,
    cotangent,
    segments,
    positions,
    routes,
    attn_gain,
    w_query,
    w_key,
    value_weight,
    q_gain,
    k_gain,
    w_out,
    ffn_gain,
    router,
    w_gate,
    w_up,
    w_down,
):
    tok_count, model_width = hidden_in.shape
    head_size = q_gain.shape[0]
    experts = router.shape[1]
    local_experts, _, hidden = w_gate.shape
    tensor_size = lax.axis_size("tensor")
    tensor_rank = lax.axis_index("tensor")
    expert_rank = lax.axis_index("expert")
    shard_rows = tok_count // tensor_size
    order = Tokens()
    group = order.size

    def own_rows(value):
        return lax.dynamic_slice_in_dim(value, tensor_rank * shard_rows, shard_rows)

    cot_own = own_rows(cotangent)
    routes_own = own_rows(routes)
    spare_cols = 128
    routes_wide = jnp.pad(bf(routes_own), ((0, 0), (0, spare_cols - routes.shape[1])))
    sent_own = jnp.concatenate([cot_own, routes_wide], 1)
    (hidden_in,) = after((hidden_in,), sent_own)
    sent = lax.all_gather(sent_own, "expert", axis=0, tiled=True)
    grad_all = sent[:, :model_width]
    expert_ids = jnp.arange(experts, dtype=jnp.int32)

    def mask_of(route_rows):
        return jnp.any(route_rows[:, :, None] == expert_ids[None, None, :], 1)

    mask_own = mask_of(routes_own)
    own_mats = [value.reshape(local_experts * hidden, model_width) for value in (w_gate.transpose(0, 2, 1), w_up.transpose(0, 2, 1), w_down)]

    cosine, sine_table = rope_tables(positions, head_size)
    half = jnp.arange(head_size, dtype=jnp.int32) < head_size // 2
    sine_table = jnp.where(half, -sine_table, sine_table)
    ranks = jnp.stack([tensor_rank, expert_rank]).astype(jnp.int32)
    normalized_input, qp, kp, q, k, v, prob, attended_rows, keep, give_part = attend(
        ranks, hidden_in, attn_gain, w_query, w_key, value_weight, q_gain, k_gain, cosine, sine_table,
        segments, w_out, shard_rows,
    )

    def reduce_rows(keep, give, first=None):
        half = keep + swap(give, 1).astype(jnp.float32)
        high = tensor_rank // 2
        keep = lax.dynamic_index_in_dim(half, high, 0, False)
        give = bf(lax.dynamic_index_in_dim(half, 1 - high, 0, False))
        (give,) = after((give,), first)
        return keep + swap(give, 2).astype(jnp.float32)

    def gather_rows(own):
        far = swap(own, 2)
        high, low = tensor_rank // 2, tensor_rank % 2
        mine = jnp.where(high == 0, jnp.stack([own, far]), jnp.stack([far, own]))
        theirs = swap(mine, 1)
        both = jnp.where(low == 0, jnp.stack([mine, theirs], 1), jnp.stack([theirs, mine], 1))
        return both.reshape(tok_count, model_width)

    far_gate = swap(own_mats[0], 2)
    attn_sum = reduce_rows(keep, give_part, far_gate)
    residual = own_rows(hidden_in).astype(jnp.float32) + attn_sum
    inv_second = lax.rsqrt(jnp.mean(residual * residual, -1, keepdims=True) + epsilon)
    normed_ffn = (residual * inv_second * ffn_gain).astype(jnp.bfloat16)

    def gates_of(rows, mask):
        logits = jnp.where(mask, mm(rows, router), far_below)
        return jax.nn.softmax(logits, -1)

    gates_own = gates_of(normed_ffn, mask_own)
    far_up = swap(own_mats[1], 2)
    far_mats = [far_gate, far_up, swap(own_mats[2], 2)]
    normed_all = order.gather(normed_ffn, sent, far_up).reshape(group * shard_rows, model_width)
    near_mats = [swap(value, 1) for value in own_mats]
    last_mats = [swap(value, 1) for value in far_mats]
    shards = (own_mats, near_mats, far_mats, last_mats)
    in_mats = [value for shard in shards for value in shard[:2]]
    down_mats = [shard[2] for shard in shards]
    width = local_experts * hidden
    out_part, pre, gated_middles, gates_packed = experts_forward(
        ranks, normed_all, sent, router.T, in_mats, down_mats, local_experts, routes.shape[1]
    )
    out_sum = lax.psum_scatter(
        out_part.reshape(group, shard_rows, model_width), "expert", scatter_dimension=0, tiled=False
    )
    spare_cols = 128 * (-(-2 * experts // 128))
    back_part, pre_grads = experts_backward(
        ranks, sent, gates_packed, pre, in_mats, down_mats, local_experts, spare_cols
    )
    back_sum = order.scatter(back_part.reshape(group, shard_rows, -1), second=out_sum)
    gate_grad_own = (
        back_sum[:, model_width : model_width + experts]
        + back_sum[:, model_width + spare_cols // 2 :][:, :experts]
    )
    back_sum = back_sum[:, :model_width]
    def weight_grads(step):
        cols = slice(step * 2 * width, (step + 1) * 2 * width)
        mids = slice(step * width, (step + 1) * width)
        return mm(pre_grads[:, cols], normed_all, (0, 0)), mm(gated_middles[:, mids], grad_all, (0, 0))

    def give(parts, step):
        return [swap(bf(part), step).astype(jnp.float32) for part in parts]

    far = give(weight_grads(3), 1)
    near = give(weight_grads(1), 1)
    far_part = [bf(a + b) for a, b in zip(weight_grads(2), far)]
    near_part = [a + b for a, b in zip(weight_grads(0), near)]
    far_part = [far_part[0][:width], far_part[0][width:], far_part[1]]
    arrived = give(far_part, 2)
    grad_out = cot_own.astype(jnp.float32)
    grad_chosen = gates_own * (
        gate_grad_own - jnp.sum(gates_own * gate_grad_own, -1, keepdims=True)
    )
    grad_logits = bf(jnp.where(mask_own, grad_chosen, 0.0))
    router_part = mm(normed_ffn, grad_logits, (0, 0))
    grad_normed_ffn = back_sum + mm(grad_logits, router, (1, 1))
    ffn_gain_part = jnp.sum(grad_normed_ffn * residual * inv_second, 0)
    grad_residual = grad_out + norm_back(grad_normed_ffn * ffn_gain, residual, inv_second)
    grad_attn = gather_rows(bf(grad_residual))
    out_blocks = out_grad(grad_attn, attended_rows, group)
    (grad_attn,) = after((grad_attn,), out_blocks)
    w_out_grad = (
        lax.psum_scatter(
            out_blocks, "expert", scatter_dimension=0, tiled=False
        )
        .astype(jnp.float32)
        .T
    )
    slice_rows = model_width // group
    spare = 16
    packed, gain_parts, attn_gain_part, keep, give_part = attend_back(
        ranks, hidden_in, normalized_input, grad_attn, w_query, w_key, value_weight, q_gain, k_gain, cosine,
        sine_table, w_out, qp, kp, q, k, v, prob, shard_rows, group, spare,
    )
    (give_part,) = after((give_part,), arrived[0])
    grad_normed = reduce_rows(keep, give_part)
    layer_out = gather_rows(bf(residual + out_sum.astype(jnp.float32)))
    inputs_own = own_rows(hidden_in).astype(jnp.float32)
    inv_own = lax.rsqrt(jnp.mean(inputs_own * inputs_own, -1, keepdims=True) + epsilon)
    input_grad = gather_rows(
        bf(grad_residual + norm_back(grad_normed * attn_gain, inputs_own, inv_own))
    ).astype(jnp.float32)

    small = jnp.concatenate(
        [
            router_part.reshape(group, -1),
            attn_gain_part.reshape(group, -1),
            ffn_gain_part.reshape(group, -1),
            jnp.broadcast_to(gain_parts[:2].reshape(1, -1), (group, 2 * head_size)),
        ],
        1,
    )
    small = jnp.pad(small, ((0, 0), (0, spare * packed.shape[2] - small.shape[1])))
    packed = lax.dynamic_update_slice(
        packed, bf(small).reshape(group, spare, packed.shape[2]), (0, slice_rows, 0)
    )
    packed = order.scatter(packed, first=arrived[1], second=arrived[2], last=w_out_grad)
    query_width, key_width = w_query.shape[1], w_key.shape[1]
    w_query_grad = packed[:slice_rows, :query_width]
    w_key_grad = packed[:slice_rows, query_width : query_width + key_width]
    w_value_grad = packed[:slice_rows, query_width + key_width :]
    small = packed[slice_rows:]
    small = small + swap(bf(small), 1).astype(jnp.float32)
    small = (small + swap(bf(small), 2).astype(jnp.float32)).reshape(-1)
    cuts = [slice_rows * experts, slice_rows, slice_rows, head_size, head_size]
    router_grad, attn_gain_grad, ffn_gain_grad, q_gain_all, k_gain_all = [
        small[sum(cuts[:i]) : sum(cuts[: i + 1])] for i in range(len(cuts))
    ]
    parts = [near_part[0][:width], near_part[0][width:], near_part[1]]
    gate_t, up_t, w_down_grad = [
        (a + b).reshape(local_experts, hidden, model_width) for a, b in zip(parts, arrived)
    ]
    w_gate_grad, w_up_grad = gate_t.transpose(0, 2, 1), up_t.transpose(0, 2, 1)
    gain_count = head_size // group
    gain_at = expert_rank * gain_count
    return (
        layer_out,
        input_grad,
        attn_gain_grad,
        w_query_grad,
        w_key_grad,
        w_value_grad,
        lax.dynamic_slice_in_dim(q_gain_all, gain_at, gain_count),
        lax.dynamic_slice_in_dim(k_gain_all, gain_at, gain_count),
        w_out_grad,
        ffn_gain_grad,
        router_grad.reshape(slice_rows, experts),
        w_gate_grad,
        w_up_grad,
        w_down_grad,
    )


def solution(mesh):
    placed = (
        P("expert", None),
        P("expert", None),
        P("expert"),
        P("expert"),
        P("expert", None),
        P(),
        P(None, "tensor"),
        P(None, "tensor"),
        P(None, "tensor"),
        P(),
        P(),
        P("tensor", None),
        P(),
        P(),
        P("expert", None, "tensor"),
        P("expert", None, "tensor"),
        P("expert", "tensor", None),
    )
    return jax.shard_map(
        body,
        mesh=mesh,
        in_specs=placed,
        out_specs=(
            P("expert", None),
            P("expert", None),
            P("expert"),
            P("expert", "tensor"),
            P("expert", "tensor"),
            P("expert", "tensor"),
            P("expert"),
            P("expert"),
            P("tensor", "expert"),
            P("expert"),
            P("expert", None),
            P("expert", None, "tensor"),
            P("expert", None, "tensor"),
            P("expert", "tensor", None),
        ),
        check_vma=False,
    )
```

```python
import functools

import jax
import jax.numpy as jnp
from jax import lax
from jax.experimental import pallas as pl
from jax.experimental.pallas import tpu as pltpu
from jax.sharding import PartitionSpec as P

epsilon = 1e-06
rope_base = 1000000.0
far_below = -1e30


def rope_tables(positions, head_size):
    half_size = head_size // 2
    frequency = rope_base ** (-(jnp.arange(half_size, dtype=jnp.float32) * 2.0) / head_size)
    angles = positions.astype(jnp.float32)[:, None] * frequency[None, :]
    cosine = jnp.cos(angles)
    sine_table = jnp.sin(angles)
    return (jnp.concatenate([cosine, cosine], -1), jnp.concatenate([sine_table, sine_table], -1))


def norm_back(grad_scaled, value_rows, scales):
    return scales * (
        grad_scaled
        - value_rows * scales * scales * jnp.mean(grad_scaled * value_rows, -1, keepdims=True)
    )


def bf(value):
    return value.astype(jnp.bfloat16)


def mm(left, right, contract=(1, 0)):
    return lax.dot_general(
        left, right, (((contract[0],), (contract[1],)), ((), ())), preferred_element_type=jnp.float32
    )


def tie(*values):
    return lax.optimization_barrier(values)


def swap(value, step):
    size = lax.axis_size("tensor")
    return lax.ppermute(value, "tensor", [(i, i ^ step) for i in range(size)])


vmem_bytes = 58 * 2**20
small_cost = pl.CostEstimate(flops=2**20, bytes_accessed=2**16, transcendentals=0)


def whole(shape):
    return pl.BlockSpec(shape, lambda *_: (0,) * len(shape))


def turn(rows):
    return pltpu.roll(rows, rows.shape[-1] // 2, 1)


def inverse_rms(rows):
    return lax.rsqrt(jnp.mean(rows * rows, -1, keepdims=True) + epsilon)


def split_rows(rank_ref, total, keep, give):
    rows = keep.shape[1]
    low = rank_ref[0] % 2
    for high in range(keep.shape[0]):
        start = pl.multiple_of((2 * high + low) * rows, rows)
        keep[high] = total[pl.ds(start, rows), :]
        start = pl.multiple_of((2 * high + 1 - low) * rows, rows)
        give[high] = bf(total[pl.ds(start, rows), :])


def attend_kernel(
    rank_ref, x, gain, w_query, w_key, w_value, q_gain, k_gain, cosine, sine, seg_col, seg_row, w_out,
    xn, qp, kp, q, k, v, prob, o, keep, give, total,
):
    step, steps = pl.program_id(0), pl.num_programs(0)
    tokens, head = kp.shape
    cut = keep.shape[1]

    @pl.when(step == 0)
    def _():
        @pl.loop(0, tokens // cut)
        def _(i):
            rows = pl.ds(pl.multiple_of(i * cut, cut), cut)
            value = x[rows, :].astype(jnp.float32)
            xn[rows, :] = bf(value * inverse_rms(value) * gain[...])

        raw = mm(xn[...], w_key[...])
        kp[...] = raw
        scaled = raw * inverse_rms(raw) * k_gain[...]
        k[...] = bf(scaled * cosine[...] + turn(scaled) * sine[...])
        v[...] = bf(mm(xn[...], w_value[...]))
        total[...] = jnp.zeros_like(total)

    raw_pair = mm(xn[...], w_query[...])
    qp[...] = raw_pair
    visible = (seg_col[...] == seg_row[...]) & (
        lax.broadcasted_iota(jnp.int32, (tokens, tokens), 0)
        >= lax.broadcasted_iota(jnp.int32, (tokens, tokens), 1)
    )
    for i in range(prob.shape[0]):
        cols = slice(i * head, (i + 1) * head)
        raw = raw_pair[:, cols]
        scaled = raw * inverse_rms(raw) * q_gain[...]
        rows = bf(scaled * cosine[...] + turn(scaled) * sine[...])
        q[:, cols] = rows
        scores = jnp.where(visible, mm(rows, k[...], (1, 1)) * head**-0.5, far_below)
        weight = jnp.exp(scores - jnp.max(scores, -1, keepdims=True))
        low = bf(weight * (1.0 / jnp.sum(weight, -1, keepdims=True)))
        prob[i] = low
        o[:, cols] = bf(mm(low, v[...]))
    wide = 512

    @pl.loop(0, total.shape[1] // wide)
    def _(n):
        at = pl.ds(pl.multiple_of(n * wide, wide), wide)
        total[:, at] += mm(o[...], w_out[:, at])

    @pl.when(step == steps - 1)
    def _():
        split_rows(rank_ref, total, keep, give)


def attend(rank, x, gain, w_query, w_key, w_value, q_gain, k_gain, cosine, sine, segments, w_out, cut):
    tokens, width = x.shape
    head = q_gain.shape[0]
    query = w_query.shape[1]
    pair = 2
    steps = query // (pair * head)
    heads = pl.BlockSpec((tokens, pair * head), lambda j, _: (0, j))
    halves = tokens // cut // 2
    return pl.pallas_call(
        attend_kernel,
        grid_spec=pltpu.PrefetchScalarGridSpec(
            num_scalar_prefetch=1,
            grid=(steps,),
            in_specs=[
                whole((tokens, width)),
                whole((1, width)),
                pl.BlockSpec((width, pair * head), lambda j, _: (0, j)),
                whole((width, head)),
                whole((width, head)),
                whole((1, head)),
                whole((1, head)),
                whole((tokens, head)),
                whole((tokens, head)),
                whole((tokens, 1)),
                whole((1, tokens)),
                pl.BlockSpec((pair * head, width), lambda j, _: (j, 0)),
            ],
            out_specs=[
                whole((tokens, width)),
                heads,
                whole((tokens, head)),
                heads,
                whole((tokens, head)),
                whole((tokens, head)),
                pl.BlockSpec((pair, tokens, tokens), lambda j, _: (j, 0, 0)),
                heads,
                whole((halves, cut, width)),
                whole((halves, cut, width)),
            ],
            scratch_shapes=[pltpu.VMEM((tokens, width), jnp.float32)],
        ),
        out_shape=[
            jax.ShapeDtypeStruct((tokens, width), jnp.bfloat16),
            jax.ShapeDtypeStruct((tokens, query), jnp.float32),
            jax.ShapeDtypeStruct((tokens, head), jnp.float32),
            jax.ShapeDtypeStruct((tokens, query), jnp.bfloat16),
            jax.ShapeDtypeStruct((tokens, head), jnp.bfloat16),
            jax.ShapeDtypeStruct((tokens, head), jnp.bfloat16),
            jax.ShapeDtypeStruct((query // head, tokens, tokens), jnp.bfloat16),
            jax.ShapeDtypeStruct((tokens, query), jnp.bfloat16),
            jax.ShapeDtypeStruct((halves, cut, width), jnp.float32),
            jax.ShapeDtypeStruct((halves, cut, width), jnp.bfloat16),
        ],
        compiler_params=pltpu.CompilerParams(vmem_limit_bytes=vmem_bytes),
        cost_estimate=small_cost,
        name="attend",
    )(
        rank, x, gain[None], w_query, w_key, w_value, q_gain[None], k_gain[None], cosine, sine,
        segments[:, None], segments[None, :], w_out,
    )


def attend_back_kernel(
    rank_ref, x, xn, dattn, w_query, w_key, w_value, q_gain, k_gain, cosine, sine, w_out, qp, kp, q, k, v, prob,
    packed, gains, attn_gain, keep, give, total, dk, dv, low,
):
    step, steps = pl.program_id(0), pl.num_programs(0)
    tokens, head = kp.shape
    cut = keep.shape[1]
    scale = head**-0.5
    width = x.shape[1]
    wide = 512
    blocks = packed.shape[0]
    block_rows = width // blocks

    def unrotate(grad):
        return grad * cosine[...] - turn(grad) * sine[...]

    def unnorm(grad, raw, inverse, gain):
        scaled = grad * gain
        return inverse * (scaled - raw * inverse * inverse * jnp.mean(scaled * raw, -1, keepdims=True))

    def add_total(left, right, at):
        total[:, at] += mm(left, right[at, :], (1, 1))

    def put_packed(n):
        at = pl.ds(pl.multiple_of(n * wide, wide), wide)
        grad = bf(mm(xn[:, at], low[...], (0, 0)))
        many = wide // block_rows
        first = n * many
        packed[pl.ds(first, many), pl.ds(0, block_rows), :] = grad.reshape(many, block_rows, -1)

    @pl.when(step == 0)
    def _():
        total[...] = jnp.zeros_like(total)
        dk[...] = jnp.zeros_like(dk)
        dv[...] = jnp.zeros_like(dv)
        gains[...] = jnp.zeros_like(gains)

    @pl.when(step < steps - 1)
    def _():
        dout_pair = bf(mm(dattn[...], w_out[...], (1, 1)))
        for i in range(prob.shape[0]):
            cols = slice(i * head, (i + 1) * head)
            dout = dout_pair[:, cols]
            weight = prob[i]
            dp = mm(dout, v[...], (1, 1))
            wide_weight = weight.astype(jnp.float32)
            ds = bf(wide_weight * (dp - jnp.sum(wide_weight * dp, -1, keepdims=True)))
            dv[...] += mm(weight, dout, (0, 0))
            dk[...] += mm(ds, q[:, cols], (0, 0))
            dqu = unrotate(mm(ds, k[...]) * scale)
            raw = qp[:, cols]
            inverse = inverse_rms(raw)
            gains[0:1, :] += jnp.sum(dqu * raw * inverse, 0, keepdims=True)
            low[:, cols] = bf(unnorm(dqu, raw, inverse, q_gain[...]))

        @pl.loop(0, width // wide)
        def _(n):
            put_packed(n)
            add_total(low[...], w_query, pl.ds(pl.multiple_of(n * wide, wide), wide))

    @pl.when(step == steps - 1)
    def _():
        dku = unrotate(dk[...] * scale)
        raw = kp[...]
        inverse = inverse_rms(raw)
        gains[1:2, :] = jnp.sum(dku * raw * inverse, 0, keepdims=True)
        low[:, :head] = bf(unnorm(dku, raw, inverse, k_gain[...]))
        low[:, head:] = bf(dv[...])

        @pl.loop(0, width // wide)
        def _(n):
            put_packed(n)
            at = pl.ds(pl.multiple_of(n * wide, wide), wide)
            add_total(low[:, :head], w_key, at)
            add_total(low[:, head:], w_value, at)

        attn_gain[...] = jnp.zeros_like(attn_gain)

        @pl.loop(0, tokens // cut)
        def _(i):
            rows = pl.ds(pl.multiple_of(i * cut, cut), cut)
            value = x[rows, :].astype(jnp.float32)
            attn_gain[...] += jnp.sum(total[rows, :] * value * inverse_rms(value), 0, keepdims=True)

        split_rows(rank_ref, total, keep, give)


def attend_back(
    rank, x, xn, dattn, w_query, w_key, w_value, q_gain, k_gain, cosine, sine, w_out, qp, kp, q, k, v, prob,
    cut, blocks, spare,
):
    tokens, width = x.shape
    head = q_gain.shape[0]
    query = w_query.shape[1]
    pair = 2
    steps = query // (pair * head)
    last = steps - 1
    heads = pl.BlockSpec((tokens, pair * head), lambda j, _: (0, jnp.minimum(j, last)))
    halves = tokens // cut // 2
    block_rows = width // blocks + spare
    return pl.pallas_call(
        attend_back_kernel,
        grid_spec=pltpu.PrefetchScalarGridSpec(
            num_scalar_prefetch=1,
            grid=(steps + 1,),
            in_specs=[
                whole((tokens, width)),
                whole((tokens, width)),
                whole((tokens, width)),
                pl.BlockSpec((width, pair * head), lambda j, _: (0, jnp.minimum(j, last))),
                whole((width, head)),
                whole((width, head)),
                whole((1, head)),
                whole((1, head)),
                whole((tokens, head)),
                whole((tokens, head)),
                pl.BlockSpec((pair * head, width), lambda j, _: (jnp.minimum(j, last), 0)),
                heads,
                whole((tokens, head)),
                heads,
                whole((tokens, head)),
                whole((tokens, head)),
                pl.BlockSpec((pair, tokens, tokens), lambda j, _: (jnp.minimum(j, last), 0, 0)),
            ],
            out_specs=[
                pl.BlockSpec((blocks, block_rows, pair * head), lambda j, _: (0, 0, j)),
                whole((8, head)),
                whole((1, width)),
                whole((halves, cut, width)),
                whole((halves, cut, width)),
            ],
            scratch_shapes=[
                pltpu.VMEM((tokens, width), jnp.float32),
                pltpu.VMEM((tokens, head), jnp.float32),
                pltpu.VMEM((tokens, head), jnp.float32),
                pltpu.VMEM((tokens, pair * head), jnp.bfloat16),
            ],
        ),
        out_shape=[
            jax.ShapeDtypeStruct((blocks, block_rows, query + 2 * head), jnp.bfloat16),
            jax.ShapeDtypeStruct((8, head), jnp.float32),
            jax.ShapeDtypeStruct((1, width), jnp.float32),
            jax.ShapeDtypeStruct((halves, cut, width), jnp.float32),
            jax.ShapeDtypeStruct((halves, cut, width), jnp.bfloat16),
        ],
        compiler_params=pltpu.CompilerParams(vmem_limit_bytes=vmem_bytes),
        cost_estimate=pl.CostEstimate(flops=3 * 10**10, bytes_accessed=2**20, transcendentals=0),
        name="attend_back",
    )(
        rank, x, xn, dattn, w_query, w_key, w_value, q_gain[None], k_gain[None], cosine, sine, w_out,
        qp, kp, q, k, v, prob,
    )


class Loads:
    def __init__(self, sources, target, sems, shards):
        height = sources[0].shape[0]
        self.each = len(sources) // shards
        self.copies = [
            pltpu.make_async_copy(source, target.at[pl.ds(i * height, height), :], sems.at[i])
            for i, source in enumerate(sources)
        ]

    def start(self, shard):
        for copy in self.copies[shard * self.each : (shard + 1) * self.each]:
            copy.start()

    def wait(self, shard):
        for copy in self.copies[shard * self.each : (shard + 1) * self.each]:
            copy.wait()


def experts_kernel(rank_ref, hn, g, *rest, shards, before, local, hidden, top_count):
    last = before > 0
    every = before + shards
    in_count = every if last else shards
    if last:
        gates, totals_in, pre_before, gated_before = rest[:4]
        rest = rest[4:]
    else:
        sent, router = rest[:2]
        rest = rest[2:]
    in_hbm, down_hbm, rest = rest[: 2 * in_count], rest[2 * in_count : 3 * in_count], rest[3 * in_count :]
    if last:
        out, back, pre_grad, gated = rest[:4]
        rest = rest[4:]
        totals = rest[-1]
    else:
        pre_grad, gated, gates, totals = rest[:4]
        rest = rest[4:]
    in_all, down_all, gates_wide, in_sems, down_sems = rest[:5]
    chunk, shard = pl.program_id(0), pl.program_id(1)
    width = local * hidden
    rows, model = hn.shape
    first = before if last else 0
    in_loads = Loads(in_hbm, in_all, in_sems, in_count)
    down_loads = Loads(down_hbm, down_all, down_sems, in_count)
    owner = lax.broadcasted_iota(jnp.int32, (rows, width), 1) // hidden

    @pl.when((chunk == 0) & (shard == 0))
    def _():
        order = list(range(first, in_count)) + list(range(first))
        for i in order:
            in_loads.start(i)
            down_loads.start(i)

    @pl.when(shard == 0)
    def _():
        if last:
            totals[...] = totals_in[...]
        else:
            names = lax.broadcasted_iota(jnp.int32, (rows, router.shape[0]), 1).astype(jnp.float32)
            chosen = sent[...].astype(jnp.float32)
            mask = jnp.zeros(names.shape, jnp.bool_)
            for j in range(top_count):
                mask = mask | (chosen[:, j : j + 1] == names)
            logits = jnp.where(mask, mm(hn[...], router[...], (1, 1)), far_below)
            weight = jnp.exp(logits - jnp.max(logits, -1, keepdims=True))
            weight = weight * (1.0 / jnp.sum(weight, -1, keepdims=True))
            lanes = lax.broadcasted_iota(jnp.int32, gates.shape, 1)
            packed = jnp.zeros(gates.shape, jnp.float32)
            for e in range(local):
                here = names == (rank_ref[1] * local + e).astype(jnp.float32)
                value = jnp.sum(jnp.where(here, weight, 0.0), -1, keepdims=True)
                packed = packed + jnp.where(lanes == e, value, 0.0)
            gates[...] = packed
            totals[...] = jnp.zeros_like(totals)
        wide = jnp.zeros((rows, width), jnp.float32)
        for e in range(local):
            wide = jnp.where(owner == e, gates[:, e : e + 1], wide)
        gates_wide[...] = wide

    for i in range(shards):
        @pl.when((chunk == 0) & (shard == i))
        def _(i=i):
            in_loads.wait(first + i)
            down_loads.wait(first + i)

    in_at = pl.multiple_of((first + shard) * 2 * width, 2 * width)
    down_at = pl.multiple_of((first + shard) * width, width)
    pre = mm(hn[...], in_all[pl.ds(in_at, 2 * width), :], (1, 1))
    grad_middle = mm(g[...], down_all[pl.ds(down_at, width), :], (1, 1))
    gate_pre, up_pre = pre[:, :width], pre[:, width:]
    sigmoid_gate = jax.nn.sigmoid(gate_pre)
    activated = gate_pre * sigmoid_gate
    middle = activated * up_pre
    mid_at = pl.multiple_of(shard * width, width)
    gated[:, pl.ds(mid_at, width)] = bf(middle * gates_wide[...])
    product = middle * grad_middle
    lanes = lax.broadcasted_iota(jnp.int32, totals.shape, 1)
    added = totals[...]
    for e in range(local):
        value = jnp.sum(jnp.where(owner == e, product, 0.0), -1, keepdims=True)
        added = added + jnp.where(lanes == e, value, 0.0)
    totals[...] = added
    grad_middle = grad_middle * gates_wide[...]
    gate_at = pl.multiple_of(shard * 2 * width, 2 * width)
    pre_grad[:, pl.ds(gate_at, width)] = bf(
        grad_middle * up_pre * (sigmoid_gate + activated * (1.0 - sigmoid_gate))
    )
    pre_grad[:, pl.ds(pl.multiple_of(gate_at + width, width), width)] = bf(grad_middle * activated)

    if last:

        @pl.when(shard == shards - 1)
        def _():
            @pl.when(chunk == 0)
            def _():
                for i in range(before):
                    in_loads.wait(i)
                    down_loads.wait(i)

            wide = 512

            @pl.loop(0, model // wide)
            def _(n):
                cols = pl.ds(pl.multiple_of(n * wide, wide), wide)
                cut = before * width
                back[:, cols] = bf(
                    mm(pre_before[...], in_all[: 2 * cut, cols]) + mm(pre_grad[...], in_all[2 * cut :, cols])
                )
                out[:, cols] = bf(
                    mm(gated_before[...], down_all[:cut, cols]) + mm(gated[...], down_all[cut:, cols])
                )

            spare = back.shape[1] - model
            places = lax.broadcasted_iota(jnp.int32, (rows, spare), 1)
            tail = jnp.zeros((rows, spare), jnp.float32)
            for e in range(local):
                value = totals[:, e : e + 1]
                high = bf(value).astype(jnp.float32)
                here = rank_ref[1] * local + e
                tail = tail + jnp.where(places == here, high, 0.0)
                tail = tail + jnp.where(places == spare // 2 + here, value - high, 0.0)
            back[:, model:] = bf(tail)


def run_experts(ranks, hn, sent, in_mats, down_mats, local, top_count, router=None, before=None, spare=0):
    tokens, model = hn.shape
    width = down_mats[0].shape[0]
    every = len(down_mats)
    earlier = 0 if before is None else before[2].shape[1] // (2 * width)
    shards = every - earlier
    rows = tokens
    while rows > 768:
        rows //= 2

    def block(cols, step=0):
        return pl.BlockSpec((rows, cols), lambda c, s, _: (c, step), pipeline_mode=pl.Buffered(1))

    hbm = [pl.BlockSpec(memory_space=pl.ANY)] * (3 * every)
    scratch = [
        pltpu.VMEM((every * 2 * width, model), jnp.bfloat16),
        pltpu.VMEM((every * width, model), jnp.bfloat16),
        pltpu.VMEM((rows, width), jnp.float32),
        pltpu.SemaphoreType.DMA((2 * every,)),
        pltpu.SemaphoreType.DMA((every,)),
    ]
    own = [(shards * 2 * width, jnp.bfloat16), (shards * width, jnp.bfloat16)]
    if before is None:
        extra, specs = (sent, router), [block(128, model // 128), whole(router.shape)]
        outs = own + [(128, jnp.float32)] * 2
    else:
        extra = before
        specs = [block(value.shape[1]) for value in before]
        outs = [(model, jnp.bfloat16), (model + spare, jnp.bfloat16)] + own
        scratch.append(pltpu.VMEM((rows, 128), jnp.float32))
    return pl.pallas_call(
        functools.partial(
            experts_kernel, shards=shards, before=earlier, local=local, hidden=width // local, top_count=top_count
        ),
        grid_spec=pltpu.PrefetchScalarGridSpec(
            num_scalar_prefetch=1,
            grid=(tokens // rows, shards),
            in_specs=[block(model), block(model)] + specs + hbm,
            out_specs=[block(cols) for cols, _ in outs],
            scratch_shapes=scratch,
        ),
        out_shape=[jax.ShapeDtypeStruct((tokens, cols), kind) for cols, kind in outs],
        compiler_params=pltpu.CompilerParams(vmem_limit_bytes=vmem_bytes),
        cost_estimate=small_cost,
        name="experts_near" if before is None else "experts_far",
    )(ranks, hn, sent, *extra, *in_mats, *down_mats)


def out_grad_kernel(dattn, o, y, packed):
    many, height, width = y.shape
    cols = o.shape[1]
    rows = dattn.shape[1] // many
    packed[:, :rows, :] = bf(mm(dattn[...], o[...], (0, 0))).reshape(many, rows, cols)
    for i in range(width // cols):
        packed[:, rows + i * height : rows + (i + 1) * height, :] = y[:, :, i * cols : (i + 1) * cols]


def out_grad(dattn, o, y):
    tokens, width = dattn.shape
    blocks, height, _ = y.shape
    cols = o.shape[1]
    rows = width // blocks
    many = max(1, 256 // rows)
    full = rows + height * (width // cols)
    return pl.pallas_call(
        out_grad_kernel,
        grid=(blocks // many,),
        in_specs=[
            pl.BlockSpec((tokens, many * rows), lambda i: (0, i)),
            whole(o.shape),
            pl.BlockSpec((many, height, width), lambda i: (i, 0, 0)),
        ],
        out_specs=pl.BlockSpec((many, full, cols), lambda i: (i, 0, 0)),
        out_shape=jax.ShapeDtypeStruct((blocks, full, cols), jnp.bfloat16),
        compiler_params=pltpu.CompilerParams(vmem_limit_bytes=vmem_bytes),
        cost_estimate=small_cost,
        name="out_grad",
    )(dattn, o, y)


class Tokens:
    def __init__(self):
        self.size = lax.axis_size("expert")
        self.line = self.size == 8
        self.me = lax.axis_index("expert")
        self.z, self.y = self.me // 2, self.me % 2

    def across(self, value):
        return lax.ppermute(value, "expert", [(i, i ^ 1) for i in range(8)])

    def along(self, value, step):
        return lax.ppermute(value, "expert", [(i, i ^ (2 * step)) for i in range(8)])

    def place(self, step, other):
        return (self.z ^ step) * 2 + (1 - self.y if other else self.y)

    def gather(self, own, early):
        if not self.line:
            return lax.all_gather(own, "expert", axis=0, tiled=False), early
        blocks = [own] + [self.along(own, step) for step in (1, 2, 3)]
        others = [self.across(own)]
        blocks[1], early = tie(blocks[1], early)
        others += [self.across(value) for value in blocks[1:]]
        rows = jnp.zeros((self.size, *own.shape), own.dtype)
        for step in range(4):
            for value, other in ((blocks[step], False), (others[step], True)):
                rows = lax.dynamic_update_index_in_dim(rows, value, self.place(step, other), 0)
        return rows, early

    def scatter(self, parts, begun, late, last):
        if not self.line:
            total = lax.psum_scatter(parts, "expert", scatter_dimension=0, tiled=False)
            return total.astype(jnp.float32), begun, late, last

        def part(step, other):
            return lax.dynamic_index_in_dim(parts, self.place(step, other), 0, False)

        def pair_sum(step):
            return part(step, False).astype(jnp.float32) + across[step].astype(jnp.float32)

        across = {step: self.across(part(step, True)) for step in (3, 2, 1, 0)}
        across[3], begun = tie(across[3], begun)
        moved = {step: self.along(bf(pair_sum(step)), step) for step in (3, 2)}
        across[1], moved[3] = tie(across[1], moved[3])
        moved[1] = self.along(bf(pair_sum(1)), 1)
        across[0], moved[2], late = tie(across[0], moved[2], late)
        moved[1], last = tie(moved[1], last)
        return pair_sum(0) + sum(value.astype(jnp.float32) for value in moved.values()), begun, late, last


def body(
    hidden_in,
    cotangent,
    segments,
    positions,
    routes,
    attn_gain,
    w_query,
    w_key,
    value_weight,
    q_gain,
    k_gain,
    w_out,
    ffn_gain,
    router,
    w_gate,
    w_up,
    w_down,
):
    tok_count, model_width = hidden_in.shape
    head_size = q_gain.shape[0]
    experts = router.shape[1]
    local_experts, _, hidden = w_gate.shape
    tensor_size = lax.axis_size("tensor")
    tensor_rank = lax.axis_index("tensor")
    expert_rank = lax.axis_index("expert")
    shard_rows = tok_count // tensor_size
    order = Tokens()
    group = order.size

    def own_rows(value):
        return lax.dynamic_slice_in_dim(value, tensor_rank * shard_rows, shard_rows)

    cot_own = own_rows(cotangent)
    routes_own = own_rows(routes)
    spare_cols = 128
    routes_wide = jnp.pad(bf(routes_own), ((0, 0), (0, spare_cols - routes.shape[1])))
    sent_own = jnp.concatenate([cot_own, routes_wide], 1)
    hidden_in, sent_own = tie(hidden_in, sent_own)
    sent = lax.all_gather(sent_own, "expert", axis=0, tiled=True)
    expert_ids = jnp.arange(experts, dtype=jnp.int32)

    def mask_of(route_rows):
        return jnp.any(route_rows[:, :, None] == expert_ids[None, None, :], 1)

    mask_own = mask_of(routes_own)
    own_mats = [value.reshape(local_experts * hidden, model_width) for value in (w_gate.transpose(0, 2, 1), w_up.transpose(0, 2, 1), w_down)]

    cosine, sine_table = rope_tables(positions, head_size)
    half = jnp.arange(head_size, dtype=jnp.int32) < head_size // 2
    sine_table = jnp.where(half, -sine_table, sine_table)
    ranks = jnp.stack([tensor_rank, expert_rank]).astype(jnp.int32)
    normalized_input, qp, kp, q, k, v, prob, attended_rows, keep, give_part = attend(
        ranks, hidden_in, attn_gain, w_query, w_key, value_weight, q_gain, k_gain, cosine, sine_table,
        segments, w_out, shard_rows,
    )

    def reduce_rows(keep, give, first=()):
        half = keep + swap(give, 1).astype(jnp.float32)
        high = tensor_rank // 2
        keep = lax.dynamic_index_in_dim(half, high, 0, False)
        give, first = tie(bf(lax.dynamic_index_in_dim(half, 1 - high, 0, False)), first)
        return keep + swap(give, 2).astype(jnp.float32), first

    def gather_rows(own):
        far = swap(own, 2)
        both = jnp.stack([own, far])
        near = swap(both, 1)
        rows = jnp.zeros((tensor_size, shard_rows, model_width), own.dtype)
        for value, step in ((own, 0), (far, 2), (near[0], 1), (near[1], 3)):
            rows = lax.dynamic_update_index_in_dim(rows, value, tensor_rank ^ step, 0)
        return rows.reshape(tok_count, model_width)

    far_gate = swap(own_mats[0], 2)
    attn_sum, far_gate = reduce_rows(keep, give_part, far_gate)
    residual = own_rows(hidden_in).astype(jnp.float32) + attn_sum
    inv_second = lax.rsqrt(jnp.mean(residual * residual, -1, keepdims=True) + epsilon)
    normed_ffn = (residual * inv_second * ffn_gain).astype(jnp.bfloat16)

    def gates_of(rows, mask):
        logits = jnp.where(mask, mm(rows, router), far_below)
        return jax.nn.softmax(logits, -1)

    gates_own = gates_of(normed_ffn, mask_own)
    far_up = swap(own_mats[1], 2)
    far_mats = [far_gate, far_up, swap(own_mats[2], 2)]
    normed_all, sent = order.gather(normed_ffn, sent)
    normed_all = normed_all.reshape(group * shard_rows, model_width)
    grad_all = sent[:, :model_width]
    near_mats = [swap(value, 1) for value in own_mats]
    last_mats = [swap(value, 1) for value in far_mats]
    shards = (own_mats, near_mats, far_mats, last_mats)
    in_mats = [value for shard in shards for value in shard[:2]]
    down_mats = [shard[2] for shard in shards]
    width = local_experts * hidden
    given = (ranks, normed_all, sent)
    near_count = len(shards) // 2
    pre_near, gated_near, gates_packed, marks = run_experts(
        *given, in_mats[: 2 * near_count], down_mats[:near_count], local_experts, routes.shape[1], router.T
    )
    spare_cols = 128 * (-(-2 * experts // 128))
    out_part, back_part, pre_last, gated_last = run_experts(
        *given, in_mats, down_mats, local_experts, routes.shape[1],
        before=(gates_packed, marks, pre_near, gated_near), spare=spare_cols,
    )
    def weight_grads(step):
        pre, gated = ((pre_near, gated_near), (pre_last, gated_last))[step // near_count]
        at = step % near_count
        pre, gated = pre[:, at * 2 * width : (at + 1) * 2 * width], gated[:, at * width : (at + 1) * width]
        return mm(pre, normed_all, (0, 0)), mm(gated, grad_all, (0, 0))

    def give(parts, step):
        return [swap(bf(part), step).astype(jnp.float32) for part in parts]

    far = give(weight_grads(3), 1)
    near = give(weight_grads(1), 1)
    far_part = [bf(a + b) for a, b in zip(weight_grads(2), far)]
    near_part = [a + b for a, b in zip(weight_grads(0), near)]
    far_part = [far_part[0][:width], far_part[0][width:], far_part[1]]

    far_part = tuple(far_part)
    arrived = [swap(far_part[0], 2)]
    back_sum, far_part, _, arrived[0] = order.scatter(
        back_part.reshape(group, shard_rows, -1), far_part, (), arrived[0]
    )
    gate_grad_own = (
        back_sum[:, model_width : model_width + experts]
        + back_sum[:, model_width + spare_cols // 2 :][:, :experts]
    )
    back_sum = back_sum[:, :model_width]
    grad_out = cot_own.astype(jnp.float32)
    grad_chosen = gates_own * (
        gate_grad_own - jnp.sum(gates_own * gate_grad_own, -1, keepdims=True)
    )
    grad_logits = bf(jnp.where(mask_own, grad_chosen, 0.0))
    router_part = mm(normed_ffn, grad_logits, (0, 0))
    grad_normed_ffn = back_sum + mm(grad_logits, router, (1, 1))
    ffn_gain_part = jnp.sum(grad_normed_ffn * residual * inv_second, 0)
    grad_residual = grad_out + norm_back(grad_normed_ffn * ffn_gain, residual, inv_second)
    grad_attn = gather_rows(bf(grad_residual))
    grad_attn, *left = tie(grad_attn, *far_part[1:])
    arrived += [swap(piece, 2) for piece in left]
    out_blocks = out_grad(grad_attn, attended_rows, out_part.reshape(group, shard_rows, model_width))
    grad_attn, out_blocks = tie(grad_attn, out_blocks)
    out_blocks = lax.psum_scatter(out_blocks, "expert", scatter_dimension=0, tiled=False)
    slice_rows = model_width // group
    spare = 16
    packed, gain_parts, attn_gain_part, keep, give_part = attend_back(
        ranks, hidden_in, normalized_input, grad_attn, w_query, w_key, value_weight, q_gain, k_gain, cosine,
        sine_table, w_out, qp, kp, q, k, v, prob, shard_rows, group, spare,
    )
    grad_normed, _ = reduce_rows(keep, give_part)
    inputs_own = own_rows(hidden_in).astype(jnp.float32)
    inv_own = lax.rsqrt(jnp.mean(inputs_own * inputs_own, -1, keepdims=True) + epsilon)
    input_grad = gather_rows(
        bf(grad_residual + norm_back(grad_normed * attn_gain, inputs_own, inv_own))
    ).astype(jnp.float32)

    small = jnp.concatenate(
        [
            router_part.reshape(group, -1),
            attn_gain_part.reshape(group, -1),
            ffn_gain_part.reshape(group, -1),
            jnp.broadcast_to(gain_parts[:2].reshape(1, -1), (group, 2 * head_size)),
        ],
        1,
    )
    small = jnp.pad(small, ((0, 0), (0, spare * packed.shape[2] - small.shape[1])))
    packed = lax.dynamic_update_slice(
        packed, bf(small).reshape(group, spare, packed.shape[2]), (0, slice_rows, 0)
    )
    packed, _, out_blocks, _ = order.scatter(packed, (), out_blocks, ())
    out_blocks = out_blocks.astype(jnp.float32)
    w_out_grad = out_blocks[:slice_rows].T
    out_sum = out_blocks[slice_rows:].reshape(-1, shard_rows, out_blocks.shape[1]).transpose(1, 0, 2)
    layer_out = gather_rows(bf(residual + out_sum.reshape(shard_rows, model_width)))
    query_width, key_width = w_query.shape[1], w_key.shape[1]
    w_query_grad = packed[:slice_rows, :query_width]
    w_key_grad = packed[:slice_rows, query_width : query_width + key_width]
    w_value_grad = packed[:slice_rows, query_width + key_width :]
    small = packed[slice_rows:]
    small = small + swap(bf(small), 1).astype(jnp.float32)
    small = (small + swap(bf(small), 2).astype(jnp.float32)).reshape(-1)
    cuts = [slice_rows * experts, slice_rows, slice_rows, head_size, head_size]
    router_grad, attn_gain_grad, ffn_gain_grad, q_gain_all, k_gain_all = [
        small[sum(cuts[:i]) : sum(cuts[: i + 1])] for i in range(len(cuts))
    ]
    parts = [near_part[0][:width], near_part[0][width:], near_part[1]]
    gate_t, up_t, w_down_grad = [
        (a + b.astype(jnp.float32)).reshape(local_experts, hidden, model_width)
        for a, b in zip(parts, arrived)
    ]
    w_gate_grad, w_up_grad = gate_t.transpose(0, 2, 1), up_t.transpose(0, 2, 1)
    gain_count = head_size // group
    gain_at = expert_rank * gain_count
    return (
        layer_out,
        input_grad,
        attn_gain_grad,
        w_query_grad,
        w_key_grad,
        w_value_grad,
        lax.dynamic_slice_in_dim(q_gain_all, gain_at, gain_count),
        lax.dynamic_slice_in_dim(k_gain_all, gain_at, gain_count),
        w_out_grad,
        ffn_gain_grad,
        router_grad.reshape(slice_rows, experts),
        w_gate_grad,
        w_up_grad,
        w_down_grad,
    )


def solution(mesh):
    placed = (
        P("expert", None),
        P("expert", None),
        P("expert"),
        P("expert"),
        P("expert", None),
        P(),
        P(None, "tensor"),
        P(None, "tensor"),
        P(None, "tensor"),
        P(),
        P(),
        P("tensor", None),
        P(),
        P(),
        P("expert", None, "tensor"),
        P("expert", None, "tensor"),
        P("expert", "tensor", None),
    )
    return jax.shard_map(
        body,
        mesh=mesh,
        in_specs=placed,
        out_specs=(
            P("expert", None),
            P("expert", None),
            P("expert"),
            P("expert", "tensor"),
            P("expert", "tensor"),
            P("expert", "tensor"),
            P("expert"),
            P("expert"),
            P("tensor", "expert"),
            P("expert"),
            P("expert", None),
            P("expert", None, "tensor"),
            P("expert", None, "tensor"),
            P("expert", "tensor", None),
        ),
        check_vma=False,
    )
```

```python
import functools

import jax
import jax.numpy as jnp
from jax import lax
from jax.experimental import pallas as pl
from jax.experimental.pallas import tpu as pltpu
from jax.sharding import PartitionSpec as P

epsilon = 1e-06
rope_base = 1000000.0
far_below = -1e30


def rope_tables(positions, head_size):
    half_size = head_size // 2
    frequency = rope_base ** (-(jnp.arange(half_size, dtype=jnp.float32) * 2.0) / head_size)
    angles = positions.astype(jnp.float32)[:, None] * frequency[None, :]
    cosine = jnp.cos(angles)
    sine_table = jnp.sin(angles)
    return (jnp.concatenate([cosine, cosine], -1), jnp.concatenate([sine_table, sine_table], -1))


def norm_back(grad_scaled, value_rows, scales):
    return scales * (
        grad_scaled
        - value_rows * scales * scales * jnp.mean(grad_scaled * value_rows, -1, keepdims=True)
    )


def bf(value):
    return value.astype(jnp.bfloat16)


def mm(left, right, contract=(1, 0)):
    return lax.dot_general(
        left, right, (((contract[0],), (contract[1],)), ((), ())), preferred_element_type=jnp.float32
    )


def tie(*values):
    return lax.optimization_barrier(values)


def swap(value, step):
    size = lax.axis_size("tensor")
    return lax.ppermute(value, "tensor", [(i, i ^ step) for i in range(size)])


vmem_bytes = 58 * 2**20
small_cost = pl.CostEstimate(flops=2**20, bytes_accessed=2**16, transcendentals=0)


def whole(shape):
    return pl.BlockSpec(shape, lambda *_: (0,) * len(shape))


def turn(rows):
    return pltpu.roll(rows, rows.shape[-1] // 2, 1)


def inverse_rms(rows):
    return lax.rsqrt(jnp.mean(rows * rows, -1, keepdims=True) + epsilon)


def split_rows(rank_ref, total, keep, give):
    rows = keep.shape[1]
    low = rank_ref[0] % 2
    for high in range(keep.shape[0]):
        start = pl.multiple_of((2 * high + low) * rows, rows)
        keep[high] = total[pl.ds(start, rows), :]
        start = pl.multiple_of((2 * high + 1 - low) * rows, rows)
        give[high] = bf(total[pl.ds(start, rows), :])


def attend_kernel(
    rank_ref, x, gain, w_query, w_key, w_value, q_gain, k_gain, cosine, sine, seg_col, seg_row, w_out,
    xn, qp, kp, q, k, v, prob, o, keep, give, total,
):
    step, steps = pl.program_id(0), pl.num_programs(0)
    tokens, head = kp.shape
    cut = keep.shape[1]

    @pl.when(step == 0)
    def _():
        @pl.loop(0, tokens // cut)
        def _(i):
            rows = pl.ds(pl.multiple_of(i * cut, cut), cut)
            value = x[rows, :].astype(jnp.float32)
            xn[rows, :] = bf(value * inverse_rms(value) * gain[...])

        raw = mm(xn[...], w_key[...])
        kp[...] = raw
        scaled = raw * inverse_rms(raw) * k_gain[...]
        k[...] = bf(scaled * cosine[...] + turn(scaled) * sine[...])
        v[...] = bf(mm(xn[...], w_value[...]))
        total[...] = jnp.zeros_like(total)

    raw_pair = mm(xn[...], w_query[...])
    qp[...] = raw_pair
    visible = (seg_col[...] == seg_row[...]) & (
        lax.broadcasted_iota(jnp.int32, (tokens, tokens), 0)
        >= lax.broadcasted_iota(jnp.int32, (tokens, tokens), 1)
    )
    for i in range(prob.shape[0]):
        cols = slice(i * head, (i + 1) * head)
        raw = raw_pair[:, cols]
        scaled = raw * inverse_rms(raw) * q_gain[...]
        rows = bf(scaled * cosine[...] + turn(scaled) * sine[...])
        q[:, cols] = rows
        scores = jnp.where(visible, mm(rows, k[...], (1, 1)) * head**-0.5, far_below)
        weight = jnp.exp(scores - jnp.max(scores, -1, keepdims=True))
        low = bf(weight * (1.0 / jnp.sum(weight, -1, keepdims=True)))
        prob[i] = low
        o[:, cols] = bf(mm(low, v[...]))
    wide = 512

    @pl.loop(0, total.shape[1] // wide)
    def _(n):
        at = pl.ds(pl.multiple_of(n * wide, wide), wide)
        total[:, at] += mm(o[...], w_out[:, at])

    @pl.when(step == steps - 1)
    def _():
        split_rows(rank_ref, total, keep, give)


def attend(rank, x, gain, w_query, w_key, w_value, q_gain, k_gain, cosine, sine, segments, w_out, cut):
    tokens, width = x.shape
    head = q_gain.shape[0]
    query = w_query.shape[1]
    pair = 2
    steps = query // (pair * head)
    heads = pl.BlockSpec((tokens, pair * head), lambda j, _: (0, j))
    halves = tokens // cut // 2
    return pl.pallas_call(
        attend_kernel,
        grid_spec=pltpu.PrefetchScalarGridSpec(
            num_scalar_prefetch=1,
            grid=(steps,),
            in_specs=[
                whole((tokens, width)),
                whole((1, width)),
                pl.BlockSpec((width, pair * head), lambda j, _: (0, j)),
                whole((width, head)),
                whole((width, head)),
                whole((1, head)),
                whole((1, head)),
                whole((tokens, head)),
                whole((tokens, head)),
                whole((tokens, 1)),
                whole((1, tokens)),
                pl.BlockSpec((pair * head, width), lambda j, _: (j, 0)),
            ],
            out_specs=[
                whole((tokens, width)),
                heads,
                whole((tokens, head)),
                heads,
                whole((tokens, head)),
                whole((tokens, head)),
                pl.BlockSpec((pair, tokens, tokens), lambda j, _: (j, 0, 0)),
                heads,
                whole((halves, cut, width)),
                whole((halves, cut, width)),
            ],
            scratch_shapes=[pltpu.VMEM((tokens, width), jnp.float32)],
        ),
        out_shape=[
            jax.ShapeDtypeStruct((tokens, width), jnp.bfloat16),
            jax.ShapeDtypeStruct((tokens, query), jnp.float32),
            jax.ShapeDtypeStruct((tokens, head), jnp.float32),
            jax.ShapeDtypeStruct((tokens, query), jnp.bfloat16),
            jax.ShapeDtypeStruct((tokens, head), jnp.bfloat16),
            jax.ShapeDtypeStruct((tokens, head), jnp.bfloat16),
            jax.ShapeDtypeStruct((query // head, tokens, tokens), jnp.bfloat16),
            jax.ShapeDtypeStruct((tokens, query), jnp.bfloat16),
            jax.ShapeDtypeStruct((halves, cut, width), jnp.float32),
            jax.ShapeDtypeStruct((halves, cut, width), jnp.bfloat16),
        ],
        compiler_params=pltpu.CompilerParams(vmem_limit_bytes=vmem_bytes),
        cost_estimate=small_cost,
        name="attend",
    )(
        rank, x, gain[None], w_query, w_key, w_value, q_gain[None], k_gain[None], cosine, sine,
        segments[:, None], segments[None, :], w_out,
    )


def attend_back_kernel(
    rank_ref, x, xn, dattn, w_query, w_key, w_value, q_gain, k_gain, cosine, sine, w_out, qp, kp, q, k, v, prob,
    packed, gains, attn_gain, keep, give, total, dk, dv, low,
):
    step, steps = pl.program_id(0), pl.num_programs(0)
    tokens, head = kp.shape
    cut = keep.shape[1]
    scale = head**-0.5
    width = x.shape[1]
    wide = 512
    blocks = packed.shape[0]
    block_rows = width // blocks

    def unrotate(grad):
        return grad * cosine[...] - turn(grad) * sine[...]

    def unnorm(grad, raw, inverse, gain):
        scaled = grad * gain
        return inverse * (scaled - raw * inverse * inverse * jnp.mean(scaled * raw, -1, keepdims=True))

    def add_total(left, right, at):
        total[:, at] += mm(left, right[at, :], (1, 1))

    def put_packed(n):
        at = pl.ds(pl.multiple_of(n * wide, wide), wide)
        grad = bf(mm(xn[:, at], low[...], (0, 0)))
        many = wide // block_rows
        first = n * many
        packed[pl.ds(first, many), pl.ds(0, block_rows), :] = grad.reshape(many, block_rows, -1)

    @pl.when(step == 0)
    def _():
        total[...] = jnp.zeros_like(total)
        dk[...] = jnp.zeros_like(dk)
        dv[...] = jnp.zeros_like(dv)
        gains[...] = jnp.zeros_like(gains)

    @pl.when(step < steps - 1)
    def _():
        dout_pair = bf(mm(dattn[...], w_out[...], (1, 1)))
        for i in range(prob.shape[0]):
            cols = slice(i * head, (i + 1) * head)
            dout = dout_pair[:, cols]
            weight = prob[i]
            dp = mm(dout, v[...], (1, 1))
            wide_weight = weight.astype(jnp.float32)
            ds = bf(wide_weight * (dp - jnp.sum(wide_weight * dp, -1, keepdims=True)))
            dv[...] += mm(weight, dout, (0, 0))
            dk[...] += mm(ds, q[:, cols], (0, 0))
            dqu = unrotate(mm(ds, k[...]) * scale)
            raw = qp[:, cols]
            inverse = inverse_rms(raw)
            gains[0:1, :] += jnp.sum(dqu * raw * inverse, 0, keepdims=True)
            low[:, cols] = bf(unnorm(dqu, raw, inverse, q_gain[...]))

        @pl.loop(0, width // wide)
        def _(n):
            put_packed(n)
            add_total(low[...], w_query, pl.ds(pl.multiple_of(n * wide, wide), wide))

    @pl.when(step == steps - 1)
    def _():
        dku = unrotate(dk[...] * scale)
        raw = kp[...]
        inverse = inverse_rms(raw)
        gains[1:2, :] = jnp.sum(dku * raw * inverse, 0, keepdims=True)
        low[:, :head] = bf(unnorm(dku, raw, inverse, k_gain[...]))
        low[:, head:] = bf(dv[...])

        @pl.loop(0, width // wide)
        def _(n):
            put_packed(n)
            at = pl.ds(pl.multiple_of(n * wide, wide), wide)
            add_total(low[:, :head], w_key, at)
            add_total(low[:, head:], w_value, at)

        attn_gain[...] = jnp.zeros_like(attn_gain)

        @pl.loop(0, tokens // cut)
        def _(i):
            rows = pl.ds(pl.multiple_of(i * cut, cut), cut)
            value = x[rows, :].astype(jnp.float32)
            attn_gain[...] += jnp.sum(total[rows, :] * value * inverse_rms(value), 0, keepdims=True)

        split_rows(rank_ref, total, keep, give)


def attend_back(
    rank, x, xn, dattn, w_query, w_key, w_value, q_gain, k_gain, cosine, sine, w_out, qp, kp, q, k, v, prob,
    cut, blocks, spare,
):
    tokens, width = x.shape
    head = q_gain.shape[0]
    query = w_query.shape[1]
    pair = 2
    steps = query // (pair * head)
    last = steps - 1
    heads = pl.BlockSpec((tokens, pair * head), lambda j, _: (0, jnp.minimum(j, last)))
    halves = tokens // cut // 2
    block_rows = width // blocks + spare
    return pl.pallas_call(
        attend_back_kernel,
        grid_spec=pltpu.PrefetchScalarGridSpec(
            num_scalar_prefetch=1,
            grid=(steps + 1,),
            in_specs=[
                whole((tokens, width)),
                whole((tokens, width)),
                whole((tokens, width)),
                pl.BlockSpec((width, pair * head), lambda j, _: (0, jnp.minimum(j, last))),
                whole((width, head)),
                whole((width, head)),
                whole((1, head)),
                whole((1, head)),
                whole((tokens, head)),
                whole((tokens, head)),
                pl.BlockSpec((pair * head, width), lambda j, _: (jnp.minimum(j, last), 0)),
                heads,
                whole((tokens, head)),
                heads,
                whole((tokens, head)),
                whole((tokens, head)),
                pl.BlockSpec((pair, tokens, tokens), lambda j, _: (jnp.minimum(j, last), 0, 0)),
            ],
            out_specs=[
                pl.BlockSpec((blocks, block_rows, pair * head), lambda j, _: (0, 0, j)),
                whole((8, head)),
                whole((1, width)),
                whole((halves, cut, width)),
                whole((halves, cut, width)),
            ],
            scratch_shapes=[
                pltpu.VMEM((tokens, width), jnp.float32),
                pltpu.VMEM((tokens, head), jnp.float32),
                pltpu.VMEM((tokens, head), jnp.float32),
                pltpu.VMEM((tokens, pair * head), jnp.bfloat16),
            ],
        ),
        out_shape=[
            jax.ShapeDtypeStruct((blocks, block_rows, query + 2 * head), jnp.bfloat16),
            jax.ShapeDtypeStruct((8, head), jnp.float32),
            jax.ShapeDtypeStruct((1, width), jnp.float32),
            jax.ShapeDtypeStruct((halves, cut, width), jnp.float32),
            jax.ShapeDtypeStruct((halves, cut, width), jnp.bfloat16),
        ],
        compiler_params=pltpu.CompilerParams(vmem_limit_bytes=vmem_bytes),
        cost_estimate=pl.CostEstimate(flops=3 * 10**10, bytes_accessed=2**20, transcendentals=0),
        name="attend_back",
    )(
        rank, x, xn, dattn, w_query, w_key, w_value, q_gain[None], k_gain[None], cosine, sine, w_out,
        qp, kp, q, k, v, prob,
    )


class Loads:
    def __init__(self, sources, target, sems, shards):
        height = sources[0].shape[0]
        self.each = len(sources) // shards
        self.copies = [
            pltpu.make_async_copy(source, target.at[pl.ds(i * height, height), :], sems.at[i])
            for i, source in enumerate(sources)
        ]

    def start(self, shard):
        for copy in self.copies[shard * self.each : (shard + 1) * self.each]:
            copy.start()

    def wait(self, shard):
        for copy in self.copies[shard * self.each : (shard + 1) * self.each]:
            copy.wait()


def experts_kernel(rank_ref, hn, g, *rest, shards, before, local, hidden, top_count):
    last = before > 0
    every = before + shards
    in_count = every if last else shards
    if last:
        gates, totals_in, pre_before, gated_before = rest[:4]
        rest = rest[4:]
    else:
        sent, router = rest[:2]
        rest = rest[2:]
    in_hbm, down_hbm, rest = rest[: 2 * in_count], rest[2 * in_count : 3 * in_count], rest[3 * in_count :]
    if last:
        out, back, pre_grad, gated = rest[:4]
        rest = rest[4:]
        totals = rest[-1]
    else:
        pre_grad, gated, gates, totals = rest[:4]
        rest = rest[4:]
    in_all, down_all, gates_wide, in_sems, down_sems = rest[:5]
    chunk, shard = pl.program_id(0), pl.program_id(1)
    width = local * hidden
    rows, model = hn.shape
    first = before if last else 0
    in_loads = Loads(in_hbm, in_all, in_sems, in_count)
    down_loads = Loads(down_hbm, down_all, down_sems, in_count)
    owner = lax.broadcasted_iota(jnp.int32, (rows, width), 1) // hidden

    @pl.when((chunk == 0) & (shard == 0))
    def _():
        order = list(range(first, in_count)) + list(range(first))
        for i in order:
            in_loads.start(i)
            down_loads.start(i)

    @pl.when(shard == 0)
    def _():
        if last:
            totals[...] = totals_in[...]
        else:
            names = lax.broadcasted_iota(jnp.int32, (rows, router.shape[0]), 1).astype(jnp.float32)
            chosen = sent[...].astype(jnp.float32)
            mask = jnp.zeros(names.shape, jnp.bool_)
            for j in range(top_count):
                mask = mask | (chosen[:, j : j + 1] == names)
            logits = jnp.where(mask, mm(hn[...], router[...], (1, 1)), far_below)
            weight = jnp.exp(logits - jnp.max(logits, -1, keepdims=True))
            weight = weight * (1.0 / jnp.sum(weight, -1, keepdims=True))
            lanes = lax.broadcasted_iota(jnp.int32, gates.shape, 1)
            packed = jnp.zeros(gates.shape, jnp.float32)
            for e in range(local):
                here = names == (rank_ref[1] * local + e).astype(jnp.float32)
                value = jnp.sum(jnp.where(here, weight, 0.0), -1, keepdims=True)
                packed = packed + jnp.where(lanes == e, value, 0.0)
            gates[...] = packed
            totals[...] = jnp.zeros_like(totals)
        wide = jnp.zeros((rows, width), jnp.float32)
        for e in range(local):
            wide = jnp.where(owner == e, gates[:, e : e + 1], wide)
        gates_wide[...] = wide

    for i in range(shards):
        @pl.when((chunk == 0) & (shard == i))
        def _(i=i):
            in_loads.wait(first + i)
            down_loads.wait(first + i)

    in_at = pl.multiple_of((first + shard) * 2 * width, 2 * width)
    down_at = pl.multiple_of((first + shard) * width, width)
    pre = mm(hn[...], in_all[pl.ds(in_at, 2 * width), :], (1, 1))
    grad_middle = mm(g[...], down_all[pl.ds(down_at, width), :], (1, 1))
    gate_pre, up_pre = pre[:, :width], pre[:, width:]
    sigmoid_gate = jax.nn.sigmoid(gate_pre)
    activated = gate_pre * sigmoid_gate
    middle = activated * up_pre
    mid_at = pl.multiple_of(shard * width, width)
    gated[:, pl.ds(mid_at, width)] = bf(middle * gates_wide[...])
    product = middle * grad_middle
    lanes = lax.broadcasted_iota(jnp.int32, totals.shape, 1)
    added = totals[...]
    for e in range(local):
        value = jnp.sum(jnp.where(owner == e, product, 0.0), -1, keepdims=True)
        added = added + jnp.where(lanes == e, value, 0.0)
    totals[...] = added
    grad_middle = grad_middle * gates_wide[...]
    gate_at = pl.multiple_of(shard * 2 * width, 2 * width)
    pre_grad[:, pl.ds(gate_at, width)] = bf(
        grad_middle * up_pre * (sigmoid_gate + activated * (1.0 - sigmoid_gate))
    )
    pre_grad[:, pl.ds(pl.multiple_of(gate_at + width, width), width)] = bf(grad_middle * activated)

    if last:

        @pl.when(shard == shards - 1)
        def _():
            @pl.when(chunk == 0)
            def _():
                for i in range(before):
                    in_loads.wait(i)
                    down_loads.wait(i)

            wide = 512

            @pl.loop(0, model // wide)
            def _(n):
                cols = pl.ds(pl.multiple_of(n * wide, wide), wide)
                cut = before * width
                back[:, cols] = bf(
                    mm(pre_before[...], in_all[: 2 * cut, cols]) + mm(pre_grad[...], in_all[2 * cut :, cols])
                )
                out[:, cols] = bf(
                    mm(gated_before[...], down_all[:cut, cols]) + mm(gated[...], down_all[cut:, cols])
                )

            spare = back.shape[1] - model
            places = lax.broadcasted_iota(jnp.int32, (rows, spare), 1)
            tail = jnp.zeros((rows, spare), jnp.float32)
            for e in range(local):
                value = totals[:, e : e + 1]
                high = bf(value).astype(jnp.float32)
                here = rank_ref[1] * local + e
                tail = tail + jnp.where(places == here, high, 0.0)
                tail = tail + jnp.where(places == spare // 2 + here, value - high, 0.0)
            back[:, model:] = bf(tail)


def run_experts(ranks, hn, sent, in_mats, down_mats, local, top_count, router=None, before=None, spare=0):
    tokens, model = hn.shape
    width = down_mats[0].shape[0]
    every = len(down_mats)
    earlier = 0 if before is None else before[2].shape[1] // (2 * width)
    shards = every - earlier
    rows = tokens
    while rows > 768:
        rows //= 2

    def block(cols, step=0):
        return pl.BlockSpec((rows, cols), lambda c, s, _: (c, step), pipeline_mode=pl.Buffered(1))

    hbm = [pl.BlockSpec(memory_space=pl.ANY)] * (3 * every)
    scratch = [
        pltpu.VMEM((every * 2 * width, model), jnp.bfloat16),
        pltpu.VMEM((every * width, model), jnp.bfloat16),
        pltpu.VMEM((rows, width), jnp.float32),
        pltpu.SemaphoreType.DMA((2 * every,)),
        pltpu.SemaphoreType.DMA((every,)),
    ]
    own = [(shards * 2 * width, jnp.bfloat16), (shards * width, jnp.bfloat16)]
    if before is None:
        extra, specs = (sent, router), [block(128, model // 128), whole(router.shape)]
        outs = own + [(128, jnp.float32)] * 2
    else:
        extra = before
        specs = [block(value.shape[1]) for value in before]
        outs = [(model, jnp.bfloat16), (model + spare, jnp.bfloat16)] + own
        scratch.append(pltpu.VMEM((rows, 128), jnp.float32))
    return pl.pallas_call(
        functools.partial(
            experts_kernel, shards=shards, before=earlier, local=local, hidden=width // local, top_count=top_count
        ),
        grid_spec=pltpu.PrefetchScalarGridSpec(
            num_scalar_prefetch=1,
            grid=(tokens // rows, shards),
            in_specs=[block(model), block(model)] + specs + hbm,
            out_specs=[block(cols) for cols, _ in outs],
            scratch_shapes=scratch,
        ),
        out_shape=[jax.ShapeDtypeStruct((tokens, cols), kind) for cols, kind in outs],
        compiler_params=pltpu.CompilerParams(vmem_limit_bytes=vmem_bytes),
        cost_estimate=small_cost,
        name="experts_near" if before is None else "experts_far",
    )(ranks, hn, sent, *extra, *in_mats, *down_mats)


class Tokens:
    def __init__(self):
        self.size = lax.axis_size("expert")
        self.line = self.size == 8
        self.me = lax.axis_index("expert")
        self.z, self.y = self.me // 2, self.me % 2

    def across(self, value):
        return lax.ppermute(value, "expert", [(i, i ^ 1) for i in range(8)])

    def along(self, value, step):
        return lax.ppermute(value, "expert", [(i, i ^ (2 * step)) for i in range(8)])

    def place(self, step, other):
        return (self.z ^ step) * 2 + (1 - self.y if other else self.y)

    def gather(self, own, early):
        if not self.line:
            return lax.all_gather(own, "expert", axis=0, tiled=False), early
        blocks = [own] + [self.along(own, step) for step in (1, 2, 3)]
        others = [self.across(own)]
        blocks[1], early = tie(blocks[1], early)
        others += [self.across(value) for value in blocks[1:]]
        rows = jnp.zeros((self.size, *own.shape), own.dtype)
        for step in range(4):
            for value, other in ((blocks[step], False), (others[step], True)):
                rows = lax.dynamic_update_index_in_dim(rows, value, self.place(step, other), 0)
        return rows, early

    def scatter(self, parts, begun, late, last, middle=()):
        if not self.line:
            total = lax.psum_scatter(parts, "expert", scatter_dimension=0, tiled=False)
            return total.astype(jnp.float32), begun, late, last, middle

        def part(step, other):
            return lax.dynamic_index_in_dim(parts, self.place(step, other), 0, False)

        def pair_sum(step):
            return part(step, False).astype(jnp.float32) + across[step].astype(jnp.float32)

        across = {step: self.across(part(step, True)) for step in (3, 2, 1, 0)}
        across[3], begun = tie(across[3], begun)
        moved = {step: self.along(bf(pair_sum(step)), step) for step in (3, 2)}
        across[1], moved[3], middle = tie(across[1], moved[3], middle)
        moved[1] = self.along(bf(pair_sum(1)), 1)
        across[0], moved[2], late = tie(across[0], moved[2], late)
        moved[1], last = tie(moved[1], last)
        total = pair_sum(0) + sum(value.astype(jnp.float32) for value in moved.values())
        return total, begun, late, last, middle


def body(
    hidden_in,
    cotangent,
    segments,
    positions,
    routes,
    attn_gain,
    w_query,
    w_key,
    value_weight,
    q_gain,
    k_gain,
    w_out,
    ffn_gain,
    router,
    w_gate,
    w_up,
    w_down,
):
    tok_count, model_width = hidden_in.shape
    head_size = q_gain.shape[0]
    experts = router.shape[1]
    local_experts, _, hidden = w_gate.shape
    tensor_size = lax.axis_size("tensor")
    tensor_rank = lax.axis_index("tensor")
    expert_rank = lax.axis_index("expert")
    shard_rows = tok_count // tensor_size
    order = Tokens()
    group = order.size

    def own_rows(value):
        return lax.dynamic_slice_in_dim(value, tensor_rank * shard_rows, shard_rows)

    cot_own = own_rows(cotangent)
    routes_own = own_rows(routes)
    spare_cols = 128
    routes_wide = jnp.pad(bf(routes_own), ((0, 0), (0, spare_cols - routes.shape[1])))
    sent_own = jnp.concatenate([cot_own, routes_wide], 1)
    hidden_in, sent_own = tie(hidden_in, sent_own)
    sent = lax.all_gather(sent_own, "expert", axis=0, tiled=True)
    expert_ids = jnp.arange(experts, dtype=jnp.int32)

    def mask_of(route_rows):
        return jnp.any(route_rows[:, :, None] == expert_ids[None, None, :], 1)

    mask_own = mask_of(routes_own)
    own_mats = [value.reshape(local_experts * hidden, model_width) for value in (w_gate.transpose(0, 2, 1), w_up.transpose(0, 2, 1), w_down)]

    cosine, sine_table = rope_tables(positions, head_size)
    half = jnp.arange(head_size, dtype=jnp.int32) < head_size // 2
    sine_table = jnp.where(half, -sine_table, sine_table)
    ranks = jnp.stack([tensor_rank, expert_rank]).astype(jnp.int32)
    normalized_input, qp, kp, q, k, v, prob, attended_rows, keep, give_part = attend(
        ranks, hidden_in, attn_gain, w_query, w_key, value_weight, q_gain, k_gain, cosine, sine_table,
        segments, w_out, shard_rows,
    )

    def reduce_rows(keep, give, first=()):
        half = keep + swap(give, 1).astype(jnp.float32)
        high = tensor_rank // 2
        keep = lax.dynamic_index_in_dim(half, high, 0, False)
        give, first = tie(bf(lax.dynamic_index_in_dim(half, 1 - high, 0, False)), first)
        return keep + swap(give, 2).astype(jnp.float32), first

    def gather_rows(own):
        far = swap(own, 2)
        both = jnp.stack([own, far])
        near = swap(both, 1)
        rows = jnp.zeros((tensor_size, shard_rows, model_width), own.dtype)
        for value, step in ((own, 0), (far, 2), (near[0], 1), (near[1], 3)):
            rows = lax.dynamic_update_index_in_dim(rows, value, tensor_rank ^ step, 0)
        return rows.reshape(tok_count, model_width)

    far_gate = swap(own_mats[0], 2)
    attn_sum, far_gate = reduce_rows(keep, give_part, far_gate)
    residual = own_rows(hidden_in).astype(jnp.float32) + attn_sum
    inv_second = lax.rsqrt(jnp.mean(residual * residual, -1, keepdims=True) + epsilon)
    normed_ffn = (residual * inv_second * ffn_gain).astype(jnp.bfloat16)

    def gates_of(rows, mask):
        logits = jnp.where(mask, mm(rows, router), far_below)
        return jax.nn.softmax(logits, -1)

    gates_own = gates_of(normed_ffn, mask_own)
    far_up = swap(own_mats[1], 2)
    far_down = swap(own_mats[2], 2)
    normed_all, (sent, far_up) = order.gather(normed_ffn, (sent, far_up))
    normed_all, attended_rows, far_down = tie(normed_all, attended_rows, far_down)
    far_mats = [far_gate, far_up, far_down]
    attended_all = lax.all_gather(attended_rows, "expert", axis=0, tiled=True)
    normed_all = normed_all.reshape(group * shard_rows, model_width)
    grad_all = sent[:, :model_width]
    near_mats = [swap(value, 1) for value in own_mats]
    last_mats = [swap(value, 1) for value in far_mats]
    shards = (own_mats, near_mats, far_mats, last_mats)
    in_mats = [value for shard in shards for value in shard[:2]]
    down_mats = [shard[2] for shard in shards]
    width = local_experts * hidden
    given = (ranks, normed_all, sent)
    near_count = len(shards) // 2
    pre_near, gated_near, gates_packed, marks = run_experts(
        *given, in_mats[: 2 * near_count], down_mats[:near_count], local_experts, routes.shape[1], router.T
    )
    spare_cols = 128 * (-(-2 * experts // 128))
    out_part, back_part, pre_last, gated_last = run_experts(
        *given, in_mats, down_mats, local_experts, routes.shape[1],
        before=(gates_packed, marks, pre_near, gated_near), spare=spare_cols,
    )
    def weight_grads(step):
        pre, gated = ((pre_near, gated_near), (pre_last, gated_last))[step // near_count]
        at = step % near_count
        pre, gated = pre[:, at * 2 * width : (at + 1) * 2 * width], gated[:, at * width : (at + 1) * width]
        return mm(pre, normed_all, (0, 0)), mm(gated, grad_all, (0, 0))

    def give(parts, step):
        return [swap(bf(part), step).astype(jnp.float32) for part in parts]

    far = give(weight_grads(3), 1)
    near = give(weight_grads(1), 1)
    far_part = [bf(a + b) for a, b in zip(weight_grads(2), far)]
    near_part = [a + b for a, b in zip(weight_grads(0), near)]
    far_part = [far_part[0][:width], far_part[0][width:], far_part[1]]

    far_part = tuple(far_part)
    arrived = [swap(far_part[0], 2)]
    back_sum, far_part, attended_all, arrived[0], _ = order.scatter(
        back_part.reshape(group, shard_rows, -1), far_part, attended_all, arrived[0]
    )
    gate_grad_own = (
        back_sum[:, model_width : model_width + experts]
        + back_sum[:, model_width + spare_cols // 2 :][:, :experts]
    )
    back_sum = back_sum[:, :model_width]
    grad_out = cot_own.astype(jnp.float32)
    grad_chosen = gates_own * (
        gate_grad_own - jnp.sum(gates_own * gate_grad_own, -1, keepdims=True)
    )
    grad_logits = bf(jnp.where(mask_own, grad_chosen, 0.0))
    router_part = mm(normed_ffn, grad_logits, (0, 0))
    grad_normed_ffn = back_sum + mm(grad_logits, router, (1, 1))
    ffn_gain_part = jnp.sum(grad_normed_ffn * residual * inv_second, 0)
    grad_residual = grad_out + norm_back(grad_normed_ffn * ffn_gain, residual, inv_second)
    grad_attn = gather_rows(bf(grad_residual))
    grad_attn, *left = tie(grad_attn, *far_part[1:])
    arrived += [swap(piece, 2) for piece in left]
    slice_rows = model_width // group
    attn_cols = lax.all_to_all(
        grad_attn.reshape(tok_count, group, slice_rows).transpose(1, 0, 2),
        "expert",
        split_axis=0,
        concat_axis=0,
        tiled=True,
    ).reshape(group * tok_count, slice_rows)
    grad_attn, out_part = tie(grad_attn, out_part)
    out_sum = lax.psum_scatter(
        out_part.reshape(group, shard_rows, model_width), "expert", scatter_dimension=0, tiled=False
    )
    spare = 16
    grad_attn, attn_cols = tie(grad_attn, attn_cols)
    packed, gain_parts, attn_gain_part, keep, give_part = attend_back(
        ranks, hidden_in, normalized_input, grad_attn, w_query, w_key, value_weight, q_gain, k_gain, cosine,
        sine_table, w_out, qp, kp, q, k, v, prob, shard_rows, group, spare,
    )
    grad_normed, _ = reduce_rows(keep, give_part)
    inputs_own = own_rows(hidden_in).astype(jnp.float32)
    inv_own = lax.rsqrt(jnp.mean(inputs_own * inputs_own, -1, keepdims=True) + epsilon)
    input_grad = gather_rows(
        bf(grad_residual + norm_back(grad_normed * attn_gain, inputs_own, inv_own))
    ).astype(jnp.float32)

    small = jnp.concatenate(
        [
            router_part.reshape(group, -1),
            attn_gain_part.reshape(group, -1),
            ffn_gain_part.reshape(group, -1),
            jnp.broadcast_to(gain_parts[:2].reshape(1, -1), (group, 2 * head_size)),
        ],
        1,
    )
    small = jnp.pad(small, ((0, 0), (0, spare * packed.shape[2] - small.shape[1])))
    packed = lax.dynamic_update_slice(
        packed, bf(small).reshape(group, spare, packed.shape[2]), (0, slice_rows, 0)
    )
    packed, out_sum, _, _, _ = order.scatter(packed, out_sum, (), ())
    w_out_grad = mm(attended_all, attn_cols, (0, 0))
    layer_out = gather_rows(bf(residual + out_sum.astype(jnp.float32)))
    query_width, key_width = w_query.shape[1], w_key.shape[1]
    w_query_grad = packed[:slice_rows, :query_width]
    w_key_grad = packed[:slice_rows, query_width : query_width + key_width]
    w_value_grad = packed[:slice_rows, query_width + key_width :]
    small = packed[slice_rows:]
    small = small + swap(bf(small), 1).astype(jnp.float32)
    small = (small + swap(bf(small), 2).astype(jnp.float32)).reshape(-1)
    cuts = [slice_rows * experts, slice_rows, slice_rows, head_size, head_size]
    router_grad, attn_gain_grad, ffn_gain_grad, q_gain_all, k_gain_all = [
        small[sum(cuts[:i]) : sum(cuts[: i + 1])] for i in range(len(cuts))
    ]
    parts = [near_part[0][:width], near_part[0][width:], near_part[1]]
    gate_t, up_t, w_down_grad = [
        (a + b.astype(jnp.float32)).reshape(local_experts, hidden, model_width)
        for a, b in zip(parts, arrived)
    ]
    w_gate_grad, w_up_grad = gate_t.transpose(0, 2, 1), up_t.transpose(0, 2, 1)
    gain_count = head_size // group
    gain_at = expert_rank * gain_count
    return (
        layer_out,
        input_grad,
        attn_gain_grad,
        w_query_grad,
        w_key_grad,
        w_value_grad,
        lax.dynamic_slice_in_dim(q_gain_all, gain_at, gain_count),
        lax.dynamic_slice_in_dim(k_gain_all, gain_at, gain_count),
        w_out_grad,
        ffn_gain_grad,
        router_grad.reshape(slice_rows, experts),
        w_gate_grad,
        w_up_grad,
        w_down_grad,
    )


def solution(mesh):
    placed = (
        P("expert", None),
        P("expert", None),
        P("expert"),
        P("expert"),
        P("expert", None),
        P(),
        P(None, "tensor"),
        P(None, "tensor"),
        P(None, "tensor"),
        P(),
        P(),
        P("tensor", None),
        P(),
        P(),
        P("expert", None, "tensor"),
        P("expert", None, "tensor"),
        P("expert", "tensor", None),
    )
    return jax.shard_map(
        body,
        mesh=mesh,
        in_specs=placed,
        out_specs=(
            P("expert", None),
            P("expert", None),
            P("expert"),
            P("expert", "tensor"),
            P("expert", "tensor"),
            P("expert", "tensor"),
            P("expert"),
            P("expert"),
            P("tensor", "expert"),
            P("expert"),
            P("expert", None),
            P("expert", None, "tensor"),
            P("expert", None, "tensor"),
            P("expert", "tensor", None),
        ),
        check_vma=False,
    )
```

```python
import functools

import jax
import jax.numpy as jnp
from jax import lax
from jax.experimental import pallas as pl
from jax.experimental.pallas import tpu as pltpu
from jax.sharding import PartitionSpec as P

epsilon = 1e-06
rope_base = 1000000.0
far_below = -1e30


def rope_tables(positions, head_size):
    half_size = head_size // 2
    frequency = rope_base ** (-(jnp.arange(half_size, dtype=jnp.float32) * 2.0) / head_size)
    angles = positions.astype(jnp.float32)[:, None] * frequency[None, :]
    cosine = jnp.cos(angles)
    sine_table = jnp.sin(angles)
    return (jnp.concatenate([cosine, cosine], -1), jnp.concatenate([sine_table, sine_table], -1))


def norm_back(grad_scaled, value_rows, scales):
    return scales * (
        grad_scaled
        - value_rows * scales * scales * jnp.mean(grad_scaled * value_rows, -1, keepdims=True)
    )


def bf(value):
    return value.astype(jnp.bfloat16)


def mm(left, right, contract=(1, 0)):
    return lax.dot_general(
        left, right, (((contract[0],), (contract[1],)), ((), ())), preferred_element_type=jnp.float32
    )


def tie(*values):
    return lax.optimization_barrier(values)


def swap(value, step):
    size = lax.axis_size("tensor")
    return lax.ppermute(value, "tensor", [(i, i ^ step) for i in range(size)])


vmem_bytes = 58 * 2**20
small_cost = pl.CostEstimate(flops=2**20, bytes_accessed=2**16, transcendentals=0)


def whole(shape):
    return pl.BlockSpec(shape, lambda *_: (0,) * len(shape))


def turn(rows):
    return pltpu.roll(rows, rows.shape[-1] // 2, 1)


def inverse_rms(rows):
    return lax.rsqrt(jnp.mean(rows * rows, -1, keepdims=True) + epsilon)


def split_rows(rank_ref, total, keep, give):
    rows = keep.shape[1]
    low = rank_ref[0] % 2
    for high in range(keep.shape[0]):
        start = pl.multiple_of((2 * high + low) * rows, rows)
        keep[high] = total[pl.ds(start, rows), :]
        start = pl.multiple_of((2 * high + 1 - low) * rows, rows)
        give[high] = bf(total[pl.ds(start, rows), :])


def attend_kernel(
    rank_ref, x, gain, w_query, w_key, w_value, q_gain, k_gain, cosine, sine, seg_col, seg_row, w_out,
    xn, qp, kp, q, k, v, prob, o, keep, give, total,
):
    step, steps = pl.program_id(0), pl.num_programs(0)
    tokens, head = kp.shape
    cut = keep.shape[1]

    @pl.when(step == 0)
    def _():
        @pl.loop(0, tokens // cut)
        def _(i):
            rows = pl.ds(pl.multiple_of(i * cut, cut), cut)
            value = x[rows, :].astype(jnp.float32)
            xn[rows, :] = bf(value * inverse_rms(value) * gain[...])

        raw = mm(xn[...], w_key[...])
        kp[...] = raw
        scaled = raw * inverse_rms(raw) * k_gain[...]
        k[...] = bf(scaled * cosine[...] + turn(scaled) * sine[...])
        v[...] = bf(mm(xn[...], w_value[...]))
        total[...] = jnp.zeros_like(total)

    raw_pair = mm(xn[...], w_query[...])
    qp[...] = raw_pair
    visible = (seg_col[...] == seg_row[...]) & (
        lax.broadcasted_iota(jnp.int32, (tokens, tokens), 0)
        >= lax.broadcasted_iota(jnp.int32, (tokens, tokens), 1)
    )
    for i in range(prob.shape[0]):
        cols = slice(i * head, (i + 1) * head)
        raw = raw_pair[:, cols]
        scaled = raw * inverse_rms(raw) * q_gain[...]
        rows = bf(scaled * cosine[...] + turn(scaled) * sine[...])
        q[:, cols] = rows
        scores = jnp.where(visible, mm(rows, k[...], (1, 1)) * head**-0.5, far_below)
        weight = jnp.exp(scores - jnp.max(scores, -1, keepdims=True))
        low = bf(weight * (1.0 / jnp.sum(weight, -1, keepdims=True)))
        prob[i] = low
        o[:, cols] = bf(mm(low, v[...]))
    wide = 512

    @pl.loop(0, total.shape[1] // wide)
    def _(n):
        at = pl.ds(pl.multiple_of(n * wide, wide), wide)
        total[:, at] += mm(o[...], w_out[:, at])

    @pl.when(step == steps - 1)
    def _():
        split_rows(rank_ref, total, keep, give)


def attend(rank, x, gain, w_query, w_key, w_value, q_gain, k_gain, cosine, sine, segments, w_out, cut):
    tokens, width = x.shape
    head = q_gain.shape[0]
    query = w_query.shape[1]
    pair = 2
    steps = query // (pair * head)
    heads = pl.BlockSpec((tokens, pair * head), lambda j, _: (0, j))
    halves = tokens // cut // 2
    return pl.pallas_call(
        attend_kernel,
        grid_spec=pltpu.PrefetchScalarGridSpec(
            num_scalar_prefetch=1,
            grid=(steps,),
            in_specs=[
                whole((tokens, width)),
                whole((1, width)),
                pl.BlockSpec((width, pair * head), lambda j, _: (0, j)),
                whole((width, head)),
                whole((width, head)),
                whole((1, head)),
                whole((1, head)),
                whole((tokens, head)),
                whole((tokens, head)),
                whole((tokens, 1)),
                whole((1, tokens)),
                pl.BlockSpec((pair * head, width), lambda j, _: (j, 0)),
            ],
            out_specs=[
                whole((tokens, width)),
                heads,
                whole((tokens, head)),
                heads,
                whole((tokens, head)),
                whole((tokens, head)),
                pl.BlockSpec((pair, tokens, tokens), lambda j, _: (j, 0, 0)),
                heads,
                whole((halves, cut, width)),
                whole((halves, cut, width)),
            ],
            scratch_shapes=[pltpu.VMEM((tokens, width), jnp.float32)],
        ),
        out_shape=[
            jax.ShapeDtypeStruct((tokens, width), jnp.bfloat16),
            jax.ShapeDtypeStruct((tokens, query), jnp.float32),
            jax.ShapeDtypeStruct((tokens, head), jnp.float32),
            jax.ShapeDtypeStruct((tokens, query), jnp.bfloat16),
            jax.ShapeDtypeStruct((tokens, head), jnp.bfloat16),
            jax.ShapeDtypeStruct((tokens, head), jnp.bfloat16),
            jax.ShapeDtypeStruct((query // head, tokens, tokens), jnp.bfloat16),
            jax.ShapeDtypeStruct((tokens, query), jnp.bfloat16),
            jax.ShapeDtypeStruct((halves, cut, width), jnp.float32),
            jax.ShapeDtypeStruct((halves, cut, width), jnp.bfloat16),
        ],
        compiler_params=pltpu.CompilerParams(vmem_limit_bytes=vmem_bytes),
        cost_estimate=small_cost,
        name="attend",
    )(
        rank, x, gain[None], w_query, w_key, w_value, q_gain[None], k_gain[None], cosine, sine,
        segments[:, None], segments[None, :], w_out,
    )


def attend_back_kernel(
    rank_ref, x, xn, dattn, w_query, w_key, w_value, q_gain, k_gain, cosine, sine, w_out, qp, kp, q, k, v, prob,
    packed, gains, attn_gain, keep, give, total, dk, dv, low,
):
    step, steps = pl.program_id(0), pl.num_programs(0)
    tokens, head = kp.shape
    cut = keep.shape[1]
    scale = head**-0.5
    width = x.shape[1]
    wide = 512
    blocks = packed.shape[0]
    block_rows = width // blocks

    def unrotate(grad):
        return grad * cosine[...] - turn(grad) * sine[...]

    def unnorm(grad, raw, inverse, gain):
        scaled = grad * gain
        return inverse * (scaled - raw * inverse * inverse * jnp.mean(scaled * raw, -1, keepdims=True))

    def add_total(left, right, at):
        total[:, at] += mm(left, right[at, :], (1, 1))

    def put_packed(n):
        at = pl.ds(pl.multiple_of(n * wide, wide), wide)
        grad = bf(mm(xn[:, at], low[...], (0, 0)))
        many = wide // block_rows
        first = n * many
        packed[pl.ds(first, many), pl.ds(0, block_rows), :] = grad.reshape(many, block_rows, -1)

    @pl.when(step == 0)
    def _():
        total[...] = jnp.zeros_like(total)
        dk[...] = jnp.zeros_like(dk)
        dv[...] = jnp.zeros_like(dv)
        gains[...] = jnp.zeros_like(gains)

    @pl.when(step < steps - 1)
    def _():
        dout_pair = bf(mm(dattn[...], w_out[...], (1, 1)))
        for i in range(prob.shape[0]):
            cols = slice(i * head, (i + 1) * head)
            dout = dout_pair[:, cols]
            weight = prob[i]
            dp = mm(dout, v[...], (1, 1))
            wide_weight = weight.astype(jnp.float32)
            ds = bf(wide_weight * (dp - jnp.sum(wide_weight * dp, -1, keepdims=True)))
            dv[...] += mm(weight, dout, (0, 0))
            dk[...] += mm(ds, q[:, cols], (0, 0))
            dqu = unrotate(mm(ds, k[...]) * scale)
            raw = qp[:, cols]
            inverse = inverse_rms(raw)
            gains[0:1, :] += jnp.sum(dqu * raw * inverse, 0, keepdims=True)
            low[:, cols] = bf(unnorm(dqu, raw, inverse, q_gain[...]))

        @pl.loop(0, width // wide)
        def _(n):
            put_packed(n)
            add_total(low[...], w_query, pl.ds(pl.multiple_of(n * wide, wide), wide))

    @pl.when(step == steps - 1)
    def _():
        dku = unrotate(dk[...] * scale)
        raw = kp[...]
        inverse = inverse_rms(raw)
        gains[1:2, :] = jnp.sum(dku * raw * inverse, 0, keepdims=True)
        low[:, :head] = bf(unnorm(dku, raw, inverse, k_gain[...]))
        low[:, head:] = bf(dv[...])

        @pl.loop(0, width // wide)
        def _(n):
            put_packed(n)
            at = pl.ds(pl.multiple_of(n * wide, wide), wide)
            add_total(low[:, :head], w_key, at)
            add_total(low[:, head:], w_value, at)

        attn_gain[...] = jnp.zeros_like(attn_gain)

        @pl.loop(0, tokens // cut)
        def _(i):
            rows = pl.ds(pl.multiple_of(i * cut, cut), cut)
            value = x[rows, :].astype(jnp.float32)
            attn_gain[...] += jnp.sum(total[rows, :] * value * inverse_rms(value), 0, keepdims=True)

        split_rows(rank_ref, total, keep, give)


def attend_back(
    rank, x, xn, dattn, w_query, w_key, w_value, q_gain, k_gain, cosine, sine, w_out, qp, kp, q, k, v, prob,
    cut, blocks, spare,
):
    tokens, width = x.shape
    head = q_gain.shape[0]
    query = w_query.shape[1]
    pair = 2
    steps = query // (pair * head)
    last = steps - 1
    heads = pl.BlockSpec((tokens, pair * head), lambda j, _: (0, jnp.minimum(j, last)))
    halves = tokens // cut // 2
    block_rows = width // blocks + spare
    return pl.pallas_call(
        attend_back_kernel,
        grid_spec=pltpu.PrefetchScalarGridSpec(
            num_scalar_prefetch=1,
            grid=(steps + 1,),
            in_specs=[
                whole((tokens, width)),
                whole((tokens, width)),
                whole((tokens, width)),
                pl.BlockSpec((width, pair * head), lambda j, _: (0, jnp.minimum(j, last))),
                whole((width, head)),
                whole((width, head)),
                whole((1, head)),
                whole((1, head)),
                whole((tokens, head)),
                whole((tokens, head)),
                pl.BlockSpec((pair * head, width), lambda j, _: (jnp.minimum(j, last), 0)),
                heads,
                whole((tokens, head)),
                heads,
                whole((tokens, head)),
                whole((tokens, head)),
                pl.BlockSpec((pair, tokens, tokens), lambda j, _: (jnp.minimum(j, last), 0, 0)),
            ],
            out_specs=[
                pl.BlockSpec((blocks, block_rows, pair * head), lambda j, _: (0, 0, j)),
                whole((8, head)),
                whole((1, width)),
                whole((halves, cut, width)),
                whole((halves, cut, width)),
            ],
            scratch_shapes=[
                pltpu.VMEM((tokens, width), jnp.float32),
                pltpu.VMEM((tokens, head), jnp.float32),
                pltpu.VMEM((tokens, head), jnp.float32),
                pltpu.VMEM((tokens, pair * head), jnp.bfloat16),
            ],
        ),
        out_shape=[
            jax.ShapeDtypeStruct((blocks, block_rows, query + 2 * head), jnp.bfloat16),
            jax.ShapeDtypeStruct((8, head), jnp.float32),
            jax.ShapeDtypeStruct((1, width), jnp.float32),
            jax.ShapeDtypeStruct((halves, cut, width), jnp.float32),
            jax.ShapeDtypeStruct((halves, cut, width), jnp.bfloat16),
        ],
        compiler_params=pltpu.CompilerParams(vmem_limit_bytes=vmem_bytes),
        cost_estimate=pl.CostEstimate(flops=3 * 10**10, bytes_accessed=2**20, transcendentals=0),
        name="attend_back",
    )(
        rank, x, xn, dattn, w_query, w_key, w_value, q_gain[None], k_gain[None], cosine, sine, w_out,
        qp, kp, q, k, v, prob,
    )


class Loads:
    def __init__(self, sources, target, sems, shards):
        height = sources[0].shape[0]
        self.each = len(sources) // shards
        self.copies = [
            pltpu.make_async_copy(source, target.at[pl.ds(i * height, height), :], sems.at[i])
            for i, source in enumerate(sources)
        ]

    def start(self, shard):
        for copy in self.copies[shard * self.each : (shard + 1) * self.each]:
            copy.start()

    def wait(self, shard):
        for copy in self.copies[shard * self.each : (shard + 1) * self.each]:
            copy.wait()


def experts_kernel(rank_ref, hn, g, *rest, shards, before, local, hidden, top_count):
    last = before > 0
    every = before + shards
    in_count = every if last else shards
    if last:
        gates, totals_in, pre_before, gated_before = rest[:4]
        rest = rest[4:]
    else:
        sent, router = rest[:2]
        rest = rest[2:]
    in_hbm, down_hbm, rest = rest[: 2 * in_count], rest[2 * in_count : 3 * in_count], rest[3 * in_count :]
    if last:
        out, back, pre_grad, gated = rest[:4]
        rest = rest[4:]
        totals = rest[-1]
    else:
        pre_grad, gated, gates, totals = rest[:4]
        rest = rest[4:]
    in_all, down_all, gates_wide, in_sems, down_sems = rest[:5]
    chunk, shard = pl.program_id(0), pl.program_id(1)
    width = local * hidden
    rows, model = hn.shape
    first = before if last else 0
    in_loads = Loads(in_hbm, in_all, in_sems, in_count)
    down_loads = Loads(down_hbm, down_all, down_sems, in_count)
    owner = lax.broadcasted_iota(jnp.int32, (rows, width), 1) // hidden

    @pl.when((chunk == 0) & (shard == 0))
    def _():
        order = list(range(first, in_count)) + list(range(first))
        for i in order:
            in_loads.start(i)
            down_loads.start(i)

    @pl.when(shard == 0)
    def _():
        if last:
            totals[...] = totals_in[...]
        else:
            names = lax.broadcasted_iota(jnp.int32, (rows, router.shape[0]), 1).astype(jnp.float32)
            chosen = sent[...].astype(jnp.float32)
            mask = jnp.zeros(names.shape, jnp.bool_)
            for j in range(top_count):
                mask = mask | (chosen[:, j : j + 1] == names)
            logits = jnp.where(mask, mm(hn[...], router[...], (1, 1)), far_below)
            weight = jnp.exp(logits - jnp.max(logits, -1, keepdims=True))
            weight = weight * (1.0 / jnp.sum(weight, -1, keepdims=True))
            lanes = lax.broadcasted_iota(jnp.int32, gates.shape, 1)
            packed = jnp.zeros(gates.shape, jnp.float32)
            for e in range(local):
                here = names == (rank_ref[1] * local + e).astype(jnp.float32)
                value = jnp.sum(jnp.where(here, weight, 0.0), -1, keepdims=True)
                packed = packed + jnp.where(lanes == e, value, 0.0)
            gates[...] = packed
            totals[...] = jnp.zeros_like(totals)
        wide = jnp.zeros((rows, width), jnp.float32)
        for e in range(local):
            wide = jnp.where(owner == e, gates[:, e : e + 1], wide)
        gates_wide[...] = wide

    for i in range(shards):
        @pl.when((chunk == 0) & (shard == i))
        def _(i=i):
            in_loads.wait(first + i)
            down_loads.wait(first + i)

    in_at = pl.multiple_of((first + shard) * 2 * width, 2 * width)
    down_at = pl.multiple_of((first + shard) * width, width)
    pre = mm(hn[...], in_all[pl.ds(in_at, 2 * width), :], (1, 1))
    grad_middle = mm(g[...], down_all[pl.ds(down_at, width), :], (1, 1))
    gate_pre, up_pre = pre[:, :width], pre[:, width:]
    sigmoid_gate = jax.nn.sigmoid(gate_pre)
    activated = gate_pre * sigmoid_gate
    middle = activated * up_pre
    mid_at = pl.multiple_of(shard * width, width)
    gated[:, pl.ds(mid_at, width)] = bf(middle * gates_wide[...])
    product = middle * grad_middle
    lanes = lax.broadcasted_iota(jnp.int32, totals.shape, 1)
    added = totals[...]
    for e in range(local):
        value = jnp.sum(jnp.where(owner == e, product, 0.0), -1, keepdims=True)
        added = added + jnp.where(lanes == e, value, 0.0)
    totals[...] = added
    grad_middle = grad_middle * gates_wide[...]
    gate_at = pl.multiple_of(shard * 2 * width, 2 * width)
    pre_grad[:, pl.ds(gate_at, width)] = bf(
        grad_middle * up_pre * (sigmoid_gate + activated * (1.0 - sigmoid_gate))
    )
    pre_grad[:, pl.ds(pl.multiple_of(gate_at + width, width), width)] = bf(grad_middle * activated)

    if last:

        @pl.when(shard == shards - 1)
        def _():
            @pl.when(chunk == 0)
            def _():
                for i in range(before):
                    in_loads.wait(i)
                    down_loads.wait(i)

            wide = 512

            @pl.loop(0, model // wide)
            def _(n):
                cols = pl.ds(pl.multiple_of(n * wide, wide), wide)
                cut = before * width
                back[:, cols] = bf(
                    mm(pre_before[...], in_all[: 2 * cut, cols]) + mm(pre_grad[...], in_all[2 * cut :, cols])
                )
                out[:, cols] = bf(
                    mm(gated_before[...], down_all[:cut, cols]) + mm(gated[...], down_all[cut:, cols])
                )

            spare = back.shape[1] - model
            places = lax.broadcasted_iota(jnp.int32, (rows, spare), 1)
            tail = jnp.zeros((rows, spare), jnp.float32)
            for e in range(local):
                value = totals[:, e : e + 1]
                high = bf(value).astype(jnp.float32)
                here = rank_ref[1] * local + e
                tail = tail + jnp.where(places == here, high, 0.0)
                tail = tail + jnp.where(places == spare // 2 + here, value - high, 0.0)
            back[:, model:] = bf(tail)


def run_experts(ranks, hn, sent, in_mats, down_mats, local, top_count, router=None, before=None, spare=0):
    tokens, model = hn.shape
    width = down_mats[0].shape[0]
    every = len(down_mats)
    earlier = 0 if before is None else before[2].shape[1] // (2 * width)
    shards = every - earlier
    rows = tokens
    while rows > 768:
        rows //= 2

    def block(cols, step=0):
        return pl.BlockSpec((rows, cols), lambda c, s, _: (c, step), pipeline_mode=pl.Buffered(1))

    hbm = [pl.BlockSpec(memory_space=pl.ANY)] * (3 * every)
    scratch = [
        pltpu.VMEM((every * 2 * width, model), jnp.bfloat16),
        pltpu.VMEM((every * width, model), jnp.bfloat16),
        pltpu.VMEM((rows, width), jnp.float32),
        pltpu.SemaphoreType.DMA((2 * every,)),
        pltpu.SemaphoreType.DMA((every,)),
    ]
    own = [(shards * 2 * width, jnp.bfloat16), (shards * width, jnp.bfloat16)]
    if before is None:
        extra, specs = (sent, router), [block(128, model // 128), whole(router.shape)]
        outs = own + [(128, jnp.float32)] * 2
    else:
        extra = before
        specs = [block(value.shape[1]) for value in before]
        outs = [(model, jnp.bfloat16), (model + spare, jnp.bfloat16)] + own
        scratch.append(pltpu.VMEM((rows, 128), jnp.float32))
    return pl.pallas_call(
        functools.partial(
            experts_kernel, shards=shards, before=earlier, local=local, hidden=width // local, top_count=top_count
        ),
        grid_spec=pltpu.PrefetchScalarGridSpec(
            num_scalar_prefetch=1,
            grid=(tokens // rows, shards),
            in_specs=[block(model), block(model)] + specs + hbm,
            out_specs=[block(cols) for cols, _ in outs],
            scratch_shapes=scratch,
        ),
        out_shape=[jax.ShapeDtypeStruct((tokens, cols), kind) for cols, kind in outs],
        compiler_params=pltpu.CompilerParams(vmem_limit_bytes=vmem_bytes),
        cost_estimate=small_cost,
        name="experts_near" if before is None else "experts_far",
    )(ranks, hn, sent, *extra, *in_mats, *down_mats)


class Tokens:
    def __init__(self):
        self.size = lax.axis_size("expert")
        self.line = self.size == 8
        self.me = lax.axis_index("expert")
        self.z, self.y = self.me // 2, self.me % 2

    def across(self, value):
        return lax.ppermute(value, "expert", [(i, i ^ 1) for i in range(8)])

    def along(self, value, step):
        return lax.ppermute(value, "expert", [(i, i ^ (2 * step)) for i in range(8)])

    def place(self, step, other):
        return (self.z ^ step) * 2 + (1 - self.y if other else self.y)

    def gather(self, own, early):
        if not self.line:
            return lax.all_gather(own, "expert", axis=0, tiled=False), early
        blocks = [own] + [self.along(own, step) for step in (1, 2, 3)]
        others = [self.across(own)]
        blocks[1], early = tie(blocks[1], early)
        others += [self.across(value) for value in blocks[1:]]
        rows = jnp.zeros((self.size, *own.shape), own.dtype)
        for step in range(4):
            for value, other in ((blocks[step], False), (others[step], True)):
                rows = lax.dynamic_update_index_in_dim(rows, value, self.place(step, other), 0)
        return rows, early

    def scatter(self, parts, begun, late, last, middle=()):
        if not self.line:
            total = lax.psum_scatter(parts, "expert", scatter_dimension=0, tiled=False)
            return total.astype(jnp.float32), begun, late, last, middle

        def part(step, other):
            return lax.dynamic_index_in_dim(parts, self.place(step, other), 0, False)

        def pair_sum(step):
            return part(step, False).astype(jnp.float32) + across[step].astype(jnp.float32)

        across = {step: self.across(part(step, True)) for step in (3, 2, 1, 0)}
        across[3], begun = tie(across[3], begun)
        moved = {step: self.along(bf(pair_sum(step)), step) for step in (3, 2)}
        across[1], moved[3], middle = tie(across[1], moved[3], middle)
        moved[1] = self.along(bf(pair_sum(1)), 1)
        across[0], moved[2], late = tie(across[0], moved[2], late)
        moved[1], last = tie(moved[1], last)
        total = pair_sum(0) + sum(value.astype(jnp.float32) for value in moved.values())
        return total, begun, late, last, middle


def body(
    hidden_in,
    cotangent,
    segments,
    positions,
    routes,
    attn_gain,
    w_query,
    w_key,
    value_weight,
    q_gain,
    k_gain,
    w_out,
    ffn_gain,
    router,
    w_gate,
    w_up,
    w_down,
):
    tok_count, model_width = hidden_in.shape
    head_size = q_gain.shape[0]
    experts = router.shape[1]
    local_experts, _, hidden = w_gate.shape
    tensor_size = lax.axis_size("tensor")
    tensor_rank = lax.axis_index("tensor")
    expert_rank = lax.axis_index("expert")
    shard_rows = tok_count // tensor_size
    order = Tokens()
    group = order.size

    def own_rows(value):
        return lax.dynamic_slice_in_dim(value, tensor_rank * shard_rows, shard_rows)

    cot_own = own_rows(cotangent)
    routes_own = own_rows(routes)
    spare_cols = 128
    routes_wide = jnp.pad(bf(routes_own), ((0, 0), (0, spare_cols - routes.shape[1])))
    sent_own = jnp.concatenate([cot_own, routes_wide], 1)
    hidden_in, sent_own = tie(hidden_in, sent_own)
    sent = lax.all_gather(sent_own, "expert", axis=0, tiled=True)
    expert_ids = jnp.arange(experts, dtype=jnp.int32)

    def mask_of(route_rows):
        return jnp.any(route_rows[:, :, None] == expert_ids[None, None, :], 1)

    mask_own = mask_of(routes_own)
    own_mats = [value.reshape(local_experts * hidden, model_width) for value in (w_gate.transpose(0, 2, 1), w_up.transpose(0, 2, 1), w_down)]

    cosine, sine_table = rope_tables(positions, head_size)
    half = jnp.arange(head_size, dtype=jnp.int32) < head_size // 2
    sine_table = jnp.where(half, -sine_table, sine_table)
    ranks = jnp.stack([tensor_rank, expert_rank]).astype(jnp.int32)
    normalized_input, qp, kp, q, k, v, prob, attended_rows, keep, give_part = attend(
        ranks, hidden_in, attn_gain, w_query, w_key, value_weight, q_gain, k_gain, cosine, sine_table,
        segments, w_out, shard_rows,
    )

    def reduce_rows(keep, give, first=()):
        half = keep + swap(give, 1).astype(jnp.float32)
        high = tensor_rank // 2
        keep = lax.dynamic_index_in_dim(half, high, 0, False)
        give, first = tie(bf(lax.dynamic_index_in_dim(half, 1 - high, 0, False)), first)
        return keep + swap(give, 2).astype(jnp.float32), first

    def gather_rows(own):
        far = swap(own, 2)
        both = jnp.stack([own, far])
        near = swap(both, 1)
        rows = jnp.zeros((tensor_size, shard_rows, model_width), own.dtype)
        for value, step in ((own, 0), (far, 2), (near[0], 1), (near[1], 3)):
            rows = lax.dynamic_update_index_in_dim(rows, value, tensor_rank ^ step, 0)
        return rows.reshape(tok_count, model_width)

    far_gate = swap(own_mats[0], 2)
    attn_sum, far_gate = reduce_rows(keep, give_part, far_gate)
    residual = own_rows(hidden_in).astype(jnp.float32) + attn_sum
    inv_second = lax.rsqrt(jnp.mean(residual * residual, -1, keepdims=True) + epsilon)
    normed_ffn = (residual * inv_second * ffn_gain).astype(jnp.bfloat16)

    def gates_of(rows, mask):
        logits = jnp.where(mask, mm(rows, router), far_below)
        return jax.nn.softmax(logits, -1)

    gates_own = gates_of(normed_ffn, mask_own)
    far_up = swap(own_mats[1], 2)
    far_down = swap(own_mats[2], 2)
    normed_all, (sent, far_up) = order.gather(normed_ffn, (sent, far_up))
    normed_all, attended_rows, far_down = tie(normed_all, attended_rows, far_down)
    far_mats = [far_gate, far_up, far_down]
    attended_all = lax.all_gather(attended_rows, "expert", axis=0, tiled=True)
    normed_all = normed_all.reshape(group * shard_rows, model_width)
    grad_all = sent[:, :model_width]
    near_mats = [swap(value, 1) for value in own_mats]
    last_mats = [swap(value, 1) for value in far_mats]
    shards = (own_mats, near_mats, far_mats, last_mats)
    in_mats = [value for shard in shards for value in shard[:2]]
    down_mats = [shard[2] for shard in shards]
    width = local_experts * hidden
    given = (ranks, normed_all, sent)
    near_count = len(shards) // 2
    pre_near, gated_near, gates_packed, marks = run_experts(
        *given, in_mats[: 2 * near_count], down_mats[:near_count], local_experts, routes.shape[1], router.T
    )
    spare_cols = 128 * (-(-2 * experts // 128))
    out_part, back_part, pre_last, gated_last = run_experts(
        *given, in_mats, down_mats, local_experts, routes.shape[1],
        before=(gates_packed, marks, pre_near, gated_near), spare=spare_cols,
    )
    def weight_grads(step):
        pre, gated = ((pre_near, gated_near), (pre_last, gated_last))[step // near_count]
        at = step % near_count
        pre, gated = pre[:, at * 2 * width : (at + 1) * 2 * width], gated[:, at * width : (at + 1) * width]
        return mm(pre, normed_all, (0, 0)), mm(gated, grad_all, (0, 0))

    def give(parts, step):
        return [swap(bf(part), step).astype(jnp.float32) for part in parts]

    far = give(weight_grads(3), 1)
    near = give(weight_grads(1), 1)
    far_part = [bf(a + b) for a, b in zip(weight_grads(2), far)]
    near_part = [a + b for a, b in zip(weight_grads(0), near)]
    far_part = [far_part[0][:width], far_part[0][width:], far_part[1]]

    far_part = tuple(far_part)
    arrived = [swap(far_part[0], 2)]
    back_sum, far_part, attended_all, arrived[0], _ = order.scatter(
        back_part.reshape(group, shard_rows, -1), far_part, attended_all, arrived[0]
    )
    gate_grad_own = (
        back_sum[:, model_width : model_width + experts]
        + back_sum[:, model_width + spare_cols // 2 :][:, :experts]
    )
    back_sum = back_sum[:, :model_width]
    grad_out = cot_own.astype(jnp.float32)
    grad_chosen = gates_own * (
        gate_grad_own - jnp.sum(gates_own * gate_grad_own, -1, keepdims=True)
    )
    grad_logits = bf(jnp.where(mask_own, grad_chosen, 0.0))
    router_part = mm(normed_ffn, grad_logits, (0, 0))
    grad_normed_ffn = back_sum + mm(grad_logits, router, (1, 1))
    ffn_gain_part = jnp.sum(grad_normed_ffn * residual * inv_second, 0)
    grad_residual = grad_out + norm_back(grad_normed_ffn * ffn_gain, residual, inv_second)
    slice_rows = model_width // group
    own_cols = lax.all_to_all(
        bf(grad_residual).reshape(shard_rows, group, slice_rows).transpose(1, 0, 2),
        "expert",
        split_axis=0,
        concat_axis=0,
        tiled=True,
    )
    grad_attn = gather_rows(bf(grad_residual))
    grad_attn, far_cols, *left = tie(grad_attn, swap(own_cols, 2), *far_part[1:])
    arrived += [swap(piece, 2) for piece in left]
    grad_attn, out_part = tie(grad_attn, out_part)
    out_sum = lax.psum_scatter(
        out_part.reshape(group, shard_rows, model_width), "expert", scatter_dimension=0, tiled=False
    )
    spare = 16
    packed, gain_parts, attn_gain_part, keep, give_part = attend_back(
        ranks, hidden_in, normalized_input, grad_attn, w_query, w_key, value_weight, q_gain, k_gain, cosine,
        sine_table, w_out, qp, kp, q, k, v, prob, shard_rows, group, spare,
    )
    grad_normed, _ = reduce_rows(keep, give_part)
    inputs_own = own_rows(hidden_in).astype(jnp.float32)
    inv_own = lax.rsqrt(jnp.mean(inputs_own * inputs_own, -1, keepdims=True) + epsilon)
    input_grad = gather_rows(
        bf(grad_residual + norm_back(grad_normed * attn_gain, inputs_own, inv_own))
    ).astype(jnp.float32)

    small = jnp.concatenate(
        [
            router_part.reshape(group, -1),
            attn_gain_part.reshape(group, -1),
            ffn_gain_part.reshape(group, -1),
            jnp.broadcast_to(gain_parts[:2].reshape(1, -1), (group, 2 * head_size)),
        ],
        1,
    )
    small = jnp.pad(small, ((0, 0), (0, spare * packed.shape[2] - small.shape[1])))
    packed = lax.dynamic_update_slice(
        packed, bf(small).reshape(group, spare, packed.shape[2]), (0, slice_rows, 0)
    )
    packed, _, _, _, out_sum = order.scatter(packed, (), (), (), out_sum)
    near_cols = swap(jnp.stack([own_cols, far_cols]), 1)
    attn_cols = jnp.zeros((tensor_size, *own_cols.shape), own_cols.dtype)
    for value, step in ((own_cols, 0), (far_cols, 2), (near_cols[0], 1), (near_cols[1], 3)):
        attn_cols = lax.dynamic_update_index_in_dim(attn_cols, value, tensor_rank ^ step, 0)
    attn_cols = attn_cols.transpose(1, 0, 2, 3).reshape(group * tok_count, slice_rows)
    w_out_grad = mm(attended_all, attn_cols, (0, 0))
    layer_out = gather_rows(bf(residual + out_sum.astype(jnp.float32)))
    query_width, key_width = w_query.shape[1], w_key.shape[1]
    w_query_grad = packed[:slice_rows, :query_width]
    w_key_grad = packed[:slice_rows, query_width : query_width + key_width]
    w_value_grad = packed[:slice_rows, query_width + key_width :]
    small = packed[slice_rows:]
    small = small + swap(bf(small), 1).astype(jnp.float32)
    small = (small + swap(bf(small), 2).astype(jnp.float32)).reshape(-1)
    cuts = [slice_rows * experts, slice_rows, slice_rows, head_size, head_size]
    router_grad, attn_gain_grad, ffn_gain_grad, q_gain_all, k_gain_all = [
        small[sum(cuts[:i]) : sum(cuts[: i + 1])] for i in range(len(cuts))
    ]
    parts = [near_part[0][:width], near_part[0][width:], near_part[1]]
    gate_t, up_t, w_down_grad = [
        (a + b.astype(jnp.float32)).reshape(local_experts, hidden, model_width)
        for a, b in zip(parts, arrived)
    ]
    w_gate_grad, w_up_grad = gate_t.transpose(0, 2, 1), up_t.transpose(0, 2, 1)
    gain_count = head_size // group
    gain_at = expert_rank * gain_count
    return (
        layer_out,
        input_grad,
        attn_gain_grad,
        w_query_grad,
        w_key_grad,
        w_value_grad,
        lax.dynamic_slice_in_dim(q_gain_all, gain_at, gain_count),
        lax.dynamic_slice_in_dim(k_gain_all, gain_at, gain_count),
        w_out_grad,
        ffn_gain_grad,
        router_grad.reshape(slice_rows, experts),
        w_gate_grad,
        w_up_grad,
        w_down_grad,
    )


def solution(mesh):
    placed = (
        P("expert", None),
        P("expert", None),
        P("expert"),
        P("expert"),
        P("expert", None),
        P(),
        P(None, "tensor"),
        P(None, "tensor"),
        P(None, "tensor"),
        P(),
        P(),
        P("tensor", None),
        P(),
        P(),
        P("expert", None, "tensor"),
        P("expert", None, "tensor"),
        P("expert", "tensor", None),
    )
    return jax.shard_map(
        body,
        mesh=mesh,
        in_specs=placed,
        out_specs=(
            P("expert", None),
            P("expert", None),
            P("expert"),
            P("expert", "tensor"),
            P("expert", "tensor"),
            P("expert", "tensor"),
            P("expert"),
            P("expert"),
            P("tensor", "expert"),
            P("expert"),
            P("expert", None),
            P("expert", None, "tensor"),
            P("expert", None, "tensor"),
            P("expert", "tensor", None),
        ),
        check_vma=False,
    )
```

```python
import functools

import jax
import jax.numpy as jnp
from jax import lax
from jax.experimental import pallas as pl
from jax.experimental.pallas import tpu as pltpu
from jax.sharding import PartitionSpec as P

epsilon = 1e-06
rope_base = 1000000.0
far_below = -1e30


def rope_tables(positions, head_size):
    half_size = head_size // 2
    frequency = rope_base ** (-(jnp.arange(half_size, dtype=jnp.float32) * 2.0) / head_size)
    angles = positions.astype(jnp.float32)[:, None] * frequency[None, :]
    cosine = jnp.cos(angles)
    sine_table = jnp.sin(angles)
    return (jnp.concatenate([cosine, cosine], -1), jnp.concatenate([sine_table, sine_table], -1))


def norm_back(grad_scaled, value_rows, scales):
    return scales * (
        grad_scaled
        - value_rows * scales * scales * jnp.mean(grad_scaled * value_rows, -1, keepdims=True)
    )


def bf(value):
    return value.astype(jnp.bfloat16)


def mm(left, right, contract=(1, 0)):
    return lax.dot_general(
        left, right, (((contract[0],), (contract[1],)), ((), ())), preferred_element_type=jnp.float32
    )


def tie(*values):
    return lax.optimization_barrier(values)


def swap(value, step):
    size = lax.axis_size("tensor")
    return lax.ppermute(value, "tensor", [(i, i ^ step) for i in range(size)])


vmem_bytes = 58 * 2**20
small_cost = pl.CostEstimate(flops=2**20, bytes_accessed=2**16, transcendentals=0)


def whole(shape):
    return pl.BlockSpec(shape, lambda *_: (0,) * len(shape))


def turn(rows):
    return pltpu.roll(rows, rows.shape[-1] // 2, 1)


def inverse_rms(rows):
    return lax.rsqrt(jnp.mean(rows * rows, -1, keepdims=True) + epsilon)


def split_rows(rank_ref, total, keep, give):
    rows = keep.shape[1]
    low = rank_ref[0] % 2
    for high in range(keep.shape[0]):
        start = pl.multiple_of((2 * high + low) * rows, rows)
        keep[high] = total[pl.ds(start, rows), :]
        start = pl.multiple_of((2 * high + 1 - low) * rows, rows)
        give[high] = bf(total[pl.ds(start, rows), :])


def attend_kernel(
    rank_ref, x, gain, w_query, w_key, w_value, q_gain, k_gain, cosine, sine, seg_col, seg_row, w_out,
    xn, qp, kp, q, k, v, prob, o, keep, give, total,
):
    step, steps = pl.program_id(0), pl.num_programs(0)
    tokens, head = kp.shape
    cut = keep.shape[1]

    @pl.when(step == 0)
    def _():
        @pl.loop(0, tokens // cut)
        def _(i):
            rows = pl.ds(pl.multiple_of(i * cut, cut), cut)
            value = x[rows, :].astype(jnp.float32)
            xn[rows, :] = bf(value * inverse_rms(value) * gain[...])

        raw = mm(xn[...], w_key[...])
        kp[...] = raw
        scaled = raw * inverse_rms(raw) * k_gain[...]
        k[...] = bf(scaled * cosine[...] + turn(scaled) * sine[...])
        v[...] = bf(mm(xn[...], w_value[...]))
        total[...] = jnp.zeros_like(total)

    raw_pair = mm(xn[...], w_query[...])
    qp[...] = raw_pair
    visible = (seg_col[...] == seg_row[...]) & (
        lax.broadcasted_iota(jnp.int32, (tokens, tokens), 0)
        >= lax.broadcasted_iota(jnp.int32, (tokens, tokens), 1)
    )
    for i in range(prob.shape[0]):
        cols = slice(i * head, (i + 1) * head)
        raw = raw_pair[:, cols]
        scaled = raw * inverse_rms(raw) * q_gain[...]
        rows = bf(scaled * cosine[...] + turn(scaled) * sine[...])
        q[:, cols] = rows
        scores = jnp.where(visible, mm(rows, k[...], (1, 1)) * head**-0.5, far_below)
        weight = jnp.exp(scores - jnp.max(scores, -1, keepdims=True))
        low = bf(weight * (1.0 / jnp.sum(weight, -1, keepdims=True)))
        prob[i] = low
        o[:, cols] = bf(mm(low, v[...]))
    wide = 512

    @pl.loop(0, total.shape[1] // wide)
    def _(n):
        at = pl.ds(pl.multiple_of(n * wide, wide), wide)
        total[:, at] += mm(o[...], w_out[:, at])

    @pl.when(step == steps - 1)
    def _():
        split_rows(rank_ref, total, keep, give)


def attend(rank, x, gain, w_query, w_key, w_value, q_gain, k_gain, cosine, sine, segments, w_out, cut):
    tokens, width = x.shape
    head = q_gain.shape[0]
    query = w_query.shape[1]
    pair = 2
    steps = query // (pair * head)
    heads = pl.BlockSpec((tokens, pair * head), lambda j, _: (0, j))
    halves = tokens // cut // 2
    return pl.pallas_call(
        attend_kernel,
        grid_spec=pltpu.PrefetchScalarGridSpec(
            num_scalar_prefetch=1,
            grid=(steps,),
            in_specs=[
                whole((tokens, width)),
                whole((1, width)),
                pl.BlockSpec((width, pair * head), lambda j, _: (0, j)),
                whole((width, head)),
                whole((width, head)),
                whole((1, head)),
                whole((1, head)),
                whole((tokens, head)),
                whole((tokens, head)),
                whole((tokens, 1)),
                whole((1, tokens)),
                pl.BlockSpec((pair * head, width), lambda j, _: (j, 0)),
            ],
            out_specs=[
                whole((tokens, width)),
                heads,
                whole((tokens, head)),
                heads,
                whole((tokens, head)),
                whole((tokens, head)),
                pl.BlockSpec((pair, tokens, tokens), lambda j, _: (j, 0, 0)),
                heads,
                whole((halves, cut, width)),
                whole((halves, cut, width)),
            ],
            scratch_shapes=[pltpu.VMEM((tokens, width), jnp.float32)],
        ),
        out_shape=[
            jax.ShapeDtypeStruct((tokens, width), jnp.bfloat16),
            jax.ShapeDtypeStruct((tokens, query), jnp.float32),
            jax.ShapeDtypeStruct((tokens, head), jnp.float32),
            jax.ShapeDtypeStruct((tokens, query), jnp.bfloat16),
            jax.ShapeDtypeStruct((tokens, head), jnp.bfloat16),
            jax.ShapeDtypeStruct((tokens, head), jnp.bfloat16),
            jax.ShapeDtypeStruct((query // head, tokens, tokens), jnp.bfloat16),
            jax.ShapeDtypeStruct((tokens, query), jnp.bfloat16),
            jax.ShapeDtypeStruct((halves, cut, width), jnp.float32),
            jax.ShapeDtypeStruct((halves, cut, width), jnp.bfloat16),
        ],
        compiler_params=pltpu.CompilerParams(vmem_limit_bytes=vmem_bytes),
        cost_estimate=small_cost,
        name="attend",
    )(
        rank, x, gain[None], w_query, w_key, w_value, q_gain[None], k_gain[None], cosine, sine,
        segments[:, None], segments[None, :], w_out,
    )


def attend_back_kernel(
    rank_ref, x, xn, dattn, w_query, w_key, w_value, q_gain, k_gain, cosine, sine, w_out, qp, kp, q, k, v, prob,
    packed, gains, attn_gain, keep, give, total, dk, dv, low,
):
    step, steps = pl.program_id(0), pl.num_programs(0)
    tokens, head = kp.shape
    cut = keep.shape[1]
    scale = head**-0.5
    width = x.shape[1]
    wide = 512
    blocks = packed.shape[0]
    block_rows = width // blocks

    def unrotate(grad):
        return grad * cosine[...] - turn(grad) * sine[...]

    def unnorm(grad, raw, inverse, gain):
        scaled = grad * gain
        return inverse * (scaled - raw * inverse * inverse * jnp.mean(scaled * raw, -1, keepdims=True))

    def add_total(left, right, at):
        total[:, at] += mm(left, right[at, :], (1, 1))

    def put_packed(n):
        at = pl.ds(pl.multiple_of(n * wide, wide), wide)
        grad = bf(mm(xn[:, at], low[...], (0, 0)))
        many = wide // block_rows
        first = n * many
        packed[pl.ds(first, many), pl.ds(0, block_rows), :] = grad.reshape(many, block_rows, -1)

    @pl.when(step == 0)
    def _():
        total[...] = jnp.zeros_like(total)
        dk[...] = jnp.zeros_like(dk)
        dv[...] = jnp.zeros_like(dv)
        gains[...] = jnp.zeros_like(gains)

    @pl.when(step < steps - 1)
    def _():
        dout_pair = bf(mm(dattn[...], w_out[...], (1, 1)))
        for i in range(prob.shape[0]):
            cols = slice(i * head, (i + 1) * head)
            dout = dout_pair[:, cols]
            weight = prob[i]
            dp = mm(dout, v[...], (1, 1))
            wide_weight = weight.astype(jnp.float32)
            ds = bf(wide_weight * (dp - jnp.sum(wide_weight * dp, -1, keepdims=True)))
            dv[...] += mm(weight, dout, (0, 0))
            dk[...] += mm(ds, q[:, cols], (0, 0))
            dqu = unrotate(mm(ds, k[...]) * scale)
            raw = qp[:, cols]
            inverse = inverse_rms(raw)
            gains[0:1, :] += jnp.sum(dqu * raw * inverse, 0, keepdims=True)
            low[:, cols] = bf(unnorm(dqu, raw, inverse, q_gain[...]))

        @pl.loop(0, width // wide)
        def _(n):
            put_packed(n)
            add_total(low[...], w_query, pl.ds(pl.multiple_of(n * wide, wide), wide))

    @pl.when(step == steps - 1)
    def _():
        dku = unrotate(dk[...] * scale)
        raw = kp[...]
        inverse = inverse_rms(raw)
        gains[1:2, :] = jnp.sum(dku * raw * inverse, 0, keepdims=True)
        low[:, :head] = bf(unnorm(dku, raw, inverse, k_gain[...]))
        low[:, head:] = bf(dv[...])

        @pl.loop(0, width // wide)
        def _(n):
            put_packed(n)
            at = pl.ds(pl.multiple_of(n * wide, wide), wide)
            add_total(low[:, :head], w_key, at)
            add_total(low[:, head:], w_value, at)

        attn_gain[...] = jnp.zeros_like(attn_gain)

        @pl.loop(0, tokens // cut)
        def _(i):
            rows = pl.ds(pl.multiple_of(i * cut, cut), cut)
            value = x[rows, :].astype(jnp.float32)
            attn_gain[...] += jnp.sum(total[rows, :] * value * inverse_rms(value), 0, keepdims=True)

        split_rows(rank_ref, total, keep, give)


def attend_back(
    rank, x, xn, dattn, w_query, w_key, w_value, q_gain, k_gain, cosine, sine, w_out, qp, kp, q, k, v, prob,
    cut, blocks, spare,
):
    tokens, width = x.shape
    head = q_gain.shape[0]
    query = w_query.shape[1]
    pair = 2
    steps = query // (pair * head)
    last = steps - 1
    heads = pl.BlockSpec((tokens, pair * head), lambda j, _: (0, jnp.minimum(j, last)))
    halves = tokens // cut // 2
    block_rows = width // blocks + spare
    return pl.pallas_call(
        attend_back_kernel,
        grid_spec=pltpu.PrefetchScalarGridSpec(
            num_scalar_prefetch=1,
            grid=(steps + 1,),
            in_specs=[
                whole((tokens, width)),
                whole((tokens, width)),
                whole((tokens, width)),
                pl.BlockSpec((width, pair * head), lambda j, _: (0, jnp.minimum(j, last))),
                whole((width, head)),
                whole((width, head)),
                whole((1, head)),
                whole((1, head)),
                whole((tokens, head)),
                whole((tokens, head)),
                pl.BlockSpec((pair * head, width), lambda j, _: (jnp.minimum(j, last), 0)),
                heads,
                whole((tokens, head)),
                heads,
                whole((tokens, head)),
                whole((tokens, head)),
                pl.BlockSpec((pair, tokens, tokens), lambda j, _: (jnp.minimum(j, last), 0, 0)),
            ],
            out_specs=[
                pl.BlockSpec((blocks, block_rows, pair * head), lambda j, _: (0, 0, j)),
                whole((8, head)),
                whole((1, width)),
                whole((halves, cut, width)),
                whole((halves, cut, width)),
            ],
            scratch_shapes=[
                pltpu.VMEM((tokens, width), jnp.float32),
                pltpu.VMEM((tokens, head), jnp.float32),
                pltpu.VMEM((tokens, head), jnp.float32),
                pltpu.VMEM((tokens, pair * head), jnp.bfloat16),
            ],
        ),
        out_shape=[
            jax.ShapeDtypeStruct((blocks, block_rows, query + 2 * head), jnp.bfloat16),
            jax.ShapeDtypeStruct((8, head), jnp.float32),
            jax.ShapeDtypeStruct((1, width), jnp.float32),
            jax.ShapeDtypeStruct((halves, cut, width), jnp.float32),
            jax.ShapeDtypeStruct((halves, cut, width), jnp.bfloat16),
        ],
        compiler_params=pltpu.CompilerParams(vmem_limit_bytes=vmem_bytes),
        cost_estimate=pl.CostEstimate(flops=3 * 10**10, bytes_accessed=2**20, transcendentals=0),
        name="attend_back",
    )(
        rank, x, xn, dattn, w_query, w_key, w_value, q_gain[None], k_gain[None], cosine, sine, w_out,
        qp, kp, q, k, v, prob,
    )


class Loads:
    def __init__(self, sources, target, sems, shards):
        height = sources[0].shape[0]
        self.each = len(sources) // shards
        self.copies = [
            pltpu.make_async_copy(source, target.at[pl.ds(i * height, height), :], sems.at[i])
            for i, source in enumerate(sources)
        ]

    def start(self, shard):
        for copy in self.copies[shard * self.each : (shard + 1) * self.each]:
            copy.start()

    def wait(self, shard):
        for copy in self.copies[shard * self.each : (shard + 1) * self.each]:
            copy.wait()


def experts_kernel(rank_ref, hn, g, *rest, shards, before, local, hidden, top_count):
    last = before > 0
    every = before + shards
    in_count = every if last else shards
    if last:
        gates, totals_in, pre_before, gated_before = rest[:4]
        rest = rest[4:]
    else:
        sent, router = rest[:2]
        rest = rest[2:]
    in_hbm, down_hbm, rest = rest[: 2 * in_count], rest[2 * in_count : 3 * in_count], rest[3 * in_count :]
    if last:
        out, back, pre_grad, gated = rest[:4]
        rest = rest[4:]
        totals = rest[-1]
    else:
        pre_grad, gated, gates, totals = rest[:4]
        rest = rest[4:]
    in_all, down_all, gates_wide, in_sems, down_sems = rest[:5]
    chunk, shard = pl.program_id(0), pl.program_id(1)
    width = local * hidden
    rows, model = hn.shape
    first = before if last else 0
    in_loads = Loads(in_hbm, in_all, in_sems, in_count)
    down_loads = Loads(down_hbm, down_all, down_sems, in_count)
    owner = lax.broadcasted_iota(jnp.int32, (rows, width), 1) // hidden

    @pl.when((chunk == 0) & (shard == 0))
    def _():
        order = list(range(first, in_count)) + list(range(first))
        for i in order:
            in_loads.start(i)
            down_loads.start(i)

    @pl.when(shard == 0)
    def _():
        if last:
            totals[...] = totals_in[...]
        else:
            names = lax.broadcasted_iota(jnp.int32, (rows, router.shape[0]), 1).astype(jnp.float32)
            chosen = sent[...].astype(jnp.float32)
            mask = jnp.zeros(names.shape, jnp.bool_)
            for j in range(top_count):
                mask = mask | (chosen[:, j : j + 1] == names)
            logits = jnp.where(mask, mm(hn[...], router[...], (1, 1)), far_below)
            weight = jnp.exp(logits - jnp.max(logits, -1, keepdims=True))
            weight = weight * (1.0 / jnp.sum(weight, -1, keepdims=True))
            lanes = lax.broadcasted_iota(jnp.int32, gates.shape, 1)
            packed = jnp.zeros(gates.shape, jnp.float32)
            for e in range(local):
                here = names == (rank_ref[1] * local + e).astype(jnp.float32)
                value = jnp.sum(jnp.where(here, weight, 0.0), -1, keepdims=True)
                packed = packed + jnp.where(lanes == e, value, 0.0)
            gates[...] = packed
            totals[...] = jnp.zeros_like(totals)
        wide = jnp.zeros((rows, width), jnp.float32)
        for e in range(local):
            wide = jnp.where(owner == e, gates[:, e : e + 1], wide)
        gates_wide[...] = wide

    for i in range(shards):
        @pl.when((chunk == 0) & (shard == i))
        def _(i=i):
            in_loads.wait(first + i)
            down_loads.wait(first + i)

    in_at = pl.multiple_of((first + shard) * 2 * width, 2 * width)
    down_at = pl.multiple_of((first + shard) * width, width)
    pre = mm(hn[...], in_all[pl.ds(in_at, 2 * width), :], (1, 1))
    grad_middle = mm(g[...], down_all[pl.ds(down_at, width), :], (1, 1))
    gate_pre, up_pre = pre[:, :width], pre[:, width:]
    sigmoid_gate = jax.nn.sigmoid(gate_pre)
    activated = gate_pre * sigmoid_gate
    middle = activated * up_pre
    mid_at = pl.multiple_of(shard * width, width)
    gated[:, pl.ds(mid_at, width)] = bf(middle * gates_wide[...])
    product = middle * grad_middle
    lanes = lax.broadcasted_iota(jnp.int32, totals.shape, 1)
    added = totals[...]
    for e in range(local):
        value = jnp.sum(jnp.where(owner == e, product, 0.0), -1, keepdims=True)
        added = added + jnp.where(lanes == e, value, 0.0)
    totals[...] = added
    grad_middle = grad_middle * gates_wide[...]
    gate_at = pl.multiple_of(shard * 2 * width, 2 * width)
    pre_grad[:, pl.ds(gate_at, width)] = bf(
        grad_middle * up_pre * (sigmoid_gate + activated * (1.0 - sigmoid_gate))
    )
    pre_grad[:, pl.ds(pl.multiple_of(gate_at + width, width), width)] = bf(grad_middle * activated)

    if last:

        @pl.when(shard == shards - 1)
        def _():
            @pl.when(chunk == 0)
            def _():
                for i in range(before):
                    in_loads.wait(i)
                    down_loads.wait(i)

            wide = 512

            @pl.loop(0, model // wide)
            def _(n):
                cols = pl.ds(pl.multiple_of(n * wide, wide), wide)
                cut = before * width
                back[:, cols] = bf(
                    mm(pre_before[...], in_all[: 2 * cut, cols]) + mm(pre_grad[...], in_all[2 * cut :, cols])
                )
                out[:, cols] = bf(
                    mm(gated_before[...], down_all[:cut, cols]) + mm(gated[...], down_all[cut:, cols])
                )

            spare = back.shape[1] - model
            places = lax.broadcasted_iota(jnp.int32, (rows, spare), 1)
            tail = jnp.zeros((rows, spare), jnp.float32)
            for e in range(local):
                value = totals[:, e : e + 1]
                high = bf(value).astype(jnp.float32)
                here = rank_ref[1] * local + e
                tail = tail + jnp.where(places == here, high, 0.0)
                tail = tail + jnp.where(places == spare // 2 + here, value - high, 0.0)
            back[:, model:] = bf(tail)


def run_experts(ranks, hn, sent, in_mats, down_mats, local, top_count, router=None, before=None, spare=0):
    tokens, model = hn.shape
    width = down_mats[0].shape[0]
    every = len(down_mats)
    earlier = 0 if before is None else before[2].shape[1] // (2 * width)
    shards = every - earlier
    rows = tokens
    while rows > 768:
        rows //= 2

    def block(cols, step=0):
        return pl.BlockSpec((rows, cols), lambda c, s, _: (c, step), pipeline_mode=pl.Buffered(1))

    hbm = [pl.BlockSpec(memory_space=pl.ANY)] * (3 * every)
    scratch = [
        pltpu.VMEM((every * 2 * width, model), jnp.bfloat16),
        pltpu.VMEM((every * width, model), jnp.bfloat16),
        pltpu.VMEM((rows, width), jnp.float32),
        pltpu.SemaphoreType.DMA((2 * every,)),
        pltpu.SemaphoreType.DMA((every,)),
    ]
    own = [(shards * 2 * width, jnp.bfloat16), (shards * width, jnp.bfloat16)]
    if before is None:
        extra, specs = (sent, router), [block(128, model // 128), whole(router.shape)]
        outs = own + [(128, jnp.float32)] * 2
    else:
        extra = before
        specs = [block(value.shape[1]) for value in before]
        outs = [(model, jnp.bfloat16), (model + spare, jnp.bfloat16)] + own
        scratch.append(pltpu.VMEM((rows, 128), jnp.float32))
    return pl.pallas_call(
        functools.partial(
            experts_kernel, shards=shards, before=earlier, local=local, hidden=width // local, top_count=top_count
        ),
        grid_spec=pltpu.PrefetchScalarGridSpec(
            num_scalar_prefetch=1,
            grid=(tokens // rows, shards),
            in_specs=[block(model), block(model)] + specs + hbm,
            out_specs=[block(cols) for cols, _ in outs],
            scratch_shapes=scratch,
        ),
        out_shape=[jax.ShapeDtypeStruct((tokens, cols), kind) for cols, kind in outs],
        compiler_params=pltpu.CompilerParams(vmem_limit_bytes=vmem_bytes),
        cost_estimate=small_cost,
        name="experts_near" if before is None else "experts_far",
    )(ranks, hn, sent, *extra, *in_mats, *down_mats)


class Tokens:
    def __init__(self):
        self.size = lax.axis_size("expert")
        self.line = self.size == 8
        self.me = lax.axis_index("expert")
        self.z, self.y = self.me // 2, self.me % 2

    def across(self, value):
        return lax.ppermute(value, "expert", [(i, i ^ 1) for i in range(8)])

    def along(self, value, step):
        return lax.ppermute(value, "expert", [(i, i ^ (2 * step)) for i in range(8)])

    def place(self, step, other):
        return (self.z ^ step) * 2 + (1 - self.y if other else self.y)

    def gather(self, own, early):
        if not self.line:
            return lax.all_gather(own, "expert", axis=0, tiled=False), early
        blocks = [own] + [self.along(own, step) for step in (1, 2, 3)]
        others = [self.across(own)]
        blocks[1], early = tie(blocks[1], early)
        others += [self.across(value) for value in blocks[1:]]
        rows = jnp.zeros((self.size, *own.shape), own.dtype)
        for step in range(4):
            for value, other in ((blocks[step], False), (others[step], True)):
                rows = lax.dynamic_update_index_in_dim(rows, value, self.place(step, other), 0)
        return rows, early

    def scatter(self, parts, begun, late, last, middle=()):
        if not self.line:
            total = lax.psum_scatter(parts, "expert", scatter_dimension=0, tiled=False)
            return total.astype(jnp.float32), begun, late, last, middle

        def part(step, other):
            return lax.dynamic_index_in_dim(parts, self.place(step, other), 0, False)

        def pair_sum(step):
            return part(step, False).astype(jnp.float32) + across[step].astype(jnp.float32)

        across = {step: self.across(part(step, True)) for step in (3, 2, 1, 0)}
        across[3], begun = tie(across[3], begun)
        moved = {step: self.along(bf(pair_sum(step)), step) for step in (3, 2)}
        across[1], moved[3], middle = tie(across[1], moved[3], middle)
        moved[1] = self.along(bf(pair_sum(1)), 1)
        across[0], moved[2], late = tie(across[0], moved[2], late)
        moved[1], last = tie(moved[1], last)
        total = pair_sum(0) + sum(value.astype(jnp.float32) for value in moved.values())
        return total, begun, late, last, middle


def body(
    hidden_in,
    cotangent,
    segments,
    positions,
    routes,
    attn_gain,
    w_query,
    w_key,
    value_weight,
    q_gain,
    k_gain,
    w_out,
    ffn_gain,
    router,
    w_gate,
    w_up,
    w_down,
):
    tok_count, model_width = hidden_in.shape
    head_size = q_gain.shape[0]
    experts = router.shape[1]
    local_experts, _, hidden = w_gate.shape
    tensor_size = lax.axis_size("tensor")
    tensor_rank = lax.axis_index("tensor")
    expert_rank = lax.axis_index("expert")
    shard_rows = tok_count // tensor_size
    order = Tokens()
    group = order.size

    def own_rows(value):
        return lax.dynamic_slice_in_dim(value, tensor_rank * shard_rows, shard_rows)

    cot_own = own_rows(cotangent)
    routes_own = own_rows(routes)
    spare_cols = 128
    routes_wide = jnp.pad(bf(routes_own), ((0, 0), (0, spare_cols - routes.shape[1])))
    sent_own = jnp.concatenate([cot_own, routes_wide], 1)
    hidden_in, sent_own = tie(hidden_in, sent_own)
    sent = lax.all_gather(sent_own, "expert", axis=0, tiled=True)
    expert_ids = jnp.arange(experts, dtype=jnp.int32)

    def mask_of(route_rows):
        return jnp.any(route_rows[:, :, None] == expert_ids[None, None, :], 1)

    mask_own = mask_of(routes_own)
    own_mats = [value.reshape(local_experts * hidden, model_width) for value in (w_gate.transpose(0, 2, 1), w_up.transpose(0, 2, 1), w_down)]

    cosine, sine_table = rope_tables(positions, head_size)
    half = jnp.arange(head_size, dtype=jnp.int32) < head_size // 2
    sine_table = jnp.where(half, -sine_table, sine_table)
    ranks = jnp.stack([tensor_rank, expert_rank]).astype(jnp.int32)
    normalized_input, qp, kp, q, k, v, prob, attended_rows, keep, give_part = attend(
        ranks, hidden_in, attn_gain, w_query, w_key, value_weight, q_gain, k_gain, cosine, sine_table,
        segments, w_out, shard_rows,
    )

    def reduce_rows(keep, give, first=()):
        half = keep + swap(give, 1).astype(jnp.float32)
        high = tensor_rank // 2
        keep = lax.dynamic_index_in_dim(half, high, 0, False)
        give, first = tie(bf(lax.dynamic_index_in_dim(half, 1 - high, 0, False)), first)
        return keep + swap(give, 2).astype(jnp.float32), first

    def gather_rows(own):
        far = swap(own, 2)
        both = jnp.stack([own, far])
        near = swap(both, 1)
        rows = jnp.zeros((tensor_size, shard_rows, model_width), own.dtype)
        for value, step in ((own, 0), (far, 2), (near[0], 1), (near[1], 3)):
            rows = lax.dynamic_update_index_in_dim(rows, value, tensor_rank ^ step, 0)
        return rows.reshape(tok_count, model_width)

    far_gate = swap(own_mats[0], 2)
    attn_sum, far_gate = reduce_rows(keep, give_part, far_gate)
    residual = own_rows(hidden_in).astype(jnp.float32) + attn_sum
    inv_second = lax.rsqrt(jnp.mean(residual * residual, -1, keepdims=True) + epsilon)
    normed_ffn = (residual * inv_second * ffn_gain).astype(jnp.bfloat16)

    def gates_of(rows, mask):
        logits = jnp.where(mask, mm(rows, router), far_below)
        return jax.nn.softmax(logits, -1)

    gates_own = gates_of(normed_ffn, mask_own)
    far_up = swap(own_mats[1], 2)
    far_down = swap(own_mats[2], 2)
    normed_all, (sent, far_up) = order.gather(normed_ffn, (sent, far_up))
    normed_all, attended_rows, far_down = tie(normed_all, attended_rows, far_down)
    far_mats = [far_gate, far_up, far_down]
    attended_all = lax.all_gather(attended_rows, "expert", axis=0, tiled=True)
    normed_all = normed_all.reshape(group * shard_rows, model_width)
    grad_all = sent[:, :model_width]
    near_mats = [swap(value, 1) for value in own_mats]
    last_mats = [swap(value, 1) for value in far_mats]
    shards = (own_mats, near_mats, far_mats, last_mats)
    in_mats = [value for shard in shards for value in shard[:2]]
    down_mats = [shard[2] for shard in shards]
    width = local_experts * hidden
    given = (ranks, normed_all, sent)
    near_count = len(shards) // 2
    pre_near, gated_near, gates_packed, marks = run_experts(
        *given, in_mats[: 2 * near_count], down_mats[:near_count], local_experts, routes.shape[1], router.T
    )
    spare_cols = 128 * (-(-2 * experts // 128))
    out_part, back_part, pre_last, gated_last = run_experts(
        *given, in_mats, down_mats, local_experts, routes.shape[1],
        before=(gates_packed, marks, pre_near, gated_near), spare=spare_cols,
    )
    def weight_grads(step):
        pre, gated = ((pre_near, gated_near), (pre_last, gated_last))[step // near_count]
        at = step % near_count
        pre, gated = pre[:, at * 2 * width : (at + 1) * 2 * width], gated[:, at * width : (at + 1) * width]
        return mm(pre, normed_all, (0, 0)), mm(gated, grad_all, (0, 0))

    def give(parts, step):
        return [swap(bf(part), step).astype(jnp.float32) for part in parts]

    far = give(weight_grads(3), 1)
    near = give(weight_grads(1), 1)
    far_part = [bf(a + b) for a, b in zip(weight_grads(2), far)]
    near_part = [a + b for a, b in zip(weight_grads(0), near)]
    far_part = [far_part[0][:width], far_part[0][width:], far_part[1]]

    far_part = tuple(far_part)
    arrived = [swap(far_part[0], 2)]
    back_sum, far_part, attended_all, arrived[0], _ = order.scatter(
        back_part.reshape(group, shard_rows, -1), far_part, attended_all, arrived[0]
    )
    gate_grad_own = (
        back_sum[:, model_width : model_width + experts]
        + back_sum[:, model_width + spare_cols // 2 :][:, :experts]
    )
    back_sum = back_sum[:, :model_width]
    grad_out = cot_own.astype(jnp.float32)
    grad_chosen = gates_own * (
        gate_grad_own - jnp.sum(gates_own * gate_grad_own, -1, keepdims=True)
    )
    grad_logits = bf(jnp.where(mask_own, grad_chosen, 0.0))
    router_part = mm(normed_ffn, grad_logits, (0, 0))
    grad_normed_ffn = back_sum + mm(grad_logits, router, (1, 1))
    ffn_gain_part = jnp.sum(grad_normed_ffn * residual * inv_second, 0)
    grad_residual = grad_out + norm_back(grad_normed_ffn * ffn_gain, residual, inv_second)
    slice_rows = model_width // group
    own_cols = lax.all_to_all(
        bf(grad_residual).reshape(shard_rows, group, slice_rows).transpose(1, 0, 2),
        "expert",
        split_axis=0,
        concat_axis=0,
        tiled=True,
    )
    grad_attn = gather_rows(bf(grad_residual))
    grad_attn, far_cols, *left = tie(grad_attn, swap(own_cols, 2), *far_part[1:])
    arrived += [swap(piece, 2) for piece in left]
    grad_attn, out_part = tie(grad_attn, out_part)
    out_sum = lax.psum_scatter(
        out_part.reshape(group, shard_rows, model_width), "expert", scatter_dimension=0, tiled=False
    )
    spare = 16
    packed, gain_parts, attn_gain_part, keep, give_part = attend_back(
        ranks, hidden_in, normalized_input, grad_attn, w_query, w_key, value_weight, q_gain, k_gain, cosine,
        sine_table, w_out, qp, kp, q, k, v, prob, shard_rows, group, spare,
    )
    grad_normed, _ = reduce_rows(keep, give_part)
    inputs_own = own_rows(hidden_in).astype(jnp.float32)
    inv_own = lax.rsqrt(jnp.mean(inputs_own * inputs_own, -1, keepdims=True) + epsilon)
    input_grad = gather_rows(
        bf(grad_residual + norm_back(grad_normed * attn_gain, inputs_own, inv_own))
    ).astype(jnp.float32)

    small = jnp.concatenate(
        [
            router_part.reshape(group, -1),
            attn_gain_part.reshape(group, -1),
            ffn_gain_part.reshape(group, -1),
            jnp.broadcast_to(gain_parts[:2].reshape(1, -1), (group, 2 * head_size)),
        ],
        1,
    )
    small = jnp.pad(small, ((0, 0), (0, spare * packed.shape[2] - small.shape[1])))
    packed = lax.dynamic_update_slice(
        packed, bf(small).reshape(group, spare, packed.shape[2]), (0, slice_rows, 0)
    )
    packed, out_sum, _, _, _ = order.scatter(packed, out_sum, (), ())
    near_cols = swap(jnp.stack([own_cols, far_cols]), 1)
    attn_cols = jnp.zeros((tensor_size, *own_cols.shape), own_cols.dtype)
    for value, step in ((own_cols, 0), (far_cols, 2), (near_cols[0], 1), (near_cols[1], 3)):
        attn_cols = lax.dynamic_update_index_in_dim(attn_cols, value, tensor_rank ^ step, 0)
    attn_cols = attn_cols.transpose(1, 0, 2, 3).reshape(group * tok_count, slice_rows)
    w_out_grad = mm(attended_all, attn_cols, (0, 0))
    layer_out = gather_rows(bf(residual + out_sum.astype(jnp.float32)))
    query_width, key_width = w_query.shape[1], w_key.shape[1]
    w_query_grad = packed[:slice_rows, :query_width]
    w_key_grad = packed[:slice_rows, query_width : query_width + key_width]
    w_value_grad = packed[:slice_rows, query_width + key_width :]
    small = packed[slice_rows:]
    small = small + swap(bf(small), 1).astype(jnp.float32)
    small = (small + swap(bf(small), 2).astype(jnp.float32)).reshape(-1)
    cuts = [slice_rows * experts, slice_rows, slice_rows, head_size, head_size]
    router_grad, attn_gain_grad, ffn_gain_grad, q_gain_all, k_gain_all = [
        small[sum(cuts[:i]) : sum(cuts[: i + 1])] for i in range(len(cuts))
    ]
    parts = [near_part[0][:width], near_part[0][width:], near_part[1]]
    gate_t, up_t, w_down_grad = [
        (a + b.astype(jnp.float32)).reshape(local_experts, hidden, model_width)
        for a, b in zip(parts, arrived)
    ]
    w_gate_grad, w_up_grad = gate_t.transpose(0, 2, 1), up_t.transpose(0, 2, 1)
    gain_count = head_size // group
    gain_at = expert_rank * gain_count
    return (
        layer_out,
        input_grad,
        attn_gain_grad,
        w_query_grad,
        w_key_grad,
        w_value_grad,
        lax.dynamic_slice_in_dim(q_gain_all, gain_at, gain_count),
        lax.dynamic_slice_in_dim(k_gain_all, gain_at, gain_count),
        w_out_grad,
        ffn_gain_grad,
        router_grad.reshape(slice_rows, experts),
        w_gate_grad,
        w_up_grad,
        w_down_grad,
    )


def solution(mesh):
    placed = (
        P("expert", None),
        P("expert", None),
        P("expert"),
        P("expert"),
        P("expert", None),
        P(),
        P(None, "tensor"),
        P(None, "tensor"),
        P(None, "tensor"),
        P(),
        P(),
        P("tensor", None),
        P(),
        P(),
        P("expert", None, "tensor"),
        P("expert", None, "tensor"),
        P("expert", "tensor", None),
    )
    return jax.shard_map(
        body,
        mesh=mesh,
        in_specs=placed,
        out_specs=(
            P("expert", None),
            P("expert", None),
            P("expert"),
            P("expert", "tensor"),
            P("expert", "tensor"),
            P("expert", "tensor"),
            P("expert"),
            P("expert"),
            P("tensor", "expert"),
            P("expert"),
            P("expert", None),
            P("expert", None, "tensor"),
            P("expert", None, "tensor"),
            P("expert", "tensor", None),
        ),
        check_vma=False,
    )
```
